32 devices in a mesh: grp: 2 (over x), ctx: 4 (over y, core), fsdp: 4 (over z).
Axes of the slice: x: 2, y: 2, z: 4, core: 2. Of those that a mesh axis runs over, the one named last changes fastest.
Arguments:
- tokens: bfloat16 [8, 1024, 2048], P(('grp', 'fsdp'), 'ctx'), may hold values from -6 to 6
- places: int32 [8, 1024], P(('grp', 'fsdp')), may hold values from 0 to 1023, as said below
- segments: int32 [8, 1024], P(('grp', 'fsdp')), may hold values from 0 to 3, as said below
- routes: int32 [8, 1024, 8], P(('grp', 'fsdp'), 'ctx'), may hold values from 0 to 15, all different within a row; in each aligned block of 256 rows (0 to 255, 256 to 511, ..., all dimensions but the last counted through in order) at most 160 rows name the same one
- w_query: bfloat16 [2048, 4096], P(('ctx', 'fsdp')), may hold values from -0.125 to 0.125
- w_key: bfloat16 [2048, 512], P(('ctx', 'fsdp')), may hold values from -0.125 to 0.125
- w_value: bfloat16 [2048, 512], P(('ctx', 'fsdp')), may hold values from -0.125 to 0.125
- w_out: bfloat16 [4096, 2048], P(('ctx', 'fsdp')), may hold values from -0.25 to 0.25
- w_router: bfloat16 [2048, 16], P(('ctx', 'fsdp')), may hold values from -0.0625 to 0.0625
- w_gate: bfloat16 [16, 2048, 768], P(None, ('ctx', 'fsdp')), may hold values from -0.125 to 0.125
- w_up: bfloat16 [16, 2048, 768], P(None, ('ctx', 'fsdp')), may hold values from -0.125 to 0.125
- w_down: bfloat16 [16, 768, 2048], P(None, ('ctx', 'fsdp')), may hold values from -0.4375 to 0.4375
- gain_attn: float32 [2048], replicated, may hold values from 0.25 to 1.75
- gain_ffn: float32 [2048], replicated, may hold values from 0.25 to 1.75
- gain_query: float32 [128], replicated, may hold values from 0.25 to 1.75
- gain_key: float32 [128], replicated, may hold values from 0.25 to 1.75
- cotangent: bfloat16 [8, 1024, 2048], P(('grp', 'fsdp'), 'ctx'), may hold values from -6 to 6
Outputs:
- output: bfloat16 [8, 1024, 2048], P(('grp', 'fsdp'), 'ctx')
- grad_tokens: float32 [8, 1024, 2048], P(('grp', 'fsdp'), 'ctx')
- grad_query: float32 [2048, 4096], P(('ctx', 'fsdp'))
- grad_key: float32 [2048, 512], P(('ctx', 'fsdp'))
- grad_value: float32 [2048, 512], P(('ctx', 'fsdp'))
- grad_out: float32 [4096, 2048], P(('ctx', 'fsdp'))
- grad_router: float32 [2048, 16], P(('ctx', 'fsdp'))
- grad_gate: float32 [16, 2048, 768], P(None, ('ctx', 'fsdp'))
- grad_up: float32 [16, 2048, 768], P(None, ('ctx', 'fsdp'))
- grad_down: float32 [16, 768, 2048], P(None, ('ctx', 'fsdp'))
- grad_gain_attn: float32 [2048], replicated
- grad_gain_ffn: float32 [2048], replicated
- grad_gain_query: float32 [128], replicated
- grad_gain_key: float32 [128], replicated
The draws below stay inside these ranges and needn't reach their ends.
Inputs may be any that keep to these rules, and one draw needn't show every extreme that they name: Each sequence of 1024 tokens is cut into 8 blocks of 128 positions; the c-th 256 stored tokens hold two whole blocks b and 7 - b, each in rising order; places of one sequence are a permutation of 0 to 1023. `segments`: document numbers never fall with the position given by places; each sequence has 4 documents, each of 200 positions or more. `routes`: among the 256 tokens of one device, no expert is named by more than 160 tokens.
All inputs are finite; a program needn't handle non-finite values.
Results may differ from the reference program's by a relative error of at most 0.023.
Values may be sent and summed in bfloat16 or wider, within the bound.
A program may use at most 448 MiB of HBM per device.

```python
import math
import jax
import jax.numpy as jnp
import numpy as np
from jax import lax

D = 2048
HEADS = 32
KVH = 4
HDIM = 128
FF = 768
TOP = 8
EXPERTS = 16
TOK_DEV = 256
DOCS = 4
CAP = 160
SEQ_LEN = 1024
DOC_MIN = 200
SEQS = 8


def place_table(key):
    key = jax.random.fold_in(key, 11)
    blocks = SEQ_LEN // TOK_DEV
    half = TOK_DEV // 2

    def one_row(subkey):
        order = jax.random.permutation(jax.random.fold_in(subkey, 1), blocks)
        flips = jax.random.randint(jax.random.fold_in(subkey, 2), (blocks,), 0, 2)
        first = jnp.where(flips == 1, 2 * blocks - 1 - order, order)
        second = 2 * blocks - 1 - first
        paired = jnp.stack([first, second], axis=1)
        offsets = jnp.arange(half, dtype=jnp.int32)
        return (paired[:, :, None] * half + offsets[None, None, :]).reshape(-1).astype(jnp.int32)
    return jax.vmap(one_row)(jax.random.split(key, SEQS))


def draw_places(key, part):
    return place_table(key)


def draw_segments(key, part):
    table = place_table(key)
    key = jax.random.fold_in(key, 5)
    spare_total = SEQ_LEN - DOCS * DOC_MIN

    def one_row(subkey, place):
        spare = jnp.sort(jax.random.randint(subkey, (DOCS - 1,), 0, spare_total + 1)).astype(jnp.int32)
        starts = (jnp.arange(1, DOCS, dtype=jnp.int32) * DOC_MIN + spare).astype(jnp.int32)
        return jnp.sum((starts[None, :] <= place[:, None]).astype(jnp.int32), axis=1)
    return jax.vmap(one_row)(jax.random.split(key, SEQS), table).astype(jnp.int32)


def levels(own_key, shape, cuts, smallest, largest):
    factor_of, own = 1.0, jax.random.fold_in(own_key, 6)
    for position, blocks in cuts:
        heights = jnp.exp(jax.random.uniform(jax.random.fold_in(own, position), (blocks,), jnp.float32, smallest / len(cuts), largest / len(cuts)))
        factor_of = factor_of * jnp.repeat(heights, shape[position] // blocks).reshape([-1 if axis == position else 1 for axis in range(len(shape))])
    return factor_of


def routed_block(stream_key, own, number, rows, amount, top, most, lean):
    order = jax.random.permutation(stream_key, amount)
    crowded, ordinary = shares(amount, rows * top, most, lean, True), shares(amount, rows * top, most, lean, False)
    places = jnp.arange(amount)

    def named(lengths, offset_by):
        used = int((lengths > 0).sum())
        fixed = max(1, used // 4)
        shifted = fixed + (places - fixed + offset_by * (used - fixed)) % max(1, amount - fixed)
        return jnp.zeros((amount,), jnp.int32).at[order[jnp.where(places < fixed, places, shifted)]].set(jnp.asarray(lengths, jnp.int32))

    lengths = jnp.where(number % 4 == 0, named(crowded, number // 4), named(ordinary, number - number // 4 - 1))
    mixed = jax.random.permutation(jax.random.fold_in(own, 3), amount)
    giver, sink = mixed[0:amount // 2 * 2:2], mixed[1:amount // 2 * 2:2]
    room = jnp.minimum(lengths[giver] - 1, most - lengths[sink]) // 2
    room = jnp.where((giver == order[0]) | (sink == order[0]) | (lengths[sink] == 0), 0, jnp.maximum(room, 0))
    shifted = jax.random.randint(jax.random.fold_in(own, 4), (amount // 2,), 0, 1 << 20) % (room + 1)
    lengths = lengths.at[giver].add(-shifted).at[sink].add(shifted)
    items = jnp.searchsorted(jnp.cumsum(lengths), jnp.arange(rows * top), side="right").astype(jnp.int32)
    table = items.reshape(top, rows).T
    table = table[jax.random.permutation(jax.random.fold_in(own, 1), rows)]
    offset_by = jax.random.randint(jax.random.fold_in(own, 2), (rows, 1), 0, top)
    return jnp.take_along_axis(table, (jnp.arange(top)[None, :] + offset_by) % top, axis=1)


def shares(count, total, bound, lean, full):
    portions = [(1 << 20) // math.isqrt(grade ** lean) + 1 for grade in range(1, count + 1)]
    largest = bound if full else min(bound, max(-(-total // count), total * portions[0] // sum(portions)))
    least = 1 if total - largest >= count - 1 else 0
    counts, spare = [largest] + [least] * (count - 1), total - largest - least * (count - 1)
    while spare > 0:
        movable = [i for i in range(1, count) if counts[i] < largest] or [i for i in range(1, count) if counts[i] < bound]
        pool, budget = sum([portions[i] for i in movable]), spare
        for i in movable:
            more = min(bound - counts[i], max(1, budget * portions[i] // pool), spare)
            counts[i] = counts[i] + more
            spare = spare - more
    return np.array(counts)


def scatter_about(own_key, extent, spread, bound, shards=(), held_as=jnp.bfloat16):
    factor_of = levels(own_key, extent, shards, -0.22, 0.18) if shards else 1.0
    values = jax.random.normal(own_key, extent, jnp.float32) * spread * factor_of
    return jnp.minimum(jnp.maximum(values, -bound), bound).astype(held_as)


def setup_inputs(seed: int = 0) -> dict:
    seeds = jax.random.split(jax.random.key(seed), 18)
    tokens = scatter_about(seeds[0], (SEQS, SEQ_LEN, D), 1.0, 6.0, ((0, 8), (1, 4)))
    places = draw_places(jax.random.fold_in(seeds[17], 71), 0)
    segments = draw_segments(jax.random.fold_in(seeds[17], 71), 0)
    routes_keys = jax.random.split(jax.random.fold_in(seeds[3], 1), SEQS * SEQ_LEN // TOK_DEV)
    routes_turns = jax.random.permutation(jax.random.fold_in(seeds[3], 3), SEQS * SEQ_LEN // TOK_DEV)
    routes = jax.vmap(lambda own, number: routed_block(jax.random.fold_in(seeds[3], 2), own, number, TOK_DEV, EXPERTS, TOP, CAP, 1))(routes_keys, routes_turns).reshape((SEQS, SEQ_LEN, TOP))
    w_query = scatter_about(seeds[4], (D, HEADS * HDIM), D ** -0.5, 0.125, ((0, 16),))
    w_key = scatter_about(seeds[5], (D, KVH * HDIM), D ** -0.5, 0.125, ((0, 16),))
    w_value = scatter_about(seeds[6], (D, KVH * HDIM), D ** -0.5, 0.125, ((0, 16),))
    w_out = scatter_about(seeds[7], (HEADS * HDIM, D), (HEADS * HDIM // 8) ** -0.5, 0.25, ((0, 16),))
    w_router = scatter_about(seeds[8], (D, EXPERTS), (4 * D) ** -0.5, 0.0625, ((0, 16),))
    w_gate = scatter_about(seeds[9], (EXPERTS, D, FF), D ** -0.5, 0.125, ((1, 16),))
    w_up = scatter_about(seeds[10], (EXPERTS, D, FF), D ** -0.5, 0.125, ((1, 16),))
    w_down = scatter_about(seeds[11], (EXPERTS, FF, D), (FF // 4) ** -0.5, 0.4375, ((1, 16),))
    gain_attn = jnp.clip(1.0 + 0.15 * jax.random.normal(seeds[12], (D,), jnp.float32), 0.25, 1.75)
    gain_ffn = jnp.clip(1.0 + 0.15 * jax.random.normal(seeds[13], (D,), jnp.float32), 0.25, 1.75)
    gain_query = jnp.clip(1.0 + 0.15 * jax.random.normal(seeds[14], (HDIM,), jnp.float32), 0.25, 1.75)
    gain_key = jnp.clip(1.0 + 0.15 * jax.random.normal(seeds[15], (HDIM,), jnp.float32), 0.25, 1.75)
    cotangent = scatter_about(seeds[16], (SEQS, SEQ_LEN, D), 1.0, 6.0, ((0, 8), (1, 4)))
    return {"tokens": tokens, "places": places, "segments": segments, "routes": routes, "w_query": w_query, "w_key": w_key, "w_value": w_value, "w_out": w_out, "w_router": w_router, "w_gate": w_gate, "w_up": w_up, "w_down": w_down, "gain_attn": gain_attn, "gain_ffn": gain_ffn, "gain_query": gain_query, "gain_key": gain_key, "cotangent": cotangent}


highest = lax.Precision.HIGHEST
epsilon = 1e-06

@jax.custom_vjp
def low(v):
    return lax.optimization_barrier(v.astype(jnp.bfloat16)).astype(jnp.float32)

@jax.custom_vjp
def low_back(v):
    return v

def low_keep(v):
    return (low(v), None)

def low_pass(kept, grad):
    return (grad,)

def back_keep(v):
    return (v, None)

def back_low(kept, grad):
    return (low(grad),)
low.defvjp(low_keep, low_pass)
low_back.defvjp(back_keep, back_low)

def normed(values, gain):
    return values * lax.rsqrt(lax.optimization_barrier(jnp.mean(values * values, axis=-1, keepdims=True)) + epsilon) * gain

def angles(place, width):
    steps = jnp.arange(width // 2).astype(jnp.float32)
    inverse = jnp.exp(steps * (-2.0 * math.log(1000000.0) / width))
    return place.astype(jnp.float32)[:, None] * inverse[None, :]

def rotate(values, angle):
    half = values.shape[-1] // 2
    cosine = jnp.cos(angle)[:, None, :]
    sine = jnp.sin(angle)[:, None, :]
    first = values[..., :half]
    second = values[..., half:]
    return jnp.concatenate([first * cosine - second * sine, second * cosine + first * sine], axis=-1)

def one_sequence(params, resid, route_ids, place, segment):
    w_query, w_key, w_value, w_out, w_router, w_gate, w_up, w_down, gain_attn, gain_ffn, gain_query, gain_key = params
    length = resid.shape[0]
    normed_one = low(normed(resid, gain_attn))
    q_lin = low_back(jnp.dot(normed_one, w_query, precision=highest))
    k_lin = low_back(jnp.dot(normed_one, w_key, precision=highest))
    v_lin = low_back(low(jnp.dot(normed_one, w_value, precision=highest)))
    angle = angles(place, HDIM)
    query = low_back(low(rotate(normed(q_lin.reshape(length, HEADS, HDIM), gain_query), angle)))
    keyed = low_back(low(rotate(normed(k_lin.reshape(length, KVH, HDIM), gain_key), angle)))
    values = v_lin.reshape(length, KVH, HDIM)
    grouped = query.reshape(length, KVH, HEADS // KVH, HDIM)
    scores = jnp.einsum('ikgd,jkd->kgij', grouped, keyed, precision=highest) * (1.0 / math.sqrt(HDIM))
    scores = low_back(scores)
    allowed = (segment[:, None] == segment[None, :]) & (place[None, :] <= place[:, None])
    masked = jnp.where(allowed, scores, -1e+30)
    row_max = lax.optimization_barrier(jnp.max(masked, axis=-1, keepdims=True))
    expd = jnp.exp(masked - row_max)
    probs = low(expd / lax.optimization_barrier(jnp.sum(expd, axis=-1, keepdims=True)))
    mixed = jnp.einsum('kgij,jkd->ikgd', probs, values, precision=highest).reshape(length, HEADS * HDIM)
    mixed = low_back(low(mixed))
    resid_one = resid + low_back(jnp.dot(mixed, w_out, precision=highest))
    normed_two = low(normed(resid_one, gain_ffn))
    logits = low_back(jnp.dot(normed_two, w_router, precision=highest))
    chosen = jnp.take_along_axis(logits, route_ids, axis=1)
    gates = jax.nn.softmax(chosen, axis=-1)
    labels = jnp.arange(EXPERTS).astype(jnp.int32)
    onehot = (route_ids[:, :, None] == labels[None, None, :]).astype(jnp.float32)
    weights = lax.optimization_barrier(jnp.sum(gates[:, :, None] * onehot, axis=1))

    def expert(pieces):
        weight_gate, weight_up, weight_down, weight = pieces
        rows_in = low_back(normed_two)
        act_gate = low_back(jnp.dot(rows_in, weight_gate, precision=highest))
        act_up = low_back(jnp.dot(rows_in, weight_up, precision=highest))
        hidden = low(jax.nn.silu(act_gate) * act_up)
        made = low_back(low(jnp.dot(hidden, weight_down, precision=highest)))
        return weight[:, None] * made
    moe = lax.optimization_barrier(jnp.sum(lax.map(expert, (w_gate, w_up, w_down, weights.T)), axis=0))
    return resid_one + moe

def reference(tokens, places, segments, routes, w_query, w_key, w_value, w_out, w_router, w_gate, w_up, w_down, gain_attn, gain_ffn, gain_query, gain_key, cotangent):
    params = tuple((item.astype(jnp.float32) for item in (w_query, w_key, w_value, w_out, w_router, w_gate, w_up, w_down, gain_attn, gain_ffn, gain_query, gain_key)))

    def forward(weights, inputs):

        def step(carry, pieces):
            return (carry, jax.checkpoint(one_sequence)(weights, *pieces))
        return lax.scan(step, jnp.float32(0.0), (inputs, routes, places, segments))[1]
    result, pullback = jax.vjp(forward, params, tokens.astype(jnp.float32))
    grads, grad_tokens = pullback(cotangent.astype(jnp.float32))
    return (result.astype(jnp.bfloat16), grad_tokens, grads[0], grads[1], grads[2], grads[3], grads[4], grads[5], grads[6], grads[7], grads[8], grads[9], grads[10], grads[11])
```

```python
import math

import jax
import jax.numpy as jnp
from jax import lax
from jax.sharding import Mesh
from jax.sharding import PartitionSpec as P

epsilon = 1e-06
low = jnp.bfloat16
wide = jnp.float32
SWAP = [(0, 1), (1, 0)]
ROW_TILE = 16


def normed(values, gain):
    return values * lax.rsqrt(jnp.mean(values * values, axis=-1, keepdims=True) + epsilon) * gain


def angles(place, width):
    steps = jnp.arange(width // 2).astype(jnp.float32)
    inverse = jnp.exp(steps * (-2.0 * math.log(1000000.0) / width))
    return place.astype(jnp.float32)[:, None] * inverse[None, :]


def rotate(values, angle):
    half = values.shape[-1] // 2
    cosine = jnp.cos(angle)[:, None, :]
    sine = jnp.sin(angle)[:, None, :]
    first = values[..., :half]
    second = values[..., half:]
    return jnp.concatenate(
        [first * cosine - second * sine, second * cosine + first * sine], axis=-1
    )


def head_prep(q_lin, k_lin, gain_query, gain_key, angle):
    count = q_lin.shape[0]
    width = gain_query.shape[0]
    query = rotate(normed(q_lin.reshape(count, -1, width), gain_query), angle)
    keyed = rotate(normed(k_lin.reshape(count, -1, width), gain_key), angle)
    return (query, keyed)


def dot(left, right):
    return jnp.dot(left, right, preferred_element_type=jnp.float32)


def dot_nt(left, right):
    return lax.dot_general(left, right, (((1,), (1,)), ((), ())), preferred_element_type=jnp.float32)


def dot_tn(left, right):
    return lax.dot_general(left, right, (((0,), (0,)), ((), ())), preferred_element_type=jnp.float32)


def flat_index(axes):
    index = 0
    for axis in axes:
        index = index * 2 + lax.axis_index(axis)
    return index


def gather_rows(rows, order):
    for axis in order:
        rows = jnp.concatenate([rows, lax.ppermute(rows, axis, SWAP)], axis=0)
    return rows


def scatter_rows(rows, order, sent):
    for axis in reversed(order):
        half = rows.shape[0] // 2
        arrived = lax.ppermute(rows[half:].astype(sent), axis, SWAP)
        rows = rows[:half].astype(wide) + arrived.astype(wide)
    return rows


def all_to_all(axes, pick):
    amount = 1 << len(axes)
    here = flat_index(axes)
    own = pick(here)
    held = jnp.zeros((amount,) + own.shape, own.dtype)
    held = lax.dynamic_update_index_in_dim(held, own, here, 0)
    for step in range(1, amount):
        other = jnp.bitwise_xor(here, step)
        pairs = [(place, place ^ step) for place in range(amount)]
        arrived = lax.ppermute(pick(other), axes, pairs)
        held = lax.dynamic_update_index_in_dim(held, arrived, other, 0)
    return held


def take(stack, index):
    return lax.dynamic_index_in_dim(stack, index, 0, keepdims=False)


def gather_blocks(block, axes, at):
    if not axes:
        return block
    if len(axes) > 1:
        return lax.all_gather(block, axes, axis=at, tiled=True)
    other = lax.ppermute(block, axes[0], SWAP)
    first = lax.axis_index(axes[0]) == 0
    return jnp.concatenate(
        [jnp.where(first, block, other), jnp.where(first, other, block)], axis=at
    )


def own_first(stack, axes):
    if len(axes) != 1:
        return stack
    first = lax.axis_index(axes[0]) == 0
    return jnp.where(first, stack, jnp.flip(stack, 0))


def gather_halves(block, axes):
    if not axes:
        return block[None]
    if len(axes) > 1:
        return lax.all_gather(block, axes, axis=0, tiled=False)
    return jnp.stack([block, lax.ppermute(block, axes[0], SWAP)])


def scatter_halves(stack, axes):
    if not axes:
        return stack[0].astype(low)
    if len(axes) > 1:
        return lax.psum_scatter(stack.astype(low), axes, scatter_dimension=0, tiled=False)
    arrived = lax.ppermute(stack[1].astype(low), axes[0], SWAP)
    return (stack[0].astype(wide) + arrived.astype(wide)).astype(low)


def scatter_blocks(stack, axes):
    if not axes:
        return stack[0].astype(low)
    if len(axes) > 1:
        return lax.psum_scatter(stack.astype(low), axes, scatter_dimension=0, tiled=False)
    here = lax.axis_index(axes[0])
    arrived = lax.ppermute(take(stack, 1 - here).astype(low), axes[0], SWAP)
    return (take(stack, here).astype(wide) + arrived.astype(wide)).astype(low)


def sum_all(value, axes):
    for axis in axes:
        value = value + lax.ppermute(value, axis, SWAP)
    return value


def per_device(
    g_axes,
    c_axes,
    f_axes,
    tokens,
    places,
    segments,
    routes,
    w_query,
    w_key,
    w_value,
    w_out,
    w_router,
    w_gate,
    w_up,
    w_down,
    gain_attn,
    gain_ffn,
    gain_query,
    gain_key,
    cotangent,
):
    groups, parts_c, parts_f = 1 << len(g_axes), 1 << len(c_axes), 1 << len(f_axes)
    count = tokens.shape[1]
    width = gain_query.shape[0]
    model_width = tokens.shape[2]
    heads = w_query.shape[1] // width // parts_c
    kv_heads = w_key.shape[1] // width // parts_c
    group = heads // kv_heads
    experts = w_gate.shape[0]
    hidden_width = w_gate.shape[2]
    scale = 1.0 / math.sqrt(width)
    rows_d = w_query.shape[0]
    rows_f = w_down.shape[1]
    pair_count = experts.bit_length() - 1 - len(g_axes) - len(c_axes)
    assert 0 <= pair_count <= len(f_axes)
    far_axes = f_axes[: len(f_axes) - pair_count]
    near_axes = f_axes[len(f_axes) - pair_count :]
    parts_far, parts_near = 1 << len(far_axes), 1 << len(near_axes)
    team_axes = c_axes + near_axes
    team = parts_c * parts_near
    all_axes = g_axes + c_axes + f_axes
    g_here = flat_index(g_axes)
    c_here = flat_index(c_axes)
    expert_here = flat_index(g_axes + team_axes)

    resid = tokens[0].astype(jnp.float32)
    norm_one, back_one = jax.vjp(normed, resid, gain_attn)
    normed_one = norm_one.astype(low)
    rows_one = (
        normed_one.reshape(count, parts_c, parts_f, rows_d)
        .transpose(0, 2, 1, 3)
        .reshape(count, model_width)
    )
    all_one = gather_rows(rows_one, c_axes)

    q_cols, k_cols = heads * width, kv_heads * width
    qkv_cols = q_cols + 2 * k_cols
    own_qkv = jnp.concatenate(
        [
            w_query.reshape(rows_d, parts_c, q_cols),
            w_key.reshape(rows_d, parts_c, k_cols),
            w_value.reshape(rows_d, parts_c, k_cols),
        ],
        axis=2,
    )
    own_qkv = own_qkv.reshape(rows_d, parts_c, groups, qkv_cols // groups).transpose(2, 1, 0, 3)
    mine_qkv = take(own_qkv, g_here)
    got_qkv = all_to_all(c_axes, lambda other: take(mine_qkv, other))
    got_qkv = lax.all_gather(
        got_qkv.reshape(parts_c * rows_d, qkv_cols // groups), f_axes, axis=0, tiled=True
    )
    w_qkv = gather_blocks(got_qkv, g_axes, 1)
    out_cols = model_width // groups
    mine_out = take(w_out.reshape(-1, groups, out_cols).transpose(1, 0, 2), g_here)
    got_out = lax.all_gather(mine_out, f_axes, axis=0, tiled=True)
    w_mix = gather_blocks(got_out, g_axes, 1)
    full_router = lax.all_gather(w_router, c_axes + f_axes, axis=0, tiled=True)

    def fetch(pieces):
        got = all_to_all(team_axes, lambda other: take(pieces, g_here * team + other))
        return gather_halves(got, far_axes)

    full_gate = fetch(w_gate).reshape(model_width, hidden_width)
    full_up = fetch(w_up).reshape(model_width, hidden_width)
    got_down = own_first(fetch(w_down), far_axes)
    full_down = (
        got_down.reshape(parts_far, parts_c, parts_near * rows_f, model_width)
        .transpose(1, 0, 2, 3)
        .reshape(hidden_width, model_width)
    )

    turn = g_axes + c_axes[:-1] + near_axes
    orders = [turn[step:] + turn[:step] + c_axes[-1:] for step in range(3)]
    third = (count // 3) // ROW_TILE * ROW_TILE
    cuts = [0, count - 2 * third, count - third, count]
    spans = list(zip(cuts[:-1], cuts[1:], orders))
    grads_low = [gather_rows(cotangent[0, lo:hi], order) for lo, hi, order in spans]

    masks = jnp.array(
        [
            sum(
                ((position >> step) & 1) << (len(c_axes) - 1 - step)
                for step in range(len(c_axes))
            )
            for position in range(parts_c)
        ],
        jnp.int32,
    )
    block_ids = jnp.bitwise_xor(masks, c_here)
    place = jnp.take(places[0].reshape(parts_c, count), block_ids, axis=0).reshape(-1)
    segment = jnp.take(segments[0].reshape(parts_c, count), block_ids, axis=0).reshape(-1)
    length = place.shape[0]
    allowed = (segment[:, None] == segment[None, :]) & (place[None, :] <= place[:, None])
    angle = angles(place, width)
    lin = dot(all_one, w_qkv)
    q_lin, k_lin, v_lin = (
        lin[:, :q_cols],
        lin[:, q_cols : q_cols + k_cols],
        lin[:, q_cols + k_cols :],
    )
    (query, keyed), back_heads = jax.vjp(
        lambda first, second, third, fourth: head_prep(first, second, third, fourth, angle),
        q_lin,
        k_lin,
        gain_query,
        gain_key,
    )
    query_low = query.astype(low).reshape(length, kv_heads, group, width)
    keyed_low = keyed.astype(low)
    value_low = v_lin.astype(low).reshape(length, kv_heads, width)
    scores = (
        jnp.einsum("ikgd,jkd->kgij", query_low, keyed_low, preferred_element_type=jnp.float32)
        * scale
    )
    masked = jnp.where(allowed, scores, -1e30)
    row_max = jnp.max(masked, axis=-1, keepdims=True)
    expd = jnp.exp(masked - row_max)
    row_total = jnp.sum(expd, axis=-1, keepdims=True)
    log_total = row_max + jnp.log(row_total)
    probs_low = (expd / row_total).astype(low)
    mixed = jnp.einsum("kgij,jkd->ikgd", probs_low, value_low, preferred_element_type=jnp.float32)
    mixed_low = mixed.reshape(length, q_cols).astype(low)
    resid_one = resid + scatter_rows(dot(mixed_low, w_mix), c_axes, low)

    norm_two, back_two = jax.vjp(normed, resid_one, gain_ffn)
    normed_two = norm_two.astype(low)
    logits = dot(normed_two, full_router)
    labels = jnp.arange(experts, dtype=jnp.int32)
    chosen = jnp.any(routes[0][:, :, None] == labels[None, None, :], axis=1)
    logits = jnp.where(chosen, logits, -1e30)
    powers = jnp.where(chosen, jnp.exp(logits - jnp.max(logits, axis=-1, keepdims=True)), 0.0)
    gates = powers / jnp.sum(powers, axis=-1, keepdims=True)

    rows_two = normed_two.reshape(count, parts_c, parts_far, parts_near * rows_d)
    rows_two = own_first(rows_two.transpose(2, 0, 1, 3), far_axes)
    rows_two = rows_two.transpose(1, 0, 2, 3).reshape(count, model_width)
    column = labels == expert_here
    made_parts, back_parts, d_gate_parts = [], [], []
    part_gate = part_up = part_down = 0.0
    for (lo, hi, order), grad_rows in zip(spans, grads_low):
        rows = gather_rows(rows_two[lo:hi], order)
        gate = jnp.sum(
            jnp.where(column, gather_rows(gates[lo:hi], order), 0.0), axis=1, keepdims=True
        )
        act_gate = dot(rows, full_gate)
        act_up = dot(rows, full_up)
        d_plain = dot_nt(grad_rows, full_down)
        sigmoid = jax.nn.sigmoid(act_gate)
        silu_gate = act_gate * sigmoid
        hidden = silu_gate * act_up
        d_gate = jnp.sum(hidden * d_plain, axis=1, keepdims=True)
        d_hidden = d_plain * gate
        hidden_low = (hidden * gate).astype(low)
        d_gate_low = (d_hidden * act_up * (sigmoid * (1.0 + act_gate * (1.0 - sigmoid)))).astype(low)
        d_up_low = (d_hidden * silu_gate).astype(low)
        d_rows = dot_nt(d_gate_low, full_gate) + dot_nt(d_up_low, full_up)
        back_parts.append(scatter_rows(d_rows, order, low))
        d_gate_parts.append(scatter_rows(jnp.where(column, d_gate, 0.0), order, wide))
        part_down = part_down + dot_tn(hidden_low, grad_rows)
        part_gate = part_gate + dot_tn(rows, d_gate_low)
        part_up = part_up + dot_tn(rows, d_up_low)
        made_parts.append(scatter_rows(dot(hidden_low, full_down), order, low))
    output = (resid_one + jnp.concatenate(made_parts, axis=0)).astype(low)[None]
    d_gates = jnp.concatenate(d_gate_parts, axis=0)
    d_rows_two = jnp.concatenate(back_parts, axis=0)

    def owners(stack):
        kept = scatter_halves(stack, far_axes)
        got = all_to_all(team_axes, lambda other: take(kept, other))
        return gather_blocks(got, g_axes, 0).astype(jnp.float32)

    part_down = (
        part_down.reshape(parts_c, parts_far, parts_near, rows_f, model_width)
        .transpose(1, 0, 2, 3, 4)
        .reshape(parts_far, team, rows_f, model_width)
    )
    grad_down = owners(own_first(part_down, far_axes))
    grad_gate = owners(part_gate.reshape(parts_far, team, rows_d, hidden_width))
    grad_up = owners(part_up.reshape(parts_far, team, rows_d, hidden_width))

    d_rows_two = d_rows_two.reshape(count, parts_far, parts_c, parts_near * rows_d)
    d_rows_two = own_first(d_rows_two.transpose(1, 0, 2, 3), far_axes)
    d_rows_two = d_rows_two.transpose(1, 2, 0, 3).reshape(count, model_width)
    d_logits = (gates * (d_gates - jnp.sum(gates * d_gates, axis=-1, keepdims=True))).astype(low)
    part_router = dot_tn(normed_two, d_logits)
    d_normed_two = d_rows_two + dot_nt(d_logits, full_router)
    d_resid_one, d_gain_ffn = back_two(d_normed_two)
    d_resid_one = d_resid_one + cotangent[0].astype(jnp.float32)
    share_router = lax.psum_scatter(
        part_router.astype(low), c_axes + f_axes, scatter_dimension=0, tiled=True
    )
    grad_router = sum_all(share_router.astype(jnp.float32), g_axes)

    d_branch = gather_rows(d_resid_one.astype(low), c_axes)
    d_mixed = dot_nt(d_branch, w_mix).astype(low).reshape(length, kv_heads, group, width)
    part_out = dot_tn(mixed_low, d_branch)
    again_scores = (
        jnp.einsum("ikgd,jkd->kgij", query_low, keyed_low, preferred_element_type=jnp.float32)
        * scale
    )
    probs_full = jnp.where(allowed, jnp.exp(again_scores - log_total), 0.0)
    probs_again = probs_full.astype(low)
    d_probs = jnp.einsum("ikgd,jkd->kgij", d_mixed, value_low, preferred_element_type=jnp.float32)
    row_dot = jnp.sum(probs_full * d_probs, axis=-1, keepdims=True)
    d_scores = (probs_full * (d_probs - row_dot)).astype(low)
    d_query = (
        jnp.einsum("kgij,jkd->ikgd", d_scores, keyed_low, preferred_element_type=jnp.float32)
        * scale
    )
    d_keyed = (
        jnp.einsum("kgij,ikgd->jkd", d_scores, query_low, preferred_element_type=jnp.float32)
        * scale
    )
    d_value = jnp.einsum("kgij,ikgd->jkd", probs_again, d_mixed, preferred_element_type=jnp.float32)
    d_query_round = d_query.reshape(length, heads, width).astype(low).astype(jnp.float32)
    d_keyed_round = d_keyed.astype(low).astype(jnp.float32)
    d_q_lin, d_k_lin, d_gain_query, d_gain_key = back_heads((d_query_round, d_keyed_round))
    d_lin = jnp.concatenate(
        [d_q_lin.astype(low), d_k_lin.astype(low), d_value.astype(low).reshape(length, k_cols)],
        axis=1,
    )
    part_qkv = dot_tn(all_one, d_lin)
    d_one = scatter_rows(dot_nt(d_lin, w_qkv), c_axes, low)
    d_one = (
        d_one.reshape(count, parts_f, parts_c, rows_d)
        .transpose(0, 2, 1, 3)
        .reshape(count, model_width)
    )
    d_resid, d_gain_attn = back_one(d_one)
    grad_tokens = (d_resid + d_resid_one)[None]

    share_out = scatter_blocks(
        part_out.reshape(-1, groups, out_cols).transpose(1, 0, 2), g_axes
    )
    share_out = lax.psum_scatter(share_out, f_axes, scatter_dimension=0, tiled=True)
    grad_out = gather_blocks(share_out, g_axes, 1).astype(jnp.float32)
    share_qkv = scatter_blocks(
        part_qkv.reshape(model_width, groups, qkv_cols // groups).transpose(1, 0, 2), g_axes
    )
    share_qkv = lax.psum_scatter(share_qkv, f_axes, scatter_dimension=0, tiled=True)
    share_qkv = share_qkv.reshape(parts_c, rows_d, qkv_cols // groups)
    share_qkv = all_to_all(c_axes, lambda other: take(share_qkv, other))
    grad_qkv = gather_blocks(share_qkv, g_axes, 2).astype(jnp.float32).transpose(1, 0, 2)
    grad_query = grad_qkv[:, :, :q_cols].reshape(rows_d, -1)
    grad_key = grad_qkv[:, :, q_cols : q_cols + k_cols].reshape(rows_d, -1)
    grad_value = grad_qkv[:, :, q_cols + k_cols :].reshape(rows_d, -1)

    gains = sum_all(
        jnp.concatenate([d_gain_attn, d_gain_ffn, d_gain_query, d_gain_key]), all_axes
    )
    return (
        output,
        grad_tokens,
        grad_query,
        grad_key,
        grad_value,
        grad_out,
        grad_router,
        grad_gate,
        grad_up,
        grad_down,
        gains[:model_width],
        gains[model_width : 2 * model_width],
        gains[2 * model_width : 2 * model_width + width],
        gains[2 * model_width + width :],
    )


def solution(mesh):
    def binary(letter, size):
        return tuple(letter + str(step) for step in range(size.bit_length() - 1))

    g_axes = binary("g", mesh.shape["grp"])
    c_axes = binary("c", mesh.shape["ctx"])
    f_axes = binary("f", mesh.shape["fsdp"])
    names = g_axes + c_axes + f_axes
    fine = Mesh(mesh.devices.reshape((2,) * len(names)), names)
    rows = P(g_axes + f_axes, c_axes, None)
    line = P(g_axes + f_axes, None)
    split = P(c_axes + f_axes, None)
    expert = P(None, c_axes + f_axes, None)
    whole = P()
    in_specs = (
        (rows, line, line, rows)
        + (split,) * 5
        + (expert,) * 3
        + (whole,) * 4
        + (rows,)
    )
    out_specs = (rows, rows) + (split,) * 5 + (expert,) * 3 + (whole,) * 4

    def device_part(*arrays):
        return per_device(g_axes, c_axes, f_axes, *arrays)

    return jax.shard_map(
        device_part, mesh=fine, in_specs=in_specs, out_specs=out_specs, check_vma=False
    )
```

```python
import functools
import math

import jax
import jax.numpy as jnp
from jax import lax
from jax.experimental import pallas as pl
from jax.experimental.pallas import tpu as pltpu
from jax.sharding import Mesh
from jax.sharding import PartitionSpec as P

epsilon = 1e-06
low = jnp.bfloat16
wide = jnp.float32
SWAP = [(0, 1), (1, 0)]
ROW_TILE = 16
MIB = 1 << 20
WAIT_LAST = 8
BRIEF = pl.CostEstimate(flops=0, bytes_accessed=MIB, transcendentals=0)


def normed(values, gain):
    return values * lax.rsqrt(jnp.mean(values * values, axis=-1, keepdims=True) + epsilon) * gain


def angles(place, width):
    steps = jnp.arange(width // 2).astype(jnp.float32)
    inverse = jnp.exp(steps * (-2.0 * math.log(1000000.0) / width))
    return place.astype(jnp.float32)[:, None] * inverse[None, :]


def dot(left, right):
    return jnp.dot(left, right, preferred_element_type=jnp.float32)


def dot_nt(left, right):
    return lax.dot_general(left, right, (((1,), (1,)), ((), ())), preferred_element_type=jnp.float32)


def dot_tn(left, right):
    return lax.dot_general(left, right, (((0,), (0,)), ((), ())), preferred_element_type=jnp.float32)


def after(value, *anchors):
    return lax.optimization_barrier((value,) + anchors)[0]


def flat_index(axes):
    index = 0
    for axis in axes:
        index = index * 2 + lax.axis_index(axis)
    return index


def take(stack, index):
    return lax.dynamic_index_in_dim(stack, index, 0, keepdims=False)


def take_at(stack, index, at):
    return lax.dynamic_index_in_dim(stack, index, at, keepdims=False)


def exchange(axes, pick):
    amount = 1 << len(axes)
    here = flat_index(axes)
    arrived = [pick(here)]
    for step in range(1, amount):
        pairs = [(place, place ^ step) for place in range(amount)]
        arrived.append(lax.ppermute(pick(jnp.bitwise_xor(here, step)), axes, pairs))
    return arrived


def laid_out(blocks, here, at):
    if len(blocks) == 1:
        return jnp.expand_dims(blocks[0], at)
    if len(blocks) == 2:
        first = here == 0
        return jnp.stack(
            [jnp.where(first, blocks[0], blocks[1]), jnp.where(first, blocks[1], blocks[0])], axis=at
        )
    one = blocks[0]
    held = jnp.zeros(one.shape[:at] + (len(blocks),) + one.shape[at:], one.dtype)
    for step, block in enumerate(blocks):
        held = lax.dynamic_update_index_in_dim(held, block, jnp.bitwise_xor(here, step), at)
    return held


def sems(amount):
    return pltpu.SemaphoreType.DMA((amount,))


def toward(flips):
    return {axis: 1 - lax.axis_index(axis) for axis in flips}


def remote(src, dst, send, recv, flips):
    return pltpu.make_async_remote_copy(
        src_ref=src,
        dst_ref=dst,
        send_sem=send,
        recv_sem=recv,
        device_id=toward(flips),
        device_id_type=pl.DeviceIdType.MESH,
    )


class Direct:
    def __init__(self, axes, operand, block, pick, rounds=0):
        self.axes, self.block, self.pick, self.rounds = axes, block, pick, rounds
        self.amount = 1 << len(axes)
        self.operands = [operand]
        self.results = [jax.ShapeDtypeStruct((self.amount,) + block, operand.dtype)]
        self.scratch = [
            sems(self.amount),
            sems(self.amount),
            sems(2),
            pltpu.VMEM(block, operand.dtype),
        ]
        self.steps = [
            tuple(axis for bit, axis in enumerate(reversed(axes)) if step >> bit & 1)
            for step in range(self.amount)
        ]
        self.flips = self.steps[1:]

    def begin(self, operands, target, send, recv):
        copies = []
        for step in range(1, self.amount):
            other = 0
            for axis in self.axes:
                place = lax.axis_index(axis)
                other = other * 2 + (1 - place if axis in self.steps[step] else place)
            copy = remote(
                operands[0].at[self.pick(other)],
                target,
                send.at[step],
                recv.at[step],
                self.steps[step],
            )
            copy.start()
            copies.append(copy)
        return copies

    def keep(self, operands, target, local, held):
        load = pltpu.make_async_copy(
            operands[0].at[self.pick(flat_index(self.axes))], held, local.at[0]
        )
        load.start()
        load.wait()
        store = pltpu.make_async_copy(held, target, local.at[1])
        store.start()
        store.wait()

    def run(self, operands, results, scratch):
        send, recv, local, held = scratch
        for _ in range(self.rounds):
            yield
        target = results[0].at[flat_index(self.axes)]
        copies = self.begin(operands, target, send, recv)
        self.keep(operands, target, local, held)
        for _ in range(WAIT_LAST):
            yield
        for copy in copies:
            copy.wait()


class Spread(Direct):
    def __init__(self, axes, others, operand, block):
        super().__init__(axes, operand, block, lambda place: place)
        self.others = others
        self.results = [
            jax.ShapeDtypeStruct((self.amount,) + (2,) * len(others) + block, operand.dtype)
        ]
        self.scratch += [sems(max(1, len(others))), sems(max(1, len(others)))]
        self.flips = self.flips + [(axis,) for axis in others]

    def run(self, operands, results, scratch):
        send, recv, local, held, next_send, next_recv = scratch
        here = flat_index(self.axes)
        place = {axis: lax.axis_index(axis) for axis in self.others}
        spot = tuple(place[axis] for axis in self.others)
        copies = self.begin(operands, results[0].at[(here,) + spot], send, recv)
        self.keep(operands, results[0].at[(here,) + spot], local, held)
        yield
        for copy in copies:
            copy.wait_recv()
        for stage, axis in enumerate(self.others):
            region = tuple(
                slice(None) if other in self.others[:stage] else place[other]
                for other in self.others
            )
            region = results[0].at[(slice(None),) + region]
            copy = remote(region, region, next_send.at[stage], next_recv.at[stage], (axis,))
            copy.start()
            yield
            copy.wait()
        for copy in copies:
            copy.wait_send()


class Gather:
    def __init__(self, axes, operand, parts):
        self.axes, self.parts = axes, parts
        self.operands = [operand]
        self.results = [
            jax.ShapeDtypeStruct((2,) * len(axes) + operand.shape, operand.dtype)
        ]
        amount = len(parts) * len(axes)
        self.scratch = [sems(amount), sems(amount), sems(2), pltpu.VMEM(operand.shape, operand.dtype)]
        self.flips = [(axis,) for axis in axes]

    def run(self, operands, results, scratch):
        send, recv, local, held = scratch
        place = {axis: lax.axis_index(axis) for axis in self.axes}
        load = pltpu.make_async_copy(operands[0], held, local.at[0])
        load.start()
        load.wait()
        spot = tuple(place[axis] for axis in self.axes)
        store = pltpu.make_async_copy(held, results[0].at[spot], local.at[1])
        store.start()
        store.wait()
        copies = {}

        def start(number, stage):
            lo, hi, order = self.parts[number]
            region = tuple(
                slice(None) if axis in order[:stage] else place[axis] for axis in self.axes
            )
            region = results[0].at[region + (pl.ds(lo, hi - lo),)]
            slot = number * len(self.axes) + stage
            copies[number, stage] = remote(
                region, region, send.at[slot], recv.at[slot], (order[stage],)
            )
            copies[number, stage].start()

        for number in range(len(self.parts)):
            start(number, 0)
        yield
        for stage in range(1, len(self.axes)):
            for number in range(len(self.parts)):
                copies[number, stage - 1].wait_recv()
                start(number, stage)
            yield
        for number in range(len(self.parts)):
            copies[number, len(self.axes) - 1].wait_recv()
        for copy in copies.values():
            copy.wait_send()


class Reduce:
    def __init__(self, axes, operand, parts, owners=()):
        self.axes, self.parts, self.owners = axes, parts, owners
        count, columns = operand.shape[-2:]
        self.operands = [operand]
        self.results = [jax.ShapeDtypeStruct((count, columns), low if owners else wide)]
        self.scratch = []
        for lo, hi, order in parts:
            for stage in range(len(axes)):
                left = len(axes) - 1 - stage
                self.scratch.append(pltpu.VMEM((2,) * left + (hi - lo, columns), low))
            self.scratch.append(pltpu.VMEM((2,) * (len(axes) - 1) + (hi - lo, columns), low))
        self.scratch.append(pltpu.VMEM((count, columns), wide))
        amount = len(parts) * len(axes)
        self.flips = [(axis,) for axis in axes]
        self.last = None
        if owners:
            block = (count >> len(owners), columns)
            shape = jax.ShapeDtypeStruct((1 << len(owners),) + block, low)
            self.last = Direct(owners, shape, block, lambda place: place)
            self.results = self.last.results
            self.flips = self.flips + self.last.flips
            self.scratch += [pltpu.VMEM(shape.shape, low)] + self.last.scratch
        self.scratch += [sems(amount), sems(amount), sems(len(parts) + 1)]

    def run(self, operands, results, scratch):
        stages = len(self.axes)
        send, recv, local = scratch[-3:]
        total = scratch[len(self.parts) * (stages + 1)]
        place = {axis: lax.axis_index(axis) for axis in self.axes}
        copies, loads = {}, []

        def buffers(number):
            base = number * (stages + 1)
            return scratch[base : base + stages], scratch[base + stages]

        def start(number, stage):
            lo, hi, order = self.parts[number]
            slots, held = buffers(number)
            slot = number * stages + stage
            axis = order[stage]
            if stage == 0:
                spot = tuple(
                    1 - place[other] if other == axis else slice(None) for other in self.axes
                )
                source = operands[0].at[spot + (pl.ds(lo, hi - lo),)]
            else:
                rest = [other for other in self.axes if other != order[0]]
                spot = tuple(
                    place[other]
                    if other in order[:stage]
                    else 1 - place[other]
                    if other == axis
                    else slice(None)
                    for other in rest
                )
                source = held.at[spot]
            copies[number, stage] = remote(
                source, slots[stage], send.at[slot], recv.at[slot], (axis,)
            )
            copies[number, stage].start()

        for number, (lo, hi, order) in enumerate(self.parts):
            start(number, 0)
            spot = tuple(
                place[other] if other == order[0] else slice(None) for other in self.axes
            )
            load = pltpu.make_async_copy(
                operands[0].at[spot + (pl.ds(lo, hi - lo),)], buffers(number)[1], local.at[number]
            )
            load.start()
            loads.append(load)
        yield
        for stage in range(stages):
            for number, (lo, hi, order) in enumerate(self.parts):
                slots, held = buffers(number)
                if stage == 0:
                    loads[number].wait()
                copies[number, stage].wait_recv()
                rest = [other for other in self.axes if other != order[0]]
                gone = order[: stage + 1]
                free = [other for other in rest if other not in gone]
                for code in range(1 << len(free)):
                    bits = {axis: code >> bit & 1 for bit, axis in enumerate(free)}
                    spot = tuple(bits[axis] if axis in bits else place[axis] for axis in rest)
                    slot_spot = tuple(bits[axis] for axis in free)
                    last = stage == stages - 1

                    def add(step, carry, spot=spot, slot_spot=slot_spot, last=last):
                        rows = pl.ds(pl.multiple_of(step * ROW_TILE, ROW_TILE), ROW_TILE)
                        value = held[spot + (rows,)].astype(wide)
                        value = value + slots[stage][slot_spot + (rows,)].astype(wide)
                        if last:
                            at = pl.multiple_of(step * ROW_TILE + lo, ROW_TILE)
                            total[pl.ds(at, ROW_TILE)] = value
                        else:
                            held[spot + (rows,)] = value.astype(low)
                        return carry

                    lax.fori_loop(0, (hi - lo) // ROW_TILE, add, 0)
                if stage + 1 < stages:
                    start(number, stage + 1)
            yield
        if self.last is None:
            store = pltpu.make_async_copy(total, results[0], local.at[len(self.parts)])
            store.start()
            store.wait()
        else:
            ready, *others = scratch[len(self.parts) * (stages + 1) + 1 : -3]
            ready[...] = total[...].astype(low).reshape(ready.shape)
            yield from self.last.run([ready], results, others)
        for copy in copies.values():
            copy.wait_send()


def flow_kernel(flows, *refs):
    refs = list(refs)

    def cut(amount):
        part = refs[:amount]
        del refs[:amount]
        return part

    operands = [cut(len(flow.operands)) for flow in flows]
    results = [cut(len(flow.results)) for flow in flows]
    scratch = [cut(len(flow.scratch)) for flow in flows]
    partners = []
    for flow in flows:
        partners += [flips for flips in flow.flips if flips not in partners]
    barrier = pltpu.get_barrier_semaphore()
    for flips in partners:
        pl.semaphore_signal(
            barrier, inc=1, device_id=toward(flips), device_id_type=pl.DeviceIdType.MESH
        )
    pl.semaphore_wait(barrier, len(partners))
    running = [flow.run(*parts) for flow, *parts in zip(flows, operands, results, scratch)]
    while running:
        running = [run for run in running if next(run, run) is not run]


def transfer(number, flows):
    arrays = [array for flow in flows for array in flow.operands]
    shapes = [shape for flow in flows for shape in flow.results]
    anywhere = pl.BlockSpec(memory_space=pl.ANY)
    return pl.pallas_call(
        functools.partial(flow_kernel, flows),
        out_shape=shapes,
        in_specs=[anywhere] * len(arrays),
        out_specs=[anywhere] * len(shapes),
        scratch_shapes=[one for flow in flows for one in flow.scratch],
        compiler_params=pltpu.CompilerParams(
            collective_id=number, has_side_effects=True, vmem_limit_bytes=52 * MIB
        ),
        cost_estimate=BRIEF,
    )(*arrays)


def gather_blocks(block, axes, at):
    if not axes:
        return block
    if len(axes) > 1:
        return lax.all_gather(block, axes, axis=at, tiled=True)
    other = lax.ppermute(block, axes[0], SWAP)
    first = lax.axis_index(axes[0]) == 0
    return jnp.concatenate(
        [jnp.where(first, block, other), jnp.where(first, other, block)], axis=at
    )


def sum_all(value, axes):
    for axis in axes:
        value = value + lax.ppermute(value, axis, SWAP)
    return value


def tile_of(rows, most):
    steps = -(-rows // most)
    while rows % steps or (rows // steps) % ROW_TILE:
        steps += 1
    return rows // steps


def whole_block(shape):
    return pl.BlockSpec(shape, lambda *ids: (0,) * len(shape), pipeline_mode=pl.Buffered(1))


def expert_kernel(
    rows_ref,
    grad_ref,
    gate_ref,
    in_ref,
    down_ref,
    hidden_ref,
    d_act_ref,
    d_up_ref,
    d_gate_ref,
    made_ref,
    back_ref,
):
    hidden_width = down_ref.shape[0]
    gate = gate_ref[...]
    acts = dot(rows_ref[...], in_ref[...])
    d_plain = dot_nt(grad_ref[...], down_ref[...])
    act_gate, act_up = acts[:, :hidden_width], acts[:, hidden_width:]
    sigmoid = 1.0 / (1.0 + jnp.exp(-act_gate))
    silu_gate = act_gate * sigmoid
    hidden = silu_gate * act_up
    d_gate_ref[...] = jnp.sum(hidden * d_plain, axis=1, keepdims=True)
    d_hidden = d_plain * gate
    hidden_low = (hidden * gate).astype(low)
    d_act_gate = d_hidden * act_up * (sigmoid * (1.0 + act_gate * (1.0 - sigmoid)))
    d_in = jnp.concatenate([d_act_gate.astype(low), (d_hidden * silu_gate).astype(low)], axis=1)
    hidden_ref[...] = hidden_low
    d_act_ref[...] = d_in[:, :hidden_width]
    d_up_ref[...] = d_in[:, hidden_width:]
    back_ref[...] = dot_nt(d_in, in_ref[...]).astype(low)
    made_ref[...] = dot(hidden_low, down_ref[...]).astype(low)


def expert_rows(rows, grad_rows, gate, full_in, full_down):
    amount, model_width = rows.shape
    hidden_width = full_down.shape[0]
    tile = tile_of(amount, 256)

    def by_rows(columns):
        return pl.BlockSpec((tile, columns), lambda step: (step, 0))

    outs = [
        (hidden_width, low),
        (hidden_width, low),
        (hidden_width, low),
        (1, wide),
        (model_width, low),
        (model_width, low),
    ]
    return pl.pallas_call(
        expert_kernel,
        grid=(amount // tile,),
        in_specs=[
            by_rows(model_width),
            by_rows(model_width),
            by_rows(1),
            whole_block(full_in.shape),
            whole_block(full_down.shape),
        ],
        out_specs=[by_rows(columns) for columns, _ in outs],
        out_shape=[jax.ShapeDtypeStruct((amount, columns), kind) for columns, kind in outs],
        compiler_params=pltpu.CompilerParams(vmem_limit_bytes=52 * MIB),
        cost_estimate=BRIEF,
    )(rows, grad_rows, gate, full_in, full_down)


def weight_kernel(amount, *refs):
    total = dot_tn(refs[0][...], refs[amount][...])
    for step in range(1, amount):
        total = total + dot_tn(refs[step][...], refs[amount + step][...])
    refs[-1][...] = total.astype(low)


def weight_grad(lefts, rights, tile=256):
    amount = len(lefts)
    columns, out_columns = lefts[0].shape[1], rights[0].shape[1]
    rows = sum(left.shape[0] for left in lefts)
    return pl.pallas_call(
        functools.partial(weight_kernel, amount),
        grid=(columns // tile,),
        in_specs=[pl.BlockSpec((left.shape[0], tile), lambda step: (0, step)) for left in lefts]
        + [whole_block(right.shape) for right in rights],
        out_specs=pl.BlockSpec((tile, out_columns), lambda step: (step, 0)),
        out_shape=jax.ShapeDtypeStruct((columns, out_columns), low),
        compiler_params=pltpu.CompilerParams(vmem_limit_bytes=52 * MIB),
        cost_estimate=BRIEF,
    )(*lefts, *rights)


def turned(values, cosine, sine):
    return values * cosine + pltpu.roll(values, values.shape[1] // 2, 1) * sine


def turned_back(grads, cosine, sine):
    return grads * cosine + pltpu.roll(grads * sine, grads.shape[1] // 2, 1)


def head_scale(values):
    return lax.rsqrt(jnp.mean(values * values, axis=1, keepdims=True) + epsilon)


def prep_kernel(
    heads, rows_ref, w_ref, cosine_ref, sine_ref, gain_q, gain_k, lin_ref, query_ref, keyed_ref, value_ref
):
    width = gain_q.shape[1]
    cosine, sine = cosine_ref[...], sine_ref[...]
    lin = dot(rows_ref[...], w_ref[...])
    lin_ref[...] = lin[:, : (heads + 1) * width]
    for head in range(heads + 1):
        span = slice(head * width, (head + 1) * width)
        values = lin[:, span]
        gain = gain_q[...] if head < heads else gain_k[...]
        made = turned(values * head_scale(values) * gain, cosine, sine).astype(low)
        if head < heads:
            query_ref[:, span] = made
        else:
            keyed_ref[...] = made
    value_ref[...] = lin[:, (heads + 1) * width :].astype(low)


def unprep_kernel(
    heads,
    scale,
    d_query_ref,
    d_keyed_ref,
    d_value_ref,
    lin_ref,
    w_ref,
    cosine_ref,
    sine_ref,
    gain_q,
    gain_k,
    d_lin_ref,
    d_one_ref,
    d_gain_q,
    d_gain_k,
):
    width = gain_q.shape[1]
    cosine, sine = cosine_ref[...], sine_ref[...]

    @pl.when(pl.program_id(0) == 0)
    def _():
        d_gain_q[...] = jnp.zeros_like(d_gain_q)
        d_gain_k[...] = jnp.zeros_like(d_gain_k)

    for head in range(heads + 1):
        span = slice(head * width, (head + 1) * width)
        values = lin_ref[:, span]
        if head < heads:
            grads, gain, d_gain = d_query_ref[:, span].astype(wide), gain_q[...], d_gain_q
        else:
            grads, gain, d_gain = d_keyed_ref[...] * scale, gain_k[...], d_gain_k
        grads = turned_back(grads, cosine, sine)
        factor = head_scale(values)
        plain = values * factor
        d_gain[...] += jnp.sum(grads * plain, axis=0, keepdims=True)
        grads = grads * gain
        mean = jnp.mean(grads * plain, axis=1, keepdims=True)
        d_lin_ref[:, span] = (factor * (grads - plain * mean)).astype(low)
    d_lin_ref[:, (heads + 1) * width :] = d_value_ref[...].astype(low)
    d_one_ref[...] = dot_nt(d_lin_ref[...], w_ref[...]).astype(low)


def row_call(kernel, rows, tiled, fixed, outs, sums):
    tile = tile_of(rows, 256)

    def by_rows(columns):
        return pl.BlockSpec((tile, columns), lambda step: (step, 0))

    return pl.pallas_call(
        kernel,
        grid=(rows // tile,),
        in_specs=[
            whole_block(array.shape) if number in fixed else by_rows(array.shape[1])
            for number, array in enumerate(tiled)
        ],
        out_specs=[by_rows(columns) for columns, _ in outs]
        + [pl.BlockSpec((1, columns), lambda step: (0, 0)) for columns in sums],
        out_shape=[jax.ShapeDtypeStruct((rows, columns), kind) for columns, kind in outs]
        + [jax.ShapeDtypeStruct((1, columns), wide) for columns in sums],
        compiler_params=pltpu.CompilerParams(vmem_limit_bytes=48 * MIB),
        cost_estimate=BRIEF,
    )(*tiled)


def mask_tile(bias, k_place, k_segment, q_place, q_segment):
    allowed = (k_segment[...] == q_segment[0]) & (k_place[...] <= q_place[0])
    bias[...] = jnp.where(allowed, 0.0, -1e30)


def ahead_kernel(
    scale, k_place, k_segment, q_place, q_segment, q_ref, k_ref, vt_ref, mixed_ref, total_ref, bias
):
    @pl.when(pl.program_id(2) == 0)
    def _():
        mask_tile(bias, k_place.at[0], k_segment.at[0], q_place, q_segment)

    scores = dot_nt(k_ref[0], q_ref[0]) * scale + bias[...]
    row_max = jnp.max(scores, axis=0, keepdims=True)
    expd = jnp.exp(scores - row_max)
    row_total = jnp.sum(expd, axis=0, keepdims=True)
    mixed = dot(vt_ref[0], expd.astype(low)) / row_total
    mixed_ref[0] = mixed.T.astype(low)
    total_ref[0, 0] = row_max + jnp.log(row_total)


def behind_kernel(
    scale,
    k_place,
    k_segment,
    q_place,
    q_segment,
    q_ref,
    d_mixed_ref,
    k_ref,
    v_ref,
    kt_ref,
    total_ref,
    d_q_ref,
    d_k_ref,
    d_v_ref,
    bias,
):
    @pl.when(pl.program_id(2) == 0)
    def _():
        mask_tile(bias, k_place.at[0], k_segment.at[0], q_place, q_segment)

    @pl.when((pl.program_id(1) == 0) & (pl.program_id(2) == 0))
    def _():
        d_k_ref[...] = jnp.zeros_like(d_k_ref)
        d_v_ref[...] = jnp.zeros_like(d_v_ref)

    query, d_mixed = q_ref[0], d_mixed_ref[0]
    probs = jnp.exp(dot_nt(k_ref[0], query) * scale + bias[...] - total_ref[0, 0])
    d_probs = dot_nt(v_ref[0], d_mixed)
    row_dot = jnp.sum(probs * d_probs, axis=0, keepdims=True)
    d_scores = (probs * (d_probs - row_dot)).astype(low)
    d_v_ref[0] += dot(probs.astype(low), d_mixed)
    d_k_ref[0] += dot(d_scores, query)
    d_q_ref[0] = (dot(kt_ref[0], d_scores) * scale).T.astype(low)


def attention_call(kernel, marks, arrays, kinds, outs, width, scale, work):
    place, segment = marks
    seqs, length = place.shape
    tile = min(256, length)
    heads = arrays[0].shape[2] // width
    specs = {
        "query": pl.BlockSpec((1, tile, width), lambda s, i, h: (s, i, h)),
        "keys": pl.BlockSpec((1, length, width), lambda s, i, h: (s, 0, 0)),
        "flat": pl.BlockSpec((1, width, length), lambda s, i, h: (s, 0, 0)),
        "total": pl.BlockSpec((1, 1, 1, tile), lambda s, i, h: (s, h, 0, i)),
    }
    column = pl.BlockSpec((1, length, 1), lambda s, i, h: (s, 0, 0))
    row = pl.BlockSpec((1, 1, tile), lambda s, i, h: (s, 0, i))
    return pl.pallas_call(
        functools.partial(kernel, scale),
        grid=(seqs, length // tile, heads),
        in_specs=[column, column, row, row] + [specs[kind] for kind in kinds],
        out_specs=[specs[kind] for kind, _ in outs],
        out_shape=[shape for _, shape in outs],
        scratch_shapes=[pltpu.VMEM((length, tile), wide)],
        compiler_params=pltpu.CompilerParams(vmem_limit_bytes=48 * MIB),
        cost_estimate=BRIEF,
    )(place[:, :, None], segment[:, :, None], place[:, None, :], segment[:, None, :], *arrays)


def per_device(
    g_axes,
    c_axes,
    f_axes,
    tokens,
    places,
    segments,
    routes,
    w_query,
    w_key,
    w_value,
    w_out,
    w_router,
    w_gate,
    w_up,
    w_down,
    gain_attn,
    gain_ffn,
    gain_query,
    gain_key,
    cotangent,
):
    groups, parts_c, parts_f = 1 << len(g_axes), 1 << len(c_axes), 1 << len(f_axes)
    count = tokens.shape[1]
    width = gain_query.shape[0]
    model_width = tokens.shape[2]
    kv_heads = w_key.shape[1] // width // parts_c
    assert kv_heads == 1
    heads = w_query.shape[1] // width // parts_c // groups
    experts = w_gate.shape[0]
    hidden_width = w_gate.shape[2]
    scale = 1.0 / math.sqrt(width)
    rows_d = w_query.shape[0]
    rows_o = w_out.shape[0]
    rows_f = w_down.shape[1]
    pair_count = experts.bit_length() - 1 - len(g_axes) - len(c_axes)
    assert 0 <= pair_count <= len(f_axes)
    far_axes = f_axes[: len(f_axes) - pair_count]
    near_axes = f_axes[len(f_axes) - pair_count :]
    parts_near = 1 << len(near_axes)
    team_axes = c_axes + near_axes
    team = parts_c * parts_near
    own_axes = c_axes + f_axes
    plane_axes = g_axes + c_axes
    cluster_axes = g_axes + team_axes
    all_axes = g_axes + c_axes + f_axes
    g_here = flat_index(g_axes)
    core = c_axes[-1:]
    plane_shape = (2,) * len(plane_axes) + (count, model_width)
    cluster_shape = (2,) * len(cluster_axes) + (count, model_width)
    turn = g_axes + c_axes[:-1]
    half = count // 2
    plane_parts = [(0, half, turn), (half, count, turn[1:] + turn[:1])]
    turn = turn + near_axes
    third = (count // 3) // ROW_TILE * ROW_TILE
    cuts = [0, count - 2 * third, count - third, count]
    cluster_parts = [
        (cuts[step], cuts[step + 1], turn[step:] + turn[:step]) for step in range(len(cuts) - 1)
    ]
    def core_last(parts):
        return [(lo, hi, order + core) for lo, hi, order in parts]

    def core_first(parts):
        return [(lo, hi, core + order) for lo, hi, order in parts]

    q_cols = heads * width
    qkv_cols = q_cols + 2 * width
    even = rows_o % (groups * width) == 0
    if even:
        own_query = w_query.reshape(rows_d, parts_c, parts_f, groups, q_cols // parts_f)
        own_query = own_query.transpose(3, 1, 0, 2, 4)
    else:
        own_query = w_query.reshape(rows_d, parts_c, groups, q_cols).transpose(2, 1, 0, 3)
    own_query = take(own_query.reshape(groups, parts_c, rows_d, q_cols), g_here)
    mine_qkv = jnp.concatenate(
        [
            own_query,
            w_key.reshape(rows_d, parts_c, width).transpose(1, 0, 2),
            w_value.reshape(rows_d, parts_c, width).transpose(1, 0, 2),
        ],
        axis=2,
    )
    own_in = jnp.concatenate([w_gate, w_up], axis=2)
    wide_router = jnp.pad(w_router, ((0, 0), (0, width - experts)))
    resid = tokens[0].astype(jnp.float32)
    norm_one, back_one = jax.vjp(normed, resid, gain_attn)

    def own_experts(place):
        return flat_index(g_axes) * parts_c + place

    def by_team(pieces):
        return pieces.reshape((groups * parts_c, parts_near) + pieces.shape[1:])

    mine_out = take(w_out.reshape(groups, -1, model_width), g_here) if even else w_out
    all_grads = lax.all_gather(cotangent[0], cluster_axes, axis=0, tiled=True)
    w_qkv, all_one, full_router, marks, w_mix, got_in, got_down = transfer(
        1,
        [
            Spread(c_axes, f_axes, mine_qkv, (rows_d, qkv_cols)),
            Gather(plane_axes, norm_one.astype(low), core_last(plane_parts)),
            Direct(own_axes, wide_router[None], wide_router.shape, lambda place: 0),
            Direct(
                g_axes,
                jnp.stack([places[0], segments[0]])[None],
                (2,) + places.shape[1:],
                lambda place: 0,
            ),
            Gather(f_axes, mine_out, [(0, mine_out.shape[0], f_axes)]),
            Direct(c_axes, by_team(own_in), (parts_near,) + own_in.shape[1:], own_experts, 2),
            Direct(c_axes, by_team(w_down), (parts_near,) + w_down.shape[1:], own_experts, 2),
        ],
    )
    w_qkv = w_qkv.reshape(model_width, qkv_cols)
    all_one = all_one.reshape(-1, model_width)
    full_router = full_router.reshape(model_width, width)[:, :experts]

    w_mix = w_mix.reshape(-1, model_width)
    if not even:
        w_mix = take(w_mix.reshape(groups, q_cols, model_width), g_here)
    f_here = flat_index(f_axes)
    near_here = flat_index(near_axes)

    def whole_expert(got):
        arrived = exchange(f_axes, lambda other: take_at(got, other % parts_near, 1))
        return laid_out(arrived, f_here, 1)

    full_in = whole_expert(got_in).reshape(model_width, 2 * hidden_width)
    full_down = whole_expert(got_down).reshape(hidden_width, model_width)

    place, segment = marks[:, 0], marks[:, 1]
    length = place.shape[1]
    angle = angles(place.reshape(-1), width)
    cosine, sine = jnp.cos(angle), jnp.sin(angle)
    cosine = jnp.concatenate([cosine, cosine], axis=1)
    sine = jnp.concatenate([-sine, sine], axis=1)
    tables = (cosine, sine, gain_query[None], gain_key[None])
    rows = groups * length
    lin, query_low, keyed_low, value_low = row_call(
        functools.partial(prep_kernel, heads),
        rows,
        (all_one, w_qkv) + tables,
        (1, 4, 5),
        [(q_cols + width, wide), (q_cols, low), (width, low), (width, low)],
        [],
    )
    query_low = query_low.reshape(groups, length, q_cols)
    keyed_low = keyed_low.reshape(groups, length, width)
    value_low = value_low.reshape(groups, length, width)
    total_shape = jax.ShapeDtypeStruct((groups, heads, 1, length), wide)
    mixed_low, log_total = attention_call(
        ahead_kernel,
        (place, segment),
        (query_low, keyed_low, value_low.transpose(0, 2, 1)),
        ("query", "keys", "flat"),
        [("query", jax.ShapeDtypeStruct(query_low.shape, low)), ("total", total_shape)],
        width,
        scale,
        4,
    )
    mixed_rows = mixed_low.reshape(groups * length, q_cols)
    branch = dot(mixed_rows, w_mix).astype(low).reshape(plane_shape)
    (branch,) = transfer(2, [Reduce(plane_axes, branch, core_first(plane_parts))])
    resid_one = resid + branch

    norm_two, back_two = jax.vjp(normed, resid_one, gain_ffn)
    normed_two = norm_two.astype(low)
    logits = dot(normed_two, full_router)
    labels = jnp.arange(experts, dtype=jnp.int32)
    chosen = jnp.any(routes[0][:, :, None] == labels[None, None, :], axis=1)
    logits = jnp.where(chosen, logits, -1e30)
    powers = jnp.where(chosen, jnp.exp(logits - jnp.max(logits, axis=-1, keepdims=True)), 0.0)
    gates = powers / jnp.sum(powers, axis=-1, keepdims=True)

    all_two, all_gates = transfer(
        3,
        [
            Gather(cluster_axes, normed_two, core_last(cluster_parts)),
            Gather(cluster_axes, gates.T, [(0, experts, turn + core)]),
        ],
    )
    all_two = all_two.reshape(-1, model_width)
    gate = lax.dynamic_index_in_dim(
        all_gates.reshape(-1, experts, count), flat_index(cluster_axes), 1, keepdims=False
    )
    hiddens, d_acts, d_ups, d_gate, made, back = expert_rows(
        all_two, all_grads, gate.reshape(-1, 1), full_in, full_down
    )
    d_rows_two, d_gates = transfer(
        4,
        [
            Reduce(cluster_axes, back.reshape(cluster_shape), core_first(cluster_parts)),
            Direct(
                cluster_axes, d_gate.reshape(experts, 1, count), (1, count), lambda place: place
            ),
        ],
    )

    def over_fsdp(part, rows):
        stack = part.reshape(parts_c, parts_f, rows, -1)
        arrived = exchange(f_axes, lambda other: take_at(stack, other, 1))
        sums = []
        for near in range(parts_near):
            total = arrived[near].astype(wide)
            for step in range(near + parts_near, parts_f, parts_near):
                total = total + arrived[step].astype(wide)
            sums.append(total.astype(low))
        return laid_out(sums, near_here, 1)

    part_down = weight_grad([after(hiddens, d_rows_two)], [all_grads])
    part_gate = weight_grad([all_two], [after(d_acts, part_down)])
    part_up = weight_grad([all_two], [after(d_ups, part_gate)])
    share_down = over_fsdp(part_down, rows_f)
    share_gate = over_fsdp(part_gate, rows_d)
    share_up = over_fsdp(part_up, rows_d)
    d_gates = d_gates.reshape(experts, count).T

    d_logits = (gates * (d_gates - jnp.sum(gates * d_gates, axis=-1, keepdims=True))).astype(low)
    part_router = dot_tn(normed_two, d_logits)
    d_normed_two = d_rows_two + dot_nt(d_logits, full_router)
    d_resid_one, d_gain_ffn = back_two(d_normed_two)
    d_resid_one = d_resid_one + cotangent[0].astype(jnp.float32)
    wide_part = jnp.pad(part_router.astype(low), ((0, 0), (0, width - experts)))
    share_router = lax.psum_scatter(wide_part, own_axes, scatter_dimension=0, tiled=True)
    grad_router = sum_all(share_router[:, :experts].astype(jnp.float32), g_axes)

    made_shape = (2,) * len(plane_axes) + (parts_near * count, model_width)
    made_parts = [(lo * parts_near, hi * parts_near, order) for lo, hi, order in plane_parts]
    d_branch, made = transfer(
        5,
        [
            Gather(plane_axes, d_resid_one.astype(low), core_last(plane_parts)),
            Reduce(plane_axes, made.reshape(made_shape), core_first(made_parts)),
        ],
    )
    d_branch = d_branch.reshape(-1, model_width)
    d_mixed = dot_nt(d_branch, w_mix).astype(low).reshape(query_low.shape)
    shapes = [
        jax.ShapeDtypeStruct(query_low.shape, low),
        jax.ShapeDtypeStruct(keyed_low.shape, wide),
        jax.ShapeDtypeStruct(keyed_low.shape, wide),
    ]
    d_query, d_keyed, d_value = attention_call(
        behind_kernel,
        (place, segment),
        (query_low, d_mixed, keyed_low, value_low, keyed_low.transpose(0, 2, 1), log_total),
        ("query", "query", "keys", "keys", "flat", "total"),
        list(zip(("query", "keys", "keys"), shapes)),
        width,
        scale,
        10,
    )
    def to_owner(share):
        return Direct(c_axes, share, share.shape[1:], lambda place: place)

    share_down, share_gate = transfer(
        6, [to_owner(after(share_down, d_query)), to_owner(after(share_gate, d_query))]
    )
    share_down = gather_blocks(share_down.reshape((1, -1) + share_down.shape[2:]), g_axes, 0)
    share_gate = gather_blocks(share_gate.reshape((1, -1) + share_gate.shape[2:]), g_axes, 0)
    d_lin, d_one, d_gain_query, d_gain_key = row_call(
        functools.partial(unprep_kernel, heads, scale),
        rows,
        (
            d_query.reshape(rows, q_cols),
            d_keyed.reshape(rows, width),
            d_value.reshape(rows, width),
            lin,
            w_qkv,
        )
        + tables,
        (4, 7, 8),
        [(qkv_cols, low), (model_width, low)],
        [width, width],
    )
    d_one = d_one.reshape(plane_shape)
    part_out = weight_grad([mixed_rows], [d_branch])
    part_qkv = weight_grad([all_one], [d_lin])

    def by_f(part):
        stack = part.reshape(parts_c, parts_f, rows_d, -1).transpose(1, 0, 2, 3)
        return stack.reshape((2,) * len(f_axes) + (parts_c * rows_d, -1))

    flows = [
        Reduce(
            f_axes,
            after(by_f(part_qkv), share_down),
            [(0, parts_c * rows_d, f_axes[::-1])],
            c_axes,
        ),
        Reduce(plane_axes, d_one, core_first(plane_parts)),
        to_owner(share_up),
    ]
    if near_axes:
        near_shape = (2,) * len(near_axes) + (count, model_width)
        near_flow = Reduce(
            near_axes, made.astype(low).reshape(near_shape), [(0, count, near_axes)]
        )
        flows.append(near_flow)
    if even:
        rows = q_cols // parts_f
        stack = part_out.reshape((2,) * len(f_axes) + (rows, model_width))
        flows.append(Reduce(f_axes, stack, [(0, rows, f_axes[::-1])]))
    share_qkv, d_one, share_up, *rest = transfer(7, flows)
    if near_axes:
        made = rest.pop(0)
    output = (resid_one + made).astype(low)[None]
    d_resid, d_gain_attn = back_one(d_one)
    grad_tokens = (d_resid + d_resid_one)[None]
    share_up = gather_blocks(share_up.reshape((1, -1) + share_up.shape[2:]), g_axes, 0)
    grad_gate, grad_up, grad_down = [
        share.reshape((experts,) + share.shape[2:]).astype(wide)
        for share in (share_gate, share_up, share_down)
    ]
    if even:
        share_out = rest[0].astype(low)[None]
        grad_out = gather_blocks(share_out, g_axes, 0).astype(wide).reshape(rows_o, model_width)
    else:
        stack = jnp.where(jnp.arange(groups)[:, None, None] == g_here, part_out[None], 0)
        share_out = lax.psum_scatter(
            stack.reshape(groups * q_cols, model_width), f_axes, scatter_dimension=0, tiled=True
        )
        grad_out = sum_all(share_out.astype(wide), g_axes)
    all_qkv = gather_blocks(share_qkv[None], g_axes, 0).astype(wide)
    grad_query = all_qkv[:, :, :, :q_cols]
    if even:
        grad_query = grad_query.reshape(groups, parts_c, rows_d, parts_f, q_cols // parts_f)
        grad_query = grad_query.transpose(2, 1, 3, 0, 4).reshape(rows_d, -1)
    else:
        grad_query = grad_query.transpose(2, 1, 0, 3).reshape(rows_d, -1)
    grad_kv = jnp.sum(all_qkv[:, :, :, q_cols:], axis=0).transpose(1, 0, 2)
    grad_key = grad_kv[:, :, :width].reshape(rows_d, -1)
    grad_value = grad_kv[:, :, width:].reshape(rows_d, -1)

    gains = sum_all(
        jnp.concatenate([d_gain_attn, d_gain_ffn, d_gain_query[0], d_gain_key[0]]), all_axes
    )
    return (
        output,
        grad_tokens,
        grad_query,
        grad_key,
        grad_value,
        grad_out,
        grad_router,
        grad_gate,
        grad_up,
        grad_down,
        gains[:model_width],
        gains[model_width : 2 * model_width],
        gains[2 * model_width : 2 * model_width + width],
        gains[2 * model_width + width :],
    )


def solution(mesh):
    def binary(letter, size):
        return tuple(letter + str(step) for step in range(size.bit_length() - 1))

    g_axes = binary("g", mesh.shape["grp"])
    c_axes = binary("c", mesh.shape["ctx"])
    f_axes = binary("f", mesh.shape["fsdp"])
    names = g_axes + c_axes + f_axes
    fine = Mesh(mesh.devices.reshape((2,) * len(names)), names)
    rows = P(g_axes + f_axes, c_axes, None)
    line = P(g_axes + f_axes, None)
    split = P(c_axes + f_axes, None)
    expert = P(None, c_axes + f_axes, None)
    whole = P()
    in_specs = (
        (rows, line, line, rows)
        + (split,) * 5
        + (expert,) * 3
        + (whole,) * 4
        + (rows,)
    )
    out_specs = (rows, rows) + (split,) * 5 + (expert,) * 3 + (whole,) * 4

    def device_part(*arrays):
        return per_device(g_axes, c_axes, f_axes, *arrays)

    return jax.shard_map(
        device_part, mesh=fine, in_specs=in_specs, out_specs=out_specs, check_vma=False
    )
```

```python
import functools
import math

import jax
import jax.numpy as jnp
from jax import lax
from jax.experimental import pallas as pl
from jax.experimental.pallas import tpu as pltpu
from jax.sharding import Mesh
from jax.sharding import PartitionSpec as P

epsilon = 1e-06
low = jnp.bfloat16
wide = jnp.float32
SWAP = [(0, 1), (1, 0)]
ROW_TILE = 16
MIB = 1 << 20
WAIT_LAST = 8
LONG = 16
BRIEF = pl.CostEstimate(flops=0, bytes_accessed=0, transcendentals=0)


def normed(values, gain):
    return values * lax.rsqrt(jnp.mean(values * values, axis=-1, keepdims=True) + epsilon) * gain


def dot(left, right):
    return jnp.dot(left, right, preferred_element_type=jnp.float32)


def dot_nt(left, right):
    return lax.dot_general(left, right, (((1,), (1,)), ((), ())), preferred_element_type=jnp.float32)


def dot_tn(left, right):
    return lax.dot_general(left, right, (((0,), (0,)), ((), ())), preferred_element_type=jnp.float32)


def zero_of(anchor):
    return jnp.minimum(jnp.abs(anchor[(0,) * anchor.ndim].astype(wide)), 0.0)


def flat_index(axes):
    index = 0
    for axis in axes:
        index = index * 2 + lax.axis_index(axis)
    return index


def take(stack, index):
    return lax.dynamic_index_in_dim(stack, index, 0, keepdims=False)


def take_at(stack, index, at):
    return lax.dynamic_index_in_dim(stack, index, at, keepdims=False)


def sems(amount):
    return pltpu.SemaphoreType.DMA((amount,))


def toward(flips):
    return {axis: 1 - lax.axis_index(axis) for axis in flips}


def remote(src, dst, send, recv, flips):
    return pltpu.make_async_remote_copy(
        src_ref=src,
        dst_ref=dst,
        send_sem=send,
        recv_sem=recv,
        device_id=toward(flips),
        device_id_type=pl.DeviceIdType.MESH,
    )


class Direct:
    def __init__(self, axes, operand, block, pick=None, rounds=0):
        self.axes, self.block, self.pick, self.rounds = axes, block, pick, rounds
        self.amount = 1 << len(axes)
        self.operands = [operand]
        self.results = [jax.ShapeDtypeStruct((self.amount,) + block, operand.dtype)]
        self.scratch = [
            sems(self.amount),
            sems(self.amount),
            sems(2),
            pltpu.VMEM(block, operand.dtype),
        ]
        self.steps = [
            tuple(axis for bit, axis in enumerate(reversed(axes)) if step >> bit & 1)
            for step in range(self.amount)
        ]
        self.flips = self.steps[1:]

    def begin(self, operands, target, send, recv):
        copies = []
        for step in range(1, self.amount):
            other = 0
            for axis in self.axes:
                place = lax.axis_index(axis)
                other = other * 2 + (1 - place if axis in self.steps[step] else place)
            copy = remote(
                operands[0].at[step if self.pick is None else self.pick(other)],
                target,
                send.at[step],
                recv.at[step],
                self.steps[step],
            )
            copy.start()
            copies.append(copy)
        return copies

    def keep(self, operands, target, local, held):
        own = 0 if self.pick is None else self.pick(flat_index(self.axes))
        load = pltpu.make_async_copy(operands[0].at[own], held, local.at[0])
        load.start()
        load.wait()
        store = pltpu.make_async_copy(held, target, local.at[1])
        store.start()
        store.wait()

    def run(self, operands, results, scratch):
        send, recv, local, held = scratch
        for _ in range(self.rounds):
            yield
        target = results[0].at[flat_index(self.axes)]
        copies = self.begin(operands, target, send, recv)
        self.keep(operands, target, local, held)
        for _ in range(WAIT_LAST):
            yield
        for copy in copies:
            copy.wait()


class Spread(Direct):
    def __init__(self, axes, others, operand, block, pick=lambda place: place):
        super().__init__(axes, operand, block, pick)
        self.others = others
        self.results = [
            jax.ShapeDtypeStruct((self.amount,) + (2,) * len(others) + block, operand.dtype)
        ]
        self.scratch += [sems(max(1, len(others))), sems(max(1, len(others)))]
        self.flips = self.flips + [(axis,) for axis in others]

    def run(self, operands, results, scratch):
        send, recv, local, held, next_send, next_recv = scratch
        here = flat_index(self.axes)
        place = {axis: lax.axis_index(axis) for axis in self.others}
        spot = tuple(place[axis] for axis in self.others)
        copies = self.begin(operands, results[0].at[(here,) + spot], send, recv)
        self.keep(operands, results[0].at[(here,) + spot], local, held)
        yield
        for copy in copies:
            copy.wait_recv()
        for stage, axis in enumerate(self.others):
            region = tuple(
                slice(None) if other in self.others[:stage] else place[other]
                for other in self.others
            )
            region = results[0].at[(slice(None),) + region]
            copy = remote(region, region, next_send.at[stage], next_recv.at[stage], (axis,))
            copy.start()
            yield
            copy.wait()
        for copy in copies:
            copy.wait_send()


class Gather:
    def __init__(self, axes, operand, parts):
        self.axes, self.parts = axes, parts
        self.operands = [operand]
        self.results = [
            jax.ShapeDtypeStruct((2,) * len(axes) + operand.shape, operand.dtype)
        ]
        amount = len(parts) * len(axes)
        self.scratch = [sems(amount), sems(amount), sems(2), pltpu.VMEM(operand.shape, operand.dtype)]
        self.flips = [(axis,) for axis in axes]

    def run(self, operands, results, scratch):
        send, recv, local, held = scratch
        place = {axis: lax.axis_index(axis) for axis in self.axes}
        load = pltpu.make_async_copy(operands[0], held, local.at[0])
        load.start()
        load.wait()
        spot = tuple(place[axis] for axis in self.axes)
        store = pltpu.make_async_copy(held, results[0].at[spot], local.at[1])
        store.start()
        store.wait()
        copies = {}

        def start(number, stage):
            lo, hi, order = self.parts[number]
            region = tuple(
                slice(None) if axis in order[:stage] else place[axis] for axis in self.axes
            )
            region = results[0].at[region + (pl.ds(lo, hi - lo),)]
            slot = number * len(self.axes) + stage
            copies[number, stage] = remote(
                region, region, send.at[slot], recv.at[slot], (order[stage],)
            )
            copies[number, stage].start()

        for number in range(len(self.parts)):
            start(number, 0)
        yield
        for stage in range(1, len(self.axes)):
            for number in range(len(self.parts)):
                copies[number, stage - 1].wait_recv()
                start(number, stage)
            yield
        for number in range(len(self.parts)):
            copies[number, len(self.axes) - 1].wait_recv()
        for copy in copies.values():
            copy.wait_send()


class Reduce:
    def __init__(self, axes, operand, parts, ready=None, last=None, by_distance=False):
        self.axes, self.parts, self.by_distance = axes, parts, by_distance
        count, columns = operand.shape[-2:]
        self.operands = [operand]
        self.results = [jax.ShapeDtypeStruct((count, columns), wide)]
        self.scratch = []
        for lo, hi, order in parts:
            for stage in range(len(axes)):
                left = len(axes) - 1 - stage
                self.scratch.append(pltpu.VMEM((2,) * left + (hi - lo, columns), low))
            self.scratch.append(pltpu.VMEM((2,) * (len(axes) - 1) + (hi - lo, columns), low))
        self.scratch.append(pltpu.VMEM((count, columns), wide))
        amount = len(parts) * len(axes)
        self.flips = [(axis,) for axis in axes]
        self.last = None
        if last is not None:
            self.last = last(ready)
            self.results = self.last.results
            self.flips = self.flips + self.last.flips
            self.scratch += [pltpu.VMEM(ready.shape, low)] + self.last.scratch
        self.scratch += [sems(amount), sems(amount), sems(len(parts) + 1)]

    def run(self, operands, results, scratch):
        stages = len(self.axes)
        send, recv, local = scratch[-3:]
        total = scratch[len(self.parts) * (stages + 1)]
        place = {axis: 0 if self.by_distance else lax.axis_index(axis) for axis in self.axes}
        copies, loads = {}, []

        def buffers(number):
            base = number * (stages + 1)
            return scratch[base : base + stages], scratch[base + stages]

        def start(number, stage):
            lo, hi, order = self.parts[number]
            slots, held = buffers(number)
            slot = number * stages + stage
            axis = order[stage]
            if stage == 0:
                spot = tuple(
                    1 - place[other] if other == axis else slice(None) for other in self.axes
                )
                source = operands[0].at[spot + (pl.ds(lo, hi - lo),)]
            else:
                rest = [other for other in self.axes if other != order[0]]
                spot = tuple(
                    place[other]
                    if other in order[:stage]
                    else 1 - place[other]
                    if other == axis
                    else slice(None)
                    for other in rest
                )
                source = held.at[spot]
            copies[number, stage] = remote(
                source, slots[stage], send.at[slot], recv.at[slot], (axis,)
            )
            copies[number, stage].start()

        for number, (lo, hi, order) in enumerate(self.parts):
            start(number, 0)
            spot = tuple(
                place[other] if other == order[0] else slice(None) for other in self.axes
            )
            load = pltpu.make_async_copy(
                operands[0].at[spot + (pl.ds(lo, hi - lo),)], buffers(number)[1], local.at[number]
            )
            load.start()
            loads.append(load)
        yield
        for stage in range(stages):
            for number, (lo, hi, order) in enumerate(self.parts):
                slots, held = buffers(number)
                if stage == 0:
                    loads[number].wait()
                copies[number, stage].wait_recv()
                rest = [other for other in self.axes if other != order[0]]
                gone = order[: stage + 1]
                free = [other for other in rest if other not in gone]
                for code in range(1 << len(free)):
                    bits = {axis: code >> bit & 1 for bit, axis in enumerate(free)}
                    spot = tuple(bits[axis] if axis in bits else place[axis] for axis in rest)
                    slot_spot = tuple(bits[axis] for axis in free)
                    last = stage == stages - 1

                    def add(step, carry, spot=spot, slot_spot=slot_spot, last=last):
                        rows = pl.ds(pl.multiple_of(step * ROW_TILE, ROW_TILE), ROW_TILE)
                        value = held[spot + (rows,)].astype(wide)
                        value = value + slots[stage][slot_spot + (rows,)].astype(wide)
                        if last:
                            at = pl.multiple_of(step * ROW_TILE + lo, ROW_TILE)
                            total[pl.ds(at, ROW_TILE)] = value
                        else:
                            held[spot + (rows,)] = value.astype(low)
                        return carry

                    lax.fori_loop(0, (hi - lo) // ROW_TILE, add, 0)
                if stage + 1 < stages:
                    start(number, stage + 1)
            yield
        if self.last is None:
            store = pltpu.make_async_copy(total, results[0], local.at[len(self.parts)])
            store.start()
            store.wait()
        else:
            ready, *others = scratch[len(self.parts) * (stages + 1) + 1 : -3]
            ready[...] = total[...].astype(low).reshape(ready.shape)
            yield from self.last.run([ready], results, others)
        for copy in copies.values():
            copy.wait_send()


class ReduceBoth(Reduce):
    def __init__(self, axes, operand, other, parts):
        super().__init__(axes, operand, parts, by_distance=True)
        self.operands = [operand, other]
        shape = operand.shape
        self.scratch = [pltpu.VMEM(shape, low), pltpu.VMEM(shape, low)]
        for lo, hi, order in parts:
            for stage in range(len(axes)):
                left = len(axes) - 1 - stage
                self.scratch.append(pltpu.VMEM((2,) * left + (hi - lo, shape[-1]), low))
        self.scratch.append(pltpu.VMEM(shape[-2:], wide))
        amount = len(parts) * len(axes)
        self.scratch += [sems(amount), sems(amount), sems(2 * len(parts) + 1)]

    def run(self, operands, results, scratch):
        stages = len(self.axes)
        held, added, *slots = scratch[:-4]
        total, send, recv, local = scratch[-4:]
        copies, loads = {}, []
        every = (slice(None),) * stages

        def start(number, stage):
            lo, hi, order = self.parts[number]
            spot = tuple(
                0 if axis in order[:stage] else 1 if axis == order[stage] else slice(None)
                for axis in self.axes
            )
            slot = number * stages + stage
            copies[number, stage] = remote(
                held.at[spot + (pl.ds(lo, hi - lo),)],
                slots[slot],
                send.at[slot],
                recv.at[slot],
                (order[stage],),
            )
            copies[number, stage].start()

        def add_all(lo, hi, free, spot_of, source, last):
            for code in range(1 << len(free)):
                bits = {axis: code >> bit & 1 for bit, axis in enumerate(free)}
                spot = tuple(bits.get(axis, 0) for axis in self.axes)
                source_spot = spot_of(bits)

                def add(step, carry, spot=spot, source_spot=source_spot):
                    at = pl.multiple_of(step * ROW_TILE, ROW_TILE)
                    rows = pl.ds(pl.multiple_of(at + lo, ROW_TILE), ROW_TILE)
                    value = held[spot + (rows,)].astype(wide)
                    shift = rows if source is added else pl.ds(at, ROW_TILE)
                    value = value + source[source_spot + (shift,)].astype(wide)
                    if last:
                        total[rows] = value
                    else:
                        held[spot + (rows,)] = value.astype(low)
                    return carry

                lax.fori_loop(0, (hi - lo) // ROW_TILE, add, 0)

        for number, (lo, hi, order) in enumerate(self.parts):
            span = every + (pl.ds(lo, hi - lo),)
            for which, (operand, buffer) in enumerate(zip(operands, (held, added))):
                load = pltpu.make_async_copy(
                    operand.at[span], buffer.at[span], local.at[2 * number + which]
                )
                load.start()
                loads.append(load)
        for number, (lo, hi, order) in enumerate(self.parts):
            loads[2 * number].wait()
            loads[2 * number + 1].wait()
            add_all(
                lo, hi, self.axes, lambda bits: tuple(bits[axis] for axis in self.axes), added, False
            )
            start(number, 0)
        yield
        for stage in range(stages):
            for number, (lo, hi, order) in enumerate(self.parts):
                copies[number, stage].wait_recv()
                free = [axis for axis in self.axes if axis not in order[: stage + 1]]
                add_all(
                    lo,
                    hi,
                    free,
                    lambda bits, free=free: tuple(bits[axis] for axis in free),
                    slots[number * stages + stage],
                    stage == stages - 1,
                )
                if stage + 1 < stages:
                    start(number, stage + 1)
            yield
        store = pltpu.make_async_copy(total, results[0], local.at[2 * len(self.parts)])
        store.start()
        store.wait()
        for copy in copies.values():
            copy.wait_send()


class Task:
    flips = ()


class WeightGrad(Task):
    def __init__(self, lefts, rights, left_half, right_half, rows, tile=256):
        self.amount, self.rows, self.tile = len(lefts), rows, tile
        self.halves = left_half, right_half
        self.operands = list(lefts) + list(rights)
        self.columns, self.width = lefts[0].shape[-1], rights[0].shape[-1]
        self.blocks = lefts[0].shape[0]
        self.results = [jax.ShapeDtypeStruct((self.columns, self.width), low)]
        shape = (self.amount, self.blocks, rows, self.width)
        self.scratch = [pltpu.VMEM(shape, low), sems(self.amount)]

    def run(self, operands, results, scratch, lo=0, hi=None):
        held, done = scratch
        at = pl.ds(self.halves[1] * self.rows, self.rows)
        copies = [
            pltpu.make_async_copy(right.at[:, at], held.at[number], done.at[number])
            for number, right in enumerate(operands[self.amount :])
        ]
        for copy in copies:
            copy.start()
        for copy in copies:
            copy.wait()

        def body(*refs):
            total = 0.0
            for number, left_ref in enumerate(refs[:-1]):
                right = held[number].reshape(-1, self.width)
                total = total + dot_tn(left_ref[...].reshape(-1, self.tile), right)
            refs[-1][...] = total.astype(low)

        block = pl.BlockSpec(
            (self.blocks, self.rows, self.tile), lambda step: (0, self.halves[0], step)
        )
        pltpu.emit_pipeline(
            body,
            grid=(self.columns // self.tile,),
            in_specs=[block] * self.amount,
            out_specs=[pl.BlockSpec((self.tile, self.width), lambda step: (step, 0))],
        )(*operands[: self.amount], results[0])


def flow_kernel(flows, plan, *refs):
    refs = list(refs)

    def cut(amount):
        part = refs[:amount]
        del refs[:amount]
        return part

    operands = [cut(len(flow.operands)) for flow in flows]
    results = [cut(len(flow.results)) for flow in flows]
    scratch = [cut(len(flow.scratch)) for flow in flows]
    partners = []
    for flow in flows:
        partners += [flips for flips in flow.flips if flips not in partners]
    barrier = pltpu.get_barrier_semaphore()
    for flips in partners:
        pl.semaphore_signal(
            barrier, inc=1, device_id=toward(flips), device_id_type=pl.DeviceIdType.MESH
        )
    pl.semaphore_wait(barrier, len(partners))
    tasks = [part for part in zip(flows, operands, results, scratch) if isinstance(part[0], Task)]
    runs = [
        flow.run(*parts)
        for flow, *parts in zip(flows, operands, results, scratch)
        if not isinstance(flow, Task)
    ]
    for run in runs:
        next(run)
    for number in plan:
        if number < 0:
            flow, *parts = tasks[-1 - number]
            flow.run(*parts)
        elif number < len(runs):
            next(runs[number], None)
    while runs:
        runs = [run for run in runs if next(run, run) is not run]


def transfer(number, flows, plan=()):
    arrays = [array for flow in flows for array in flow.operands]
    shapes = [shape for flow in flows for shape in flow.results]
    anywhere = pl.BlockSpec(memory_space=pl.ANY)
    return pl.pallas_call(
        functools.partial(flow_kernel, flows, plan),
        out_shape=shapes,
        in_specs=[anywhere] * len(arrays),
        out_specs=[anywhere] * len(shapes),
        scratch_shapes=[one for flow in flows for one in flow.scratch],
        compiler_params=pltpu.CompilerParams(
            collective_id=number, has_side_effects=True, vmem_limit_bytes=60 * MIB
        ),
        cost_estimate=BRIEF,
    )(*arrays)


def tile_of(rows, most):
    steps = -(-rows // most)
    while rows % steps or (rows // steps) % ROW_TILE:
        steps += 1
    return rows // steps


def whole_block(shape):
    return pl.BlockSpec(shape, lambda *ids: (0,) * len(shape), pipeline_mode=pl.Buffered(1))


def expert_kernel(
    near,
    ids_ref,
    rows_ref,
    grad_ref,
    gate_ref,
    pieces_in,
    pieces_down,
    hidden_ref,
    d_in_ref,
    d_gate_ref,
    made_ref,
    back_ref,
    in_ref,
    down_ref,
    done,
):
    @pl.when(pl.program_id(0) == 0)
    def _():
        copies = []
        for pieces, held in ((pieces_in, in_ref), (pieces_down, down_ref)):
            amount, parts, rows = pieces.shape[:3]
            for spot in range(amount):
                for part in range(parts):
                    block = (part // near * amount + spot) * near + part % near
                    copy = pltpu.make_async_copy(
                        pieces.at[spot, part],
                        held.at[pl.ds(block * rows, rows)],
                        done.at[len(copies)],
                    )
                    copy.start()
                    copies.append(copy)
        for copy in copies:
            copy.wait()

    hidden_width = down_ref.shape[0]
    gate = gate_ref[...]
    acts = dot(rows_ref[...], in_ref[...])
    d_plain = dot_nt(grad_ref[...], down_ref[...])
    act_gate, act_up = acts[:, :hidden_width], acts[:, hidden_width:]
    sigmoid = 1.0 / (1.0 + jnp.exp(-act_gate))
    silu_gate = act_gate * sigmoid
    hidden = silu_gate * act_up
    d_gate_ref[...] = jnp.sum(hidden * d_plain, axis=1, keepdims=True)
    d_hidden = d_plain * gate
    hidden_low = (hidden * gate).astype(low)
    d_act_gate = d_hidden * act_up * (sigmoid * (1.0 + act_gate * (1.0 - sigmoid)))
    d_in = jnp.concatenate([d_act_gate.astype(low), (d_hidden * silu_gate).astype(low)], axis=1)
    hidden_ref[...] = hidden_low
    d_in_ref[...] = d_in
    back_ref[...] = dot_nt(d_in, in_ref[...]).astype(low)
    made_ref[...] = dot(hidden_low, down_ref[...]).astype(low)


def expert_rows(rows, gate, pieces_in, pieces_down, near, ids):
    blocks, tile, model_width = rows.shape
    tile = tile // 2
    pieces = (pieces_in, pieces_down)
    amount = blocks * tile
    hidden_width = pieces_in.shape[3] // 2

    def half(which):
        return pl.BlockSpec((None, tile, model_width), lambda step, ids: (ids[step], which, 0))

    def by_place(columns):
        return pl.BlockSpec((tile, columns), lambda step, ids: (ids[step], 0))

    def by_distance(columns):
        return pl.BlockSpec((tile, columns), lambda step, ids: (step, 0))

    outs = [
        (by_place, hidden_width, low),
        (by_place, 2 * hidden_width, low),
        (by_distance, 1, wide),
        (by_distance, model_width, low),
        (by_distance, model_width, low),
    ]
    anywhere = pl.BlockSpec(memory_space=pl.ANY)
    return pl.pallas_call(
        functools.partial(expert_kernel, near),
        grid_spec=pltpu.PrefetchScalarGridSpec(
            num_scalar_prefetch=1,
            grid=(blocks,),
            in_specs=[half(0), half(1), by_place(1)]
            + [anywhere] * len(pieces),
            out_specs=[spec(columns) for spec, columns, _ in outs],
            scratch_shapes=[
                pltpu.VMEM((model_width, 2 * hidden_width), low),
                pltpu.VMEM((hidden_width, model_width), low),
                sems(sum(piece.shape[0] * piece.shape[1] for piece in pieces)),
            ],
        ),
        out_shape=[jax.ShapeDtypeStruct((amount, columns), kind) for _, columns, kind in outs],
        compiler_params=pltpu.CompilerParams(vmem_limit_bytes=52 * MIB),
        cost_estimate=pl.CostEstimate(
            flops=LONG * 18 * amount * model_width * hidden_width,
            bytes_accessed=14 * amount * model_width,
            transcendentals=0,
        ),
    )(ids, rows, rows, gate, *pieces)


def weight_kernel(amount, *refs):
    total = 0.0
    for left, right in zip(refs[:amount], refs[amount:-1]):
        total = total + dot_tn(left[...], right[...])
    refs[-1][...] = total.astype(low)


def weight_grad(lefts, rights, tile=256):
    amount = len(lefts)
    columns, out_columns = lefts[0].shape[1], rights[0].shape[1]
    return pl.pallas_call(
        functools.partial(weight_kernel, amount),
        grid=(columns // tile,),
        in_specs=[pl.BlockSpec((left.shape[0], tile), lambda step: (0, step)) for left in lefts]
        + [whole_block(right.shape) for right in rights],
        out_specs=pl.BlockSpec((tile, out_columns), lambda step: (step, 0)),
        out_shape=jax.ShapeDtypeStruct((columns, out_columns), low),
        compiler_params=pltpu.CompilerParams(vmem_limit_bytes=52 * MIB),
        cost_estimate=BRIEF,
    )(*lefts, *rights)


def widen_kernel(pieces_ref, *out_refs):
    columns = out_refs[0].shape[1]
    for number, out_ref in enumerate(out_refs):
        span = slice(number * columns, (number + 1) * columns)
        out_ref[...] = pieces_ref[:, span].astype(wide)


def by_expert(pieces, amount):
    team, rows, columns = pieces.shape[0], pieces.shape[-2], pieces.shape[-1]
    pieces = pieces.reshape(team, -1, rows, columns)
    groups = pieces.shape[1]
    out = (groups * team, rows, columns // amount)
    return pl.pallas_call(
        widen_kernel,
        grid=(groups, team),
        in_specs=[pl.BlockSpec((None, None, rows, columns), lambda group, place: (place, group, 0, 0))],
        out_specs=[
            pl.BlockSpec((None,) + out[1:], lambda group, place: (group * team + place, 0, 0))
        ]
        * amount,
        out_shape=[jax.ShapeDtypeStruct(out, wide)] * amount,
        cost_estimate=BRIEF,
    )(pieces)


def turned(values, cosine, sine):
    return values * cosine + pltpu.roll(values, values.shape[1] // 2, 1) * sine


def turned_back(grads, cosine, sine):
    return grads * cosine + pltpu.roll(grads * sine, grads.shape[1] // 2, 1)


def head_scale(values):
    return lax.rsqrt(jnp.mean(values * values, axis=1, keepdims=True) + epsilon)


def prep_kernel(
    heads,
    rows_ref,
    w_ref,
    place_ref,
    inverse_ref,
    sign_ref,
    gain_q,
    gain_k,
    lin_ref,
    query_ref,
    keyed_ref,
    value_ref,
    cosine_ref,
    sine_ref,
):
    width = gain_q.shape[1]
    angle = place_ref[...].astype(wide) * inverse_ref[...]
    cosine, sine = jnp.cos(angle), jnp.sin(angle) * sign_ref[...]
    cosine_ref[...] = cosine
    sine_ref[...] = sine
    lin = dot(rows_ref[...], w_ref[...])
    lin_ref[...] = lin[:, : (heads + 1) * width]
    for head in range(heads + 1):
        span = slice(head * width, (head + 1) * width)
        values = lin[:, span]
        gain = gain_q[...] if head < heads else gain_k[...]
        made = turned(values * head_scale(values) * gain, cosine, sine).astype(low)
        if head < heads:
            query_ref[:, span] = made
        else:
            keyed_ref[...] = made
    value_ref[...] = lin[:, (heads + 1) * width :].astype(low)


def unprep_kernel(
    heads,
    scale,
    d_query_ref,
    d_keyed_ref,
    d_value_ref,
    lin_ref,
    w_ref,
    cosine_ref,
    sine_ref,
    gain_q,
    gain_k,
    rows_ref,
    gain_ref,
    d_lin_ref,
    d_one_ref,
    d_gain_q,
    d_gain_k,
    d_gain,
):
    width = gain_q.shape[1]
    cosine, sine = cosine_ref[...], sine_ref[...]

    @pl.when(pl.program_id(0) == 0)
    def _():
        d_gain_q[...] = jnp.zeros_like(d_gain_q)
        d_gain_k[...] = jnp.zeros_like(d_gain_k)
        d_gain[...] = jnp.zeros_like(d_gain)

    for head in range(heads + 1):
        span = slice(head * width, (head + 1) * width)
        values = lin_ref[:, span]
        if head < heads:
            grads, gain, d_head = d_query_ref[:, span].astype(wide), gain_q[...], d_gain_q
        else:
            grads, gain, d_head = d_keyed_ref[...] * scale, gain_k[...], d_gain_k
        grads = turned_back(grads, cosine, sine)
        factor = head_scale(values)
        plain = values * factor
        d_head[...] += jnp.sum(grads * plain, axis=0, keepdims=True)
        grads = grads * gain
        mean = jnp.mean(grads * plain, axis=1, keepdims=True)
        d_lin_ref[:, span] = (factor * (grads - plain * mean)).astype(low)
    d_lin_ref[:, (heads + 1) * width :] = d_value_ref[...].astype(low)
    d_one = dot_nt(d_lin_ref[...], w_ref[...])
    d_one_ref[...] = d_one.astype(low)
    d_gain[...] += jnp.sum(d_one * rows_ref[...].astype(wide), axis=0, keepdims=True) / gain_ref[...]


def row_call(kernel, rows, tiled, fixed, outs, sums):
    tile = tile_of(rows, 256)

    def by_rows(columns):
        return pl.BlockSpec((tile, columns), lambda step: (step, 0))

    return pl.pallas_call(
        kernel,
        grid=(rows // tile,),
        in_specs=[
            whole_block(array.shape) if number in fixed else by_rows(array.shape[1])
            for number, array in enumerate(tiled)
        ],
        out_specs=[by_rows(columns) for columns, _ in outs]
        + [pl.BlockSpec((1, columns), lambda step: (0, 0)) for columns in sums],
        out_shape=[jax.ShapeDtypeStruct((rows, columns), kind) for columns, kind in outs]
        + [jax.ShapeDtypeStruct((1, columns), wide) for columns in sums],
        compiler_params=pltpu.CompilerParams(vmem_limit_bytes=48 * MIB),
        cost_estimate=BRIEF,
    )(*tiled)


def mask_tile(bias, k_place, k_segment, q_place, q_segment):
    allowed = (k_segment[...] == q_segment[0]) & (k_place[...] <= q_place[0])
    bias[...] = jnp.where(allowed, 0.0, -1e30)


def ahead_kernel(
    scale, k_place, k_segment, q_place, q_segment, q_ref, k_ref, vt_ref, mixed_ref, total_ref, bias
):
    @pl.when(pl.program_id(2) == 0)
    def _():
        mask_tile(bias, k_place.at[0], k_segment.at[0], q_place, q_segment)

    scores = dot_nt(k_ref[0], q_ref[0]) * scale + bias[...]
    row_max = jnp.max(scores, axis=0, keepdims=True)
    expd = jnp.exp(scores - row_max)
    row_total = jnp.sum(expd, axis=0, keepdims=True)
    mixed = dot(vt_ref[0], expd.astype(low)) / row_total
    mixed_ref[0] = mixed.T.astype(low)
    total_ref[0, 0] = row_max + jnp.log(row_total)


def behind_kernel(
    scale,
    k_place,
    k_segment,
    q_place,
    q_segment,
    q_ref,
    d_mixed_ref,
    k_ref,
    v_ref,
    kt_ref,
    total_ref,
    d_q_ref,
    d_k_ref,
    d_v_ref,
    bias,
):
    @pl.when(pl.program_id(2) == 0)
    def _():
        mask_tile(bias, k_place.at[0], k_segment.at[0], q_place, q_segment)

    @pl.when((pl.program_id(1) == 0) & (pl.program_id(2) == 0))
    def _():
        d_k_ref[...] = jnp.zeros_like(d_k_ref)
        d_v_ref[...] = jnp.zeros_like(d_v_ref)

    query, d_mixed = q_ref[0], d_mixed_ref[0]
    probs = jnp.exp(dot_nt(k_ref[0], query) * scale + bias[...] - total_ref[0, 0])
    d_probs = dot_nt(v_ref[0], d_mixed)
    row_dot = jnp.sum(probs * d_probs, axis=0, keepdims=True)
    d_scores = (probs * (d_probs - row_dot)).astype(low)
    d_v_ref[0] += dot(probs.astype(low), d_mixed)
    d_k_ref[0] += dot(d_scores, query)
    d_q_ref[0] = (dot(kt_ref[0], d_scores) * scale).T.astype(low)


def attention_call(kernel, marks, arrays, kinds, outs, width, scale, work):
    place, segment = marks
    seqs, length = place.shape
    tile = min(256, length)
    heads = arrays[0].shape[2] // width
    specs = {
        "query": pl.BlockSpec((1, tile, width), lambda s, i, h: (s, i, h)),
        "keys": pl.BlockSpec((1, length, width), lambda s, i, h: (s, 0, 0)),
        "flat": pl.BlockSpec((1, width, length), lambda s, i, h: (s, 0, 0)),
        "total": pl.BlockSpec((1, 1, 1, tile), lambda s, i, h: (s, h, 0, i)),
    }
    column = pl.BlockSpec((1, length, 1), lambda s, i, h: (s, 0, 0))
    row = pl.BlockSpec((1, 1, tile), lambda s, i, h: (s, 0, i))
    return pl.pallas_call(
        functools.partial(kernel, scale),
        grid=(seqs, length // tile, heads),
        in_specs=[column, column, row, row] + [specs[kind] for kind in kinds],
        out_specs=[specs[kind] for kind, _ in outs],
        out_shape=[shape for _, shape in outs],
        scratch_shapes=[pltpu.VMEM((length, tile), wide)],
        compiler_params=pltpu.CompilerParams(vmem_limit_bytes=48 * MIB),
        cost_estimate=BRIEF,
    )(place[:, :, None], segment[:, :, None], place[:, None, :], segment[:, None, :], *arrays)


def per_device(
    g_axes,
    c_axes,
    f_axes,
    tokens,
    places,
    segments,
    routes,
    w_query,
    w_key,
    w_value,
    w_out,
    w_router,
    w_gate,
    w_up,
    w_down,
    gain_attn,
    gain_ffn,
    gain_query,
    gain_key,
    cotangent,
):
    groups, parts_c, parts_f = 1 << len(g_axes), 1 << len(c_axes), 1 << len(f_axes)
    count = tokens.shape[1]
    width = gain_query.shape[0]
    model_width = tokens.shape[2]
    kv_heads = w_key.shape[1] // width // parts_c
    assert kv_heads == 1
    heads = w_query.shape[1] // width // parts_c // groups
    experts = w_gate.shape[0]
    hidden_width = w_gate.shape[2]
    scale = 1.0 / math.sqrt(width)
    rows_d = w_query.shape[0]
    rows_o = w_out.shape[0]
    rows_f = w_down.shape[1]
    pair_count = experts.bit_length() - 1 - len(g_axes) - len(c_axes)
    assert 0 <= pair_count <= len(f_axes)
    far_axes = f_axes[: len(f_axes) - pair_count]
    near_axes = f_axes[len(f_axes) - pair_count :]
    parts_near = 1 << len(near_axes)
    team_axes = c_axes + near_axes
    team = parts_c * parts_near
    own_axes = c_axes + f_axes
    plane_axes = g_axes + c_axes
    cluster_axes = g_axes + team_axes
    all_axes = g_axes + c_axes + f_axes
    all_axes_but_core = c_axes[:-1] + f_axes[::-1] + g_axes
    g_here = flat_index(g_axes)
    core = c_axes[-1:]
    plane_shape = (2,) * len(plane_axes) + (count, model_width)
    cluster_shape = (2,) * len(cluster_axes) + (count, model_width)
    turn = g_axes + c_axes[:-1]
    half = count // 2
    plane_parts = [(0, half, turn), (half, count, turn[1:] + turn[:1])]
    turn = turn + near_axes
    third = (count // 3) // ROW_TILE * ROW_TILE
    cuts = [0, count - 2 * third, count - third, count]
    cluster_parts = [
        (cuts[step], cuts[step + 1], turn[step:] + turn[:step]) for step in range(len(cuts) - 1)
    ]
    def core_last(parts):
        return [(lo, hi, order + core) for lo, hi, order in parts]

    def core_first(parts):
        return [(lo, hi, core + order) for lo, hi, order in parts]

    q_cols = heads * width
    qkv_cols = q_cols + 2 * width
    even = rows_o % (groups * width) == 0
    if even:
        own_query = w_query.reshape(rows_d, parts_c, parts_f, groups, q_cols // parts_f)
        own_query = own_query.transpose(3, 1, 0, 2, 4)
    else:
        own_query = w_query.reshape(rows_d, parts_c, groups, q_cols).transpose(2, 1, 0, 3)
    own_query = take(own_query.reshape(groups, parts_c, rows_d, q_cols), g_here)
    mine_qkv = jnp.concatenate(
        [
            own_query,
            w_key.reshape(rows_d, parts_c, width).transpose(1, 0, 2),
            w_value.reshape(rows_d, parts_c, width).transpose(1, 0, 2),
        ],
        axis=2,
    )
    own_in = jnp.concatenate([w_gate, w_up], axis=2)
    wide_router = jnp.pad(w_router, ((0, 0), (0, width - experts)))
    resid = tokens[0].astype(jnp.float32)
    norm_one, back_one = jax.vjp(normed, resid, gain_attn)

    def own_expert(place):
        return flat_index(g_axes) * team + place

    mine_out = take(w_out.reshape(groups, -1, model_width), g_here) if even else w_out
    all_one, w_qkv, pieces_down, w_mix, got_in, full_router, marks = transfer(
        1,
        [
            Gather(plane_axes, norm_one.astype(low), core_last(plane_parts)),
            Spread(c_axes, f_axes, mine_qkv, (rows_d, qkv_cols)),
            Spread(team_axes, far_axes, w_down, w_down.shape[1:], own_expert),
            Gather(f_axes, mine_out, [(0, mine_out.shape[0], f_axes)]),
            Direct(team_axes, own_in, own_in.shape[1:], own_expert),
            Direct(own_axes, wide_router[None], wide_router.shape, lambda place: 0),
            Direct(
                g_axes,
                jnp.stack([places[0], segments[0]])[None],
                (2,) + places.shape[1:],
                lambda place: 0,
            ),
        ],
        (1, 0, 2, 0, 3, 1),
    )
    w_qkv = w_qkv.reshape(model_width, qkv_cols)
    all_one = all_one.reshape(-1, model_width)
    full_router = full_router.reshape(model_width, width)[:, :experts]

    w_mix = w_mix.reshape(-1, model_width)
    if not even:
        w_mix = take(w_mix.reshape(groups, q_cols, model_width), g_here)

    def from_far(got):
        return lax.all_gather(got, far_axes, axis=0, tiled=False) if far_axes else got[None]

    pieces_in = from_far(got_in)
    pieces_down = pieces_down.reshape((team, -1) + w_down.shape[1:]).transpose(1, 0, 2, 3)
    if rows_f % ROW_TILE:
        pieces_down = pieces_down.reshape((-1, parts_c, parts_near) + w_down.shape[1:])
        pieces_down = pieces_down.transpose(1, 0, 2, 3, 4).reshape(1, 1, hidden_width, model_width)

    place, segment = marks[:, 0], marks[:, 1]
    length = place.shape[1]
    rows = groups * length
    steps = jnp.arange(width // 2).astype(wide)
    inverse = jnp.exp(steps * (-2.0 * math.log(1000000.0) / width))
    inverse = jnp.concatenate([inverse, inverse])[None]
    sign = jnp.where(jnp.arange(width) < width // 2, -1.0, 1.0)[None]
    head_gains = (gain_query[None], gain_key[None])
    lin, query_low, keyed_low, value_low, cosine, sine = row_call(
        functools.partial(prep_kernel, heads),
        rows,
        (all_one, w_qkv, place.reshape(rows, 1), inverse, sign) + head_gains,
        (1, 3, 4, 5, 6),
        [(q_cols + width, wide), (q_cols, low), (width, low), (width, low), (width, wide), (width, wide)],
        [],
    )
    query_low = query_low.reshape(groups, length, q_cols)
    keyed_low = keyed_low.reshape(groups, length, width)
    value_low = value_low.reshape(groups, length, width)
    total_shape = jax.ShapeDtypeStruct((groups, heads, 1, length), wide)
    mixed_low, log_total = attention_call(
        ahead_kernel,
        (place, segment),
        (query_low, keyed_low, value_low.transpose(0, 2, 1)),
        ("query", "keys", "flat"),
        [("query", jax.ShapeDtypeStruct(query_low.shape, low)), ("total", total_shape)],
        width,
        scale,
        4,
    )
    mixed_rows = mixed_low.reshape(groups * length, q_cols)
    branch = dot(mixed_rows, w_mix).astype(low).reshape(plane_shape)
    (branch,) = transfer(2, [Reduce(plane_axes, branch, core_first(plane_parts))])
    resid_one = resid + branch

    norm_two, back_two = jax.vjp(normed, resid_one, gain_ffn)
    normed_two = norm_two.astype(low)
    logits = dot(normed_two, full_router)
    labels = jnp.arange(experts, dtype=jnp.int32)
    chosen = jnp.any(routes[0][:, :, None] == labels[None, None, :], axis=1)
    logits = jnp.where(chosen, logits, -1e30)
    powers = jnp.where(chosen, jnp.exp(logits - jnp.max(logits, axis=-1, keepdims=True)), 0.0)
    gates = powers / jnp.sum(powers, axis=-1, keepdims=True)

    grad_parts = [(lo + count, hi + count, order) for lo, hi, order in cluster_parts]
    own_rows, all_gates = transfer(
        3,
        [
            Gather(
                turn,
                jnp.concatenate([normed_two, cotangent[0]], axis=0),
                cluster_parts + grad_parts,
            ),
            Gather(cluster_axes, gates.T, [(0, experts, turn + core)]),
        ],
    )
    blocks = 1 << len(turn)
    own_rows = own_rows.reshape(blocks, 2 * count, model_width)
    far_rows = lax.ppermute(own_rows, core[0], SWAP)
    gate_stack = take_at(all_gates, flat_index(cluster_axes), len(cluster_axes))
    core_here, core_spot = lax.axis_index(core[0]), cluster_axes.index(core[0])
    ids = jnp.bitwise_xor(jnp.arange(blocks), flat_index(turn)).astype(jnp.int32)
    sides = []
    for side, side_rows in ((core_here, own_rows), (1 - core_here, far_rows)):
        gate = take_at(gate_stack, side, core_spot).reshape(-1, 1)
        sides.append(expert_rows(side_rows, gate, pieces_in, pieces_down, parts_near, ids))
        ids = ids + zero_of(sides[0][2]).astype(jnp.int32)
    hiddens, d_ins, d_gate_parts, made_parts, back_parts = zip(*sides)
    half_shape = (2,) * len(turn) + (count, model_width)
    far_back = lax.ppermute(back_parts[1], core[0], SWAP)
    far_made = lax.ppermute(made_parts[1], core[0], SWAP)
    d_gates = jnp.stack(d_gate_parts).reshape(experts, 1, count)
    both_rows = [own_rows, far_rows]
    hiddens = [part.reshape(blocks, count, hidden_width) for part in hiddens]
    d_ins = [part.reshape(blocks, count, 2 * hidden_width) for part in d_ins]
    back = [part.reshape(half_shape) for part in (back_parts[0], far_back)]
    d_rows_two, d_gates, part_down, part_in = transfer(
        4,
        [
            ReduceBoth(turn, *back, cluster_parts),
            Direct(core + turn, d_gates, (1, count)),
            WeightGrad(hiddens, both_rows, 0, 1, count),
            WeightGrad(both_rows, d_ins, 0, 0, count),
        ],
        (-1, 0, -2),
    )
    d_gates = d_gates.reshape((2,) * len(cluster_axes) + (count,))
    spots = [(core + turn).index(axis) for axis in cluster_axes]
    d_gates = d_gates.transpose(spots + [len(spots)]).reshape(experts, count).T

    reduced = zero_of(d_rows_two).astype(low)

    def to_far(part, rows):
        stack = part.reshape(parts_c, -1, parts_near, rows, part.shape[1]) + reduced
        stack = stack.transpose(1, 0, 2, 3, 4).reshape(-1, team, rows, part.shape[1])
        if not far_axes:
            return stack[0]
        return lax.psum_scatter(stack, far_axes, scatter_dimension=0, tiled=False)

    share_down, share_in = to_far(part_down, rows_f), to_far(part_in, rows_d)

    d_logits = (gates * (d_gates - jnp.sum(gates * d_gates, axis=-1, keepdims=True))).astype(low)
    part_router = dot_tn(normed_two, d_logits)
    d_normed_two = d_rows_two + dot_nt(d_logits, full_router)
    d_resid_one, d_gain_ffn = back_two(d_normed_two)
    d_resid_one = d_resid_one + cotangent[0].astype(jnp.float32)
    wide_part = jnp.pad(part_router.astype(low), ((0, 0), (0, width - experts)))

    made_axes = turn[: len(turn) - len(near_axes)]
    made_shape = (2,) * len(made_axes) + (parts_near * count, model_width)
    made = (made_parts[0].reshape(made_shape), far_made.reshape(made_shape))
    made_spans = [(lo * parts_near, hi * parts_near, order) for lo, hi, order in plane_parts]
    d_branch, made = transfer(
        5,
        [
            Gather(plane_axes, d_resid_one.astype(low), core_last(plane_parts)),
            ReduceBoth(made_axes, *made, made_spans),
        ],
    )
    d_branch = d_branch.reshape(-1, model_width)
    d_mixed = dot_nt(d_branch, w_mix).astype(low).reshape(query_low.shape)
    shapes = [
        jax.ShapeDtypeStruct(query_low.shape, low),
        jax.ShapeDtypeStruct(keyed_low.shape, wide),
        jax.ShapeDtypeStruct(keyed_low.shape, wide),
    ]
    d_query, d_keyed, d_value = attention_call(
        behind_kernel,
        (place, segment),
        (query_low, d_mixed, keyed_low, value_low, keyed_low.transpose(0, 2, 1), log_total),
        ("query", "query", "keys", "keys", "flat", "total"),
        list(zip(("query", "keys", "keys"), shapes)),
        width,
        scale,
        10,
    )
    d_lin, d_one, d_gain_query, d_gain_key, d_gain_attn = row_call(
        functools.partial(unprep_kernel, heads, scale),
        rows,
        (
            d_query.reshape(rows, q_cols),
            d_keyed.reshape(rows, width),
            d_value.reshape(rows, width),
            lin,
            w_qkv,
            cosine,
            sine,
        )
        + head_gains
        + (all_one, gain_attn[None]),
        (4, 7, 8, 10),
        [(qkv_cols, low), (model_width, low)],
        [width, width, model_width],
    )
    d_one = d_one.reshape(plane_shape)
    part_out = weight_grad([mixed_rows], [d_branch])
    part_qkv = weight_grad([all_one], [d_lin])

    def by_f(part):
        stack = part.reshape(parts_c, parts_f, rows_d, -1).transpose(1, 0, 2, 3)
        return stack.reshape((2,) * len(f_axes) + (parts_c * rows_d, -1))

    turn_back = plane_axes[len(g_axes) : -1] + g_axes
    def over_groups(shape):
        return Gather(g_axes, shape, [(0, shape.shape[0], g_axes)])

    def to_column_owners(shape):
        return Spread(c_axes, g_axes, shape, shape.shape[1:])

    flows = [
        Spread(team_axes, g_axes, share_down, share_down.shape[1:]),
        Spread(team_axes, g_axes, share_in, share_in.shape[1:]),
        Reduce(plane_axes, d_one, core_first([(lo, hi, turn_back) for lo, hi, _ in plane_parts])),
        Reduce(
            f_axes,
            by_f(part_qkv),
            [(0, parts_c * rows_d, f_axes[::-1])],
            jax.ShapeDtypeStruct((parts_c, rows_d, qkv_cols), low),
            to_column_owners,
        ),
        Reduce(
            own_axes,
            wide_part.reshape((2,) * len(own_axes) + (rows_d, width)),
            [(0, rows_d, own_axes)],
            jax.ShapeDtypeStruct((rows_d, width), low),
            over_groups,
        ),
    ]
    if even:
        rows = q_cols // parts_f
        stack = part_out.reshape((2,) * len(f_axes) + (rows, model_width))
        shape = jax.ShapeDtypeStruct((rows, model_width), low)
        flows.append(Reduce(f_axes, stack, [(0, rows, f_axes[::-1])], shape, over_groups))
    if near_axes:
        near_shape = (2,) * len(near_axes) + (count, model_width)
        near_flow = Reduce(
            near_axes, made.astype(low).reshape(near_shape), [(0, count, near_axes)], by_distance=True
        )
        flows.append(near_flow)
    gains = jnp.concatenate([d_gain_attn[0], d_gain_ffn, d_gain_query[0], d_gain_key[0]])
    lines = -(-gains.size // (8 * width)) * 8
    gains = jnp.pad(gains, (0, lines * width - gains.size)).reshape(lines, width)
    flows.insert(5, Gather(all_axes, gains, [(0, lines, core + all_axes_but_core)]))
    all_down, all_in, d_one, all_qkv, share_router, gains, *rest = transfer(
        7, flows, (2, 0, 1, 2, 3, 7, 6, 4, 5, 3, 3, 6, 6, 4, 5, 3, 4, 5)
    )
    gains = jnp.sum(gains.reshape(-1, lines * width), axis=0)
    share_router = share_router.reshape(groups, rows_d, width)[:, :, :experts]
    grad_router = jnp.sum(share_router.astype(wide), axis=0)
    if near_axes:
        made = rest.pop()
    output = (resid_one + made).astype(low)[None]
    d_resid = back_one(d_one)[0]
    grad_tokens = (d_resid + d_resid_one)[None]
    grad_down, = by_expert(all_down, 1)
    grad_gate, grad_up = by_expert(all_in, 2)
    if even:
        grad_out = rest[0].astype(wide).reshape(rows_o, model_width)
    else:
        stack = jnp.where(jnp.arange(groups)[:, None, None] == g_here, part_out[None], 0)
        share_out = lax.psum_scatter(
            stack.reshape(groups * q_cols, model_width), f_axes, scatter_dimension=0, tiled=True
        )
        grad_out = lax.psum(share_out.astype(wide), g_axes)
    all_qkv = all_qkv.reshape(parts_c, groups, rows_d, qkv_cols).transpose(1, 0, 2, 3).astype(wide)
    grad_query = all_qkv[:, :, :, :q_cols]
    if even:
        grad_query = grad_query.reshape(groups, parts_c, rows_d, parts_f, q_cols // parts_f)
        grad_query = grad_query.transpose(2, 1, 3, 0, 4).reshape(rows_d, -1)
    else:
        grad_query = grad_query.transpose(2, 1, 0, 3).reshape(rows_d, -1)
    grad_kv = jnp.sum(all_qkv[:, :, :, q_cols:], axis=0).transpose(1, 0, 2)
    grad_key = grad_kv[:, :, :width].reshape(rows_d, -1)
    grad_value = grad_kv[:, :, width:].reshape(rows_d, -1)

    return (
        output,
        grad_tokens,
        grad_query,
        grad_key,
        grad_value,
        grad_out,
        grad_router,
        grad_gate,
        grad_up,
        grad_down,
        gains[:model_width],
        gains[model_width : 2 * model_width],
        gains[2 * model_width : 2 * model_width + width],
        gains[2 * model_width + width : 2 * model_width + 2 * width],
    )


def solution(mesh):
    def binary(letter, size):
        return tuple(letter + str(step) for step in range(size.bit_length() - 1))

    g_axes = binary("g", mesh.shape["grp"])
    c_axes = binary("c", mesh.shape["ctx"])
    f_axes = binary("f", mesh.shape["fsdp"])
    names = g_axes + c_axes + f_axes
    fine = Mesh(mesh.devices.reshape((2,) * len(names)), names)
    rows = P(g_axes + f_axes, c_axes, None)
    line = P(g_axes + f_axes, None)
    split = P(c_axes + f_axes, None)
    expert = P(None, c_axes + f_axes, None)
    whole = P()
    in_specs = (
        (rows, line, line, rows)
        + (split,) * 5
        + (expert,) * 3
        + (whole,) * 4
        + (rows,)
    )
    out_specs = (rows, rows) + (split,) * 5 + (expert,) * 3 + (whole,) * 4

    def device_part(*arrays):
        return per_device(g_axes, c_axes, f_axes, *arrays)

    return jax.shard_map(
        device_part, mesh=fine, in_specs=in_specs, out_specs=out_specs, check_vma=False
    )
```

```python
import functools
import math

import jax
import jax.numpy as jnp
from jax import lax
from jax.experimental import pallas as pl
from jax.experimental.pallas import tpu as pltpu
from jax.sharding import Mesh
from jax.sharding import PartitionSpec as P

epsilon = 1e-06
low = jnp.bfloat16
wide = jnp.float32
SWAP = [(0, 1), (1, 0)]
ROW_TILE = 16
MIB = 1 << 20
TILE = 256
WAIT_LAST = 8
LONG = 16
BRIEF = pl.CostEstimate(flops=0, bytes_accessed=0, transcendentals=0)


def normed(values, gain):
    return values * lax.rsqrt(jnp.mean(values * values, axis=-1, keepdims=True) + epsilon) * gain


def dot(left, right):
    return jnp.dot(left, right, preferred_element_type=jnp.float32)


def dot_nt(left, right):
    return lax.dot_general(left, right, (((1,), (1,)), ((), ())), preferred_element_type=jnp.float32)


def dot_tn(left, right):
    return lax.dot_general(left, right, (((0,), (0,)), ((), ())), preferred_element_type=jnp.float32)


def zero_of(anchor):
    return jnp.minimum(jnp.abs(anchor[(0,) * anchor.ndim].astype(wide)), 0.0)


def flat_index(axes):
    index = 0
    for axis in axes:
        index = index * 2 + lax.axis_index(axis)
    return index


def take(stack, index):
    return lax.dynamic_index_in_dim(stack, index, 0, keepdims=False)


def take_at(stack, index, at):
    return lax.dynamic_index_in_dim(stack, index, at, keepdims=False)


def sems(amount):
    return pltpu.SemaphoreType.DMA((amount,))


def toward(flips):
    return {axis: 1 - lax.axis_index(axis) for axis in flips}


def remote(src, dst, send, recv, flips):
    return pltpu.make_async_remote_copy(
        src_ref=src,
        dst_ref=dst,
        send_sem=send,
        recv_sem=recv,
        device_id=toward(flips),
        device_id_type=pl.DeviceIdType.MESH,
    )


class Direct:
    def __init__(self, axes, operand, block, pick=None, rounds=0):
        self.axes, self.block, self.pick, self.rounds = axes, block, pick, rounds
        self.amount = 1 << len(axes)
        self.operands = [operand]
        self.results = [jax.ShapeDtypeStruct((self.amount,) + block, operand.dtype)]
        self.scratch = [
            sems(self.amount),
            sems(self.amount),
            sems(2),
            pltpu.VMEM(block, operand.dtype),
        ]
        self.steps = [
            tuple(axis for bit, axis in enumerate(reversed(axes)) if step >> bit & 1)
            for step in range(self.amount)
        ]
        self.flips = self.steps[1:]

    def begin(self, operands, target, send, recv):
        copies = []
        for step in range(1, self.amount):
            other = 0
            for axis in self.axes:
                place = lax.axis_index(axis)
                other = other * 2 + (1 - place if axis in self.steps[step] else place)
            copy = remote(
                operands[0].at[step if self.pick is None else self.pick(other)],
                target,
                send.at[step],
                recv.at[step],
                self.steps[step],
            )
            copy.start()
            copies.append(copy)
        return copies

    def keep(self, operands, target, local, held):
        own = 0 if self.pick is None else self.pick(flat_index(self.axes))
        load = pltpu.make_async_copy(operands[0].at[own], held, local.at[0])
        load.start()
        load.wait()
        store = pltpu.make_async_copy(held, target, local.at[1])
        store.start()
        store.wait()

    def run(self, operands, results, scratch):
        send, recv, local, held = scratch
        for _ in range(self.rounds):
            yield
        target = results[0].at[flat_index(self.axes)]
        copies = self.begin(operands, target, send, recv)
        self.keep(operands, target, local, held)
        for _ in range(WAIT_LAST):
            yield
        for copy in copies:
            copy.wait()


class Spread(Direct):
    def __init__(self, axes, others, operand, block, pick=lambda place: place):
        super().__init__(axes, operand, block, pick)
        self.others = others
        self.results = [
            jax.ShapeDtypeStruct((self.amount,) + (2,) * len(others) + block, operand.dtype)
        ]
        self.scratch += [sems(max(1, len(others))), sems(max(1, len(others)))]
        self.flips = self.flips + [(axis,) for axis in others]

    def run(self, operands, results, scratch):
        send, recv, local, held, next_send, next_recv = scratch
        here = flat_index(self.axes)
        place = {axis: lax.axis_index(axis) for axis in self.others}
        spot = tuple(place[axis] for axis in self.others)
        copies = self.begin(operands, results[0].at[(here,) + spot], send, recv)
        self.keep(operands, results[0].at[(here,) + spot], local, held)
        yield
        for copy in copies:
            copy.wait_recv()
        for stage, axis in enumerate(self.others):
            region = tuple(
                slice(None) if other in self.others[:stage] else place[other]
                for other in self.others
            )
            region = results[0].at[(slice(None),) + region]
            copy = remote(region, region, next_send.at[stage], next_recv.at[stage], (axis,))
            copy.start()
            yield
            copy.wait()
        for copy in copies:
            copy.wait_send()


class Gather:
    def __init__(self, axes, operand, parts):
        self.axes, self.parts = axes, parts
        self.operands = [operand]
        self.results = [
            jax.ShapeDtypeStruct((2,) * len(axes) + operand.shape, operand.dtype)
        ]
        amount = len(parts) * len(axes)
        self.scratch = [sems(amount), sems(amount), sems(2), pltpu.VMEM(operand.shape, operand.dtype)]
        self.flips = [(axis,) for axis in axes]

    def run(self, operands, results, scratch):
        send, recv, local, held = scratch
        place = {axis: lax.axis_index(axis) for axis in self.axes}
        load = pltpu.make_async_copy(operands[0], held, local.at[0])
        load.start()
        load.wait()
        spot = tuple(place[axis] for axis in self.axes)
        store = pltpu.make_async_copy(held, results[0].at[spot], local.at[1])
        store.start()
        store.wait()
        copies = {}

        def start(number, stage):
            lo, hi, order = self.parts[number]
            region = tuple(
                slice(None) if axis in order[:stage] else place[axis] for axis in self.axes
            )
            region = results[0].at[region + (pl.ds(lo, hi - lo),)]
            slot = number * len(self.axes) + stage
            copies[number, stage] = remote(
                region, region, send.at[slot], recv.at[slot], (order[stage],)
            )
            copies[number, stage].start()

        for number in range(len(self.parts)):
            start(number, 0)
        yield
        for stage in range(1, len(self.axes)):
            for number in range(len(self.parts)):
                copies[number, stage - 1].wait_recv()
                start(number, stage)
            yield
        for number in range(len(self.parts)):
            copies[number, len(self.axes) - 1].wait_recv()
        for copy in copies.values():
            copy.wait_send()


class Reduce:
    def __init__(self, axes, operand, parts, ready=None, last=None, by_distance=False):
        self.axes, self.parts, self.by_distance = axes, parts, by_distance
        count, columns = operand.shape[-2:]
        self.operands = [operand]
        self.results = [jax.ShapeDtypeStruct((count, columns), wide)]
        self.scratch = []
        for lo, hi, order in parts:
            for stage in range(len(axes)):
                left = len(axes) - 1 - stage
                self.scratch.append(pltpu.VMEM((2,) * left + (hi - lo, columns), low))
            self.scratch.append(pltpu.VMEM((2,) * (len(axes) - 1) + (hi - lo, columns), low))
        self.scratch.append(pltpu.VMEM((count, columns), wide))
        amount = len(parts) * len(axes)
        self.flips = [(axis,) for axis in axes]
        self.last = None
        if last is not None:
            self.last = last(ready)
            self.results = self.last.results
            self.flips = self.flips + self.last.flips
            self.scratch += [pltpu.VMEM(ready.shape, low)] + self.last.scratch
        self.scratch += [sems(amount), sems(amount), sems(len(parts) + 1)]

    def run(self, operands, results, scratch):
        stages = len(self.axes)
        send, recv, local = scratch[-3:]
        total = scratch[len(self.parts) * (stages + 1)]
        place = {axis: 0 if self.by_distance else lax.axis_index(axis) for axis in self.axes}
        copies, loads = {}, []

        def buffers(number):
            base = number * (stages + 1)
            return scratch[base : base + stages], scratch[base + stages]

        def start(number, stage):
            lo, hi, order = self.parts[number]
            slots, held = buffers(number)
            slot = number * stages + stage
            axis = order[stage]
            if stage == 0:
                spot = tuple(
                    1 - place[other] if other == axis else slice(None) for other in self.axes
                )
                source = operands[0].at[spot + (pl.ds(lo, hi - lo),)]
            else:
                rest = [other for other in self.axes if other != order[0]]
                spot = tuple(
                    place[other]
                    if other in order[:stage]
                    else 1 - place[other]
                    if other == axis
                    else slice(None)
                    for other in rest
                )
                source = held.at[spot]
            copies[number, stage] = remote(
                source, slots[stage], send.at[slot], recv.at[slot], (axis,)
            )
            copies[number, stage].start()

        for number, (lo, hi, order) in enumerate(self.parts):
            start(number, 0)
            spot = tuple(
                place[other] if other == order[0] else slice(None) for other in self.axes
            )
            load = pltpu.make_async_copy(
                operands[0].at[spot + (pl.ds(lo, hi - lo),)], buffers(number)[1], local.at[number]
            )
            load.start()
            loads.append(load)
        yield
        for stage in range(stages):
            for number, (lo, hi, order) in enumerate(self.parts):
                slots, held = buffers(number)
                if stage == 0:
                    loads[number].wait()
                copies[number, stage].wait_recv()
                rest = [other for other in self.axes if other != order[0]]
                gone = order[: stage + 1]
                free = [other for other in rest if other not in gone]
                for code in range(1 << len(free)):
                    bits = {axis: code >> bit & 1 for bit, axis in enumerate(free)}
                    spot = tuple(bits[axis] if axis in bits else place[axis] for axis in rest)
                    slot_spot = tuple(bits[axis] for axis in free)
                    last = stage == stages - 1

                    def add(step, carry, spot=spot, slot_spot=slot_spot, last=last):
                        rows = pl.ds(pl.multiple_of(step * ROW_TILE, ROW_TILE), ROW_TILE)
                        value = held[spot + (rows,)].astype(wide)
                        value = value + slots[stage][slot_spot + (rows,)].astype(wide)
                        if last:
                            at = pl.multiple_of(step * ROW_TILE + lo, ROW_TILE)
                            total[pl.ds(at, ROW_TILE)] = value
                        else:
                            held[spot + (rows,)] = value.astype(low)
                        return carry

                    lax.fori_loop(0, (hi - lo) // ROW_TILE, add, 0)
                if stage + 1 < stages:
                    start(number, stage + 1)
            yield
        if self.last is None:
            store = pltpu.make_async_copy(total, results[0], local.at[len(self.parts)])
            store.start()
            store.wait()
        else:
            ready, *others = scratch[len(self.parts) * (stages + 1) + 1 : -3]
            ready[...] = total[...].astype(low).reshape(ready.shape)
            yield from self.last.run([ready], results, others)
        for copy in copies.values():
            copy.wait_send()


class ReduceBoth(Reduce):
    def __init__(self, axes, operand, other, parts):
        super().__init__(axes, operand, parts, by_distance=True)
        self.operands = [operand, other]
        shape = operand.shape
        self.scratch = [pltpu.VMEM(shape, low), pltpu.VMEM(shape, low)]
        for lo, hi, order in parts:
            for stage in range(len(axes)):
                left = len(axes) - 1 - stage
                self.scratch.append(pltpu.VMEM((2,) * left + (hi - lo, shape[-1]), low))
        self.scratch.append(pltpu.VMEM(shape[-2:], wide))
        amount = len(parts) * len(axes)
        self.scratch += [sems(amount), sems(amount), sems(2 * len(parts) + 1)]

    def run(self, operands, results, scratch):
        stages = len(self.axes)
        held, added, *slots = scratch[:-4]
        total, send, recv, local = scratch[-4:]
        copies, loads = {}, []
        every = (slice(None),) * stages

        def start(number, stage):
            lo, hi, order = self.parts[number]
            spot = tuple(
                0 if axis in order[:stage] else 1 if axis == order[stage] else slice(None)
                for axis in self.axes
            )
            slot = number * stages + stage
            copies[number, stage] = remote(
                held.at[spot + (pl.ds(lo, hi - lo),)],
                slots[slot],
                send.at[slot],
                recv.at[slot],
                (order[stage],),
            )
            copies[number, stage].start()

        def add_all(lo, hi, free, spot_of, source, last):
            for code in range(1 << len(free)):
                bits = {axis: code >> bit & 1 for bit, axis in enumerate(free)}
                spot = tuple(bits.get(axis, 0) for axis in self.axes)
                source_spot = spot_of(bits)

                def add(step, carry, spot=spot, source_spot=source_spot):
                    at = pl.multiple_of(step * ROW_TILE, ROW_TILE)
                    rows = pl.ds(pl.multiple_of(at + lo, ROW_TILE), ROW_TILE)
                    value = held[spot + (rows,)].astype(wide)
                    shift = rows if source is added else pl.ds(at, ROW_TILE)
                    value = value + source[source_spot + (shift,)].astype(wide)
                    if last:
                        total[rows] = value
                    else:
                        held[spot + (rows,)] = value.astype(low)
                    return carry

                lax.fori_loop(0, (hi - lo) // ROW_TILE, add, 0)

        for number, (lo, hi, order) in enumerate(self.parts):
            span = every + (pl.ds(lo, hi - lo),)
            for which, (operand, buffer) in enumerate(zip(operands, (held, added))):
                load = pltpu.make_async_copy(
                    operand.at[span], buffer.at[span], local.at[2 * number + which]
                )
                load.start()
                loads.append(load)
        for number, (lo, hi, order) in enumerate(self.parts):
            loads[2 * number].wait()
            loads[2 * number + 1].wait()
            add_all(
                lo, hi, self.axes, lambda bits: tuple(bits[axis] for axis in self.axes), added, False
            )
            start(number, 0)
        yield
        for stage in range(stages):
            for number, (lo, hi, order) in enumerate(self.parts):
                copies[number, stage].wait_recv()
                free = [axis for axis in self.axes if axis not in order[: stage + 1]]
                add_all(
                    lo,
                    hi,
                    free,
                    lambda bits, free=free: tuple(bits[axis] for axis in free),
                    slots[number * stages + stage],
                    stage == stages - 1,
                )
                if stage + 1 < stages:
                    start(number, stage + 1)
            yield
        store = pltpu.make_async_copy(total, results[0], local.at[2 * len(self.parts)])
        store.start()
        store.wait()
        for copy in copies.values():
            copy.wait_send()


class Task:
    flips = ()


class WeightGrad(Task):
    def __init__(self, lefts, rights, turns=1):
        self.amount, self.turns = len(lefts), turns
        self.operands = list(lefts) + list(rights)
        self.blocks, self.rows, self.columns = lefts[0].shape
        self.width = rights[0].shape[-1]
        self.results = [jax.ShapeDtypeStruct((self.columns, self.width), low)]
        shape = (self.amount, self.blocks, self.rows, self.width)
        self.scratch = [pltpu.VMEM(shape, low), sems(self.amount)]

    def run(self, operands, results, scratch):
        held, done = scratch
        steps = self.columns // TILE
        copies = [
            pltpu.make_async_copy(right, held.at[number], done.at[number])
            for number, right in enumerate(operands[self.amount :])
        ]
        for copy in copies:
            copy.start()
        for copy in copies:
            copy.wait()

        def body(*refs):
            total = 0.0
            for number, left_ref in enumerate(refs[:-1]):
                right = held[number].reshape(-1, self.width)
                total = total + dot_tn(left_ref[...].reshape(-1, TILE), right)
            refs[-1][...] = total.astype(low)

        def place(step):
            return (step % self.turns * (steps // self.turns) + step // self.turns, 0)

        block = pl.BlockSpec((self.blocks, self.rows, TILE), lambda step: (0, 0, step))
        pltpu.emit_pipeline(
            body,
            grid=(steps,),
            in_specs=[block] * self.amount,
            out_specs=[pl.BlockSpec((TILE, self.width), place)],
        )(*operands[: self.amount], results[0])


def flow_kernel(flows, plan, *refs):
    refs = list(refs)

    def cut(amount):
        part = refs[:amount]
        del refs[:amount]
        return part

    operands = [cut(len(flow.operands)) for flow in flows]
    results = [cut(len(flow.results)) for flow in flows]
    scratch = [cut(len(flow.scratch)) for flow in flows]
    partners = []
    for flow in flows:
        partners += [flips for flips in flow.flips if flips not in partners]
    barrier = pltpu.get_barrier_semaphore()
    for flips in partners:
        pl.semaphore_signal(
            barrier, inc=1, device_id=toward(flips), device_id_type=pl.DeviceIdType.MESH
        )
    pl.semaphore_wait(barrier, len(partners))
    tasks = [part for part in zip(flows, operands, results, scratch) if isinstance(part[0], Task)]
    runs = [
        flow.run(*parts)
        for flow, *parts in zip(flows, operands, results, scratch)
        if not isinstance(flow, Task)
    ]
    for run in runs:
        next(run)
    for number in plan:
        if number < 0:
            flow, *parts = tasks[-1 - number]
            flow.run(*parts)
        elif number < len(runs):
            next(runs[number], None)
    while runs:
        runs = [run for run in runs if next(run, run) is not run]


def transfer(number, flows, plan=()):
    arrays = [array for flow in flows for array in flow.operands]
    shapes = [shape for flow in flows for shape in flow.results]
    anywhere = pl.BlockSpec(memory_space=pl.ANY)
    return pl.pallas_call(
        functools.partial(flow_kernel, flows, plan),
        out_shape=shapes,
        in_specs=[anywhere] * len(arrays),
        out_specs=[anywhere] * len(shapes),
        scratch_shapes=[one for flow in flows for one in flow.scratch],
        compiler_params=pltpu.CompilerParams(
            collective_id=number, has_side_effects=True, vmem_limit_bytes=60 * MIB
        ),
        cost_estimate=BRIEF,
    )(*arrays)


def tile_of(rows, most):
    steps = -(-rows // most)
    while rows % steps or (rows // steps) % ROW_TILE:
        steps += 1
    return rows // steps


def whole_block(shape):
    return pl.BlockSpec(shape, lambda *ids: (0,) * len(shape), pipeline_mode=pl.Buffered(1))


def expert_kernel(
    near,
    ids_ref,
    rows_ref,
    grad_ref,
    gate_ref,
    pieces_gate,
    pieces_up,
    pieces_down,
    hidden_ref,
    d_in_ref,
    d_gate_ref,
    made_ref,
    back_ref,
    in_ref,
    down_ref,
    done,
):
    @pl.when(pl.program_id(0) == 0)
    def _():
        copies = []
        half = pieces_gate.shape[3]
        for pieces, held, lo in (
            (pieces_gate, in_ref, 0),
            (pieces_up, in_ref, half),
            (pieces_down, down_ref, 0),
        ):
            amount, parts, rows, columns = pieces.shape
            for spot in range(amount):
                for part in range(parts):
                    block = (part // near * amount + spot) * near + part % near
                    copy = pltpu.make_async_copy(
                        pieces.at[spot, part],
                        held.at[pl.ds(block * rows, rows), pl.ds(lo, columns)],
                        done.at[len(copies)],
                    )
                    copy.start()
                    copies.append(copy)
        for copy in copies:
            copy.wait()

    hidden_width = down_ref.shape[0]
    gate = gate_ref[...]
    acts = dot(rows_ref[...], in_ref[...])
    d_plain = dot_nt(grad_ref[...], down_ref[...])
    act_gate, act_up = acts[:, :hidden_width], acts[:, hidden_width:]
    sigmoid = 1.0 / (1.0 + jnp.exp(-act_gate))
    silu_gate = act_gate * sigmoid
    hidden = silu_gate * act_up
    d_gate_ref[...] = jnp.sum(hidden * d_plain, axis=1, keepdims=True)
    d_hidden = d_plain * gate
    hidden_low = (hidden * gate).astype(low)
    d_act_gate = d_hidden * act_up * (sigmoid * (1.0 + act_gate * (1.0 - sigmoid)))
    d_in = jnp.concatenate([d_act_gate.astype(low), (d_hidden * silu_gate).astype(low)], axis=1)
    hidden_ref[...] = hidden_low
    d_in_ref[...] = d_in
    back_ref[...] = dot_nt(d_in, in_ref[...]).astype(low)
    made_ref[...] = dot(hidden_low, down_ref[...]).astype(low)


def expert_rows(rows, grad_rows, gate, pieces, near, ids):
    blocks, tile, model_width = rows.shape
    amount = blocks * tile
    hidden_width = pieces[0].shape[3]

    block = pl.BlockSpec((None, tile, model_width), lambda step, ids: (ids[step], 0, 0))

    def by_place(columns):
        return pl.BlockSpec((tile, columns), lambda step, ids: (ids[step], 0))

    def by_distance(columns):
        return pl.BlockSpec((tile, columns), lambda step, ids: (step, 0))

    outs = [
        (by_place, hidden_width, low),
        (by_place, 2 * hidden_width, low),
        (by_distance, 1, wide),
        (by_distance, model_width, low),
        (by_distance, model_width, low),
    ]
    anywhere = pl.BlockSpec(memory_space=pl.ANY)
    return pl.pallas_call(
        functools.partial(expert_kernel, near),
        grid_spec=pltpu.PrefetchScalarGridSpec(
            num_scalar_prefetch=1,
            grid=(blocks,),
            in_specs=[block, block, by_place(1)]
            + [anywhere] * len(pieces),
            out_specs=[spec(columns) for spec, columns, _ in outs],
            scratch_shapes=[
                pltpu.VMEM((model_width, 2 * hidden_width), low),
                pltpu.VMEM((hidden_width, model_width), low),
                sems(sum(piece.shape[0] * piece.shape[1] for piece in pieces)),
            ],
        ),
        out_shape=[jax.ShapeDtypeStruct((amount, columns), kind) for _, columns, kind in outs],
        compiler_params=pltpu.CompilerParams(vmem_limit_bytes=52 * MIB),
        cost_estimate=pl.CostEstimate(
            flops=LONG * 18 * amount * model_width * hidden_width,
            bytes_accessed=14 * amount * model_width,
            transcendentals=0,
        ),
    )(ids, rows, grad_rows, gate, *pieces)


def weight_kernel(amount, *refs):
    total = 0.0
    for left, right in zip(refs[:amount], refs[amount:-1]):
        total = total + dot_tn(left[...], right[...])
    refs[-1][...] = total.astype(low).reshape(refs[-1].shape)


def weight_grad(lefts, rights, groups=1, parts=1, tile=256):
    amount = len(lefts)
    columns, out_columns = lefts[0].shape[1], rights[0].shape[1]
    piece = columns // (groups * parts)
    tile = min(tile, piece * parts)
    if tile < piece:
        groups, parts, piece = columns // tile, 1, tile
    runs = piece * parts // tile
    return pl.pallas_call(
        functools.partial(weight_kernel, amount),
        grid=(columns // tile,),
        in_specs=[pl.BlockSpec((left.shape[0], tile), lambda step: (0, step)) for left in lefts]
        + [whole_block(right.shape) for right in rights],
        out_specs=pl.BlockSpec(
            (tile // piece, 1, piece, out_columns), lambda step: (step % runs, step // runs, 0, 0)
        ),
        out_shape=jax.ShapeDtypeStruct((parts, groups, piece, out_columns), low),
        compiler_params=pltpu.CompilerParams(vmem_limit_bytes=52 * MIB),
        cost_estimate=BRIEF,
    )(*lefts, *rights)


def widen_kernel(pieces_ref, *out_refs):
    columns = out_refs[0].shape[2]
    for number, out_ref in enumerate(out_refs):
        span = slice(number * columns, (number + 1) * columns)
        out_ref[...] = pieces_ref[:, :, span].astype(wide)


def widen_heads_kernel(parts, piece_ref, query_ref, key_ref, value_ref):
    groups, width = piece_ref.shape[0], key_ref.shape[1]
    columns = piece_ref.shape[2] - 2 * width
    piece = columns // parts
    for part in range(parts):
        for group in range(groups):
            at = (part * groups + group) * piece
            span = slice(part * piece, (part + 1) * piece)
            query_ref[:, at : at + piece] = piece_ref[group, :, span].astype(wide)
    for number, out_ref in enumerate((key_ref, value_ref)):
        span = slice(columns + number * width, columns + (number + 1) * width)
        total = piece_ref[0, :, span].astype(wide)
        for group in range(1, groups):
            total = total + piece_ref[group, :, span].astype(wide)
        out_ref[...] = total


def by_head(pieces, parts, width):
    owners, groups, rows, columns = pieces.shape
    spans = [groups * (columns - 2 * width), width, width]
    return pl.pallas_call(
        functools.partial(widen_heads_kernel, parts),
        grid=(owners,),
        in_specs=[pl.BlockSpec((None, groups, rows, columns), lambda step: (step, 0, 0, 0))],
        out_specs=[pl.BlockSpec((rows, span), lambda step: (0, step)) for span in spans],
        out_shape=[jax.ShapeDtypeStruct((rows, owners * span), wide) for span in spans],
        cost_estimate=BRIEF,
    )(pieces)


def by_expert(pieces, amount):
    team, rows, columns = pieces.shape[0], pieces.shape[-2], pieces.shape[-1]
    pieces = pieces.reshape(team, -1, rows, columns)
    groups = pieces.shape[1]
    out = (groups * team, rows, columns // amount)
    return pl.pallas_call(
        widen_kernel,
        grid=(groups, team // 4),
        in_specs=[pl.BlockSpec((4, None, rows, columns), lambda group, place: (place, group, 0, 0))],
        out_specs=[
            pl.BlockSpec((4,) + out[1:], lambda group, place: (group * (team // 4) + place, 0, 0))
        ]
        * amount,
        out_shape=[jax.ShapeDtypeStruct(out, wide)] * amount,
        cost_estimate=BRIEF,
    )(pieces)


def turned(values, cosine, sine):
    return values * cosine + pltpu.roll(values, values.shape[1] // 2, 1) * sine


def turned_back(grads, cosine, sine):
    return grads * cosine + pltpu.roll(grads * sine, grads.shape[1] // 2, 1)


def head_scale(values):
    return lax.rsqrt(jnp.mean(values * values, axis=1, keepdims=True) + epsilon)


def prep_kernel(
    heads,
    rows_ref,
    w_ref,
    place_ref,
    inverse_ref,
    sign_ref,
    gain_q,
    gain_k,
    lin_ref,
    query_ref,
    keyed_ref,
    value_ref,
    cosine_ref,
    sine_ref,
):
    width = gain_q.shape[1]
    angle = place_ref[...].astype(wide) * inverse_ref[...]
    cosine, sine = jnp.cos(angle), jnp.sin(angle) * sign_ref[...]
    cosine_ref[...] = cosine
    sine_ref[...] = sine
    lin = dot(rows_ref[...], w_ref[...])
    lin_ref[...] = lin[:, : (heads + 1) * width]
    for head in range(heads + 1):
        span = slice(head * width, (head + 1) * width)
        values = lin[:, span]
        gain = gain_q[...] if head < heads else gain_k[...]
        made = turned(values * head_scale(values) * gain, cosine, sine).astype(low)
        if head < heads:
            query_ref[:, span] = made
        else:
            keyed_ref[...] = made
    value_ref[...] = lin[:, (heads + 1) * width :].astype(low)


def unprep_kernel(
    heads,
    scale,
    d_query_ref,
    d_keyed_ref,
    d_value_ref,
    lin_ref,
    w_ref,
    cosine_ref,
    sine_ref,
    gain_q,
    gain_k,
    rows_ref,
    gain_ref,
    d_lin_ref,
    d_one_ref,
    d_gain_q,
    d_gain_k,
    d_gain,
):
    width = gain_q.shape[1]
    cosine, sine = cosine_ref[...], sine_ref[...]

    @pl.when(pl.program_id(0) == 0)
    def _():
        d_gain_q[...] = jnp.zeros_like(d_gain_q)
        d_gain_k[...] = jnp.zeros_like(d_gain_k)
        d_gain[...] = jnp.zeros_like(d_gain)

    for head in range(heads + 1):
        span = slice(head * width, (head + 1) * width)
        values = lin_ref[:, span]
        if head < heads:
            grads, gain, d_head = d_query_ref[:, span].astype(wide), gain_q[...], d_gain_q
        else:
            grads, gain, d_head = d_keyed_ref[...] * scale, gain_k[...], d_gain_k
        grads = turned_back(grads, cosine, sine)
        factor = head_scale(values)
        plain = values * factor
        d_head[...] += jnp.sum(grads * plain, axis=0, keepdims=True)
        grads = grads * gain
        mean = jnp.mean(grads * plain, axis=1, keepdims=True)
        d_lin_ref[:, span] = (factor * (grads - plain * mean)).astype(low)
    d_lin_ref[:, (heads + 1) * width :] = d_value_ref[...].astype(low)
    d_one = dot_nt(d_lin_ref[...], w_ref[...])
    d_one_ref[...] = d_one.astype(low)
    d_gain[...] += jnp.sum(d_one * rows_ref[...].astype(wide), axis=0, keepdims=True) / gain_ref[...]


def row_call(kernel, rows, tiled, fixed, outs, sums):
    tile = tile_of(rows, 256)

    def by_rows(columns):
        return pl.BlockSpec((tile, columns), lambda step: (step, 0))

    return pl.pallas_call(
        kernel,
        grid=(rows // tile,),
        in_specs=[
            whole_block(array.shape) if number in fixed else by_rows(array.shape[1])
            for number, array in enumerate(tiled)
        ],
        out_specs=[by_rows(columns) for columns, _ in outs]
        + [pl.BlockSpec((1, columns), lambda step: (0, 0)) for columns in sums],
        out_shape=[jax.ShapeDtypeStruct((rows, columns), kind) for columns, kind in outs]
        + [jax.ShapeDtypeStruct((1, columns), wide) for columns in sums],
        compiler_params=pltpu.CompilerParams(vmem_limit_bytes=48 * MIB),
        cost_estimate=BRIEF,
    )(*tiled)


def mask_tile(bias, k_place, k_segment, q_place, q_segment):
    allowed = (k_segment[...] == q_segment[0]) & (k_place[...] <= q_place[0])
    bias[...] = jnp.where(allowed, 0.0, -1e30)


def ahead_kernel(
    scale, k_place, k_segment, q_place, q_segment, q_ref, k_ref, vt_ref, mixed_ref, total_ref, bias
):
    @pl.when(pl.program_id(2) == 0)
    def _():
        mask_tile(bias, k_place.at[0], k_segment.at[0], q_place, q_segment)

    scores = dot_nt(k_ref[0], q_ref[0]) * scale + bias[...]
    row_max = jnp.max(scores, axis=0, keepdims=True)
    expd = jnp.exp(scores - row_max)
    row_total = jnp.sum(expd, axis=0, keepdims=True)
    mixed = dot(vt_ref[0], expd.astype(low)) / row_total
    mixed_ref[0] = mixed.T.astype(low)
    total_ref[0, 0] = row_max + jnp.log(row_total)


def behind_kernel(
    scale,
    k_place,
    k_segment,
    q_place,
    q_segment,
    q_ref,
    d_mixed_ref,
    k_ref,
    v_ref,
    kt_ref,
    total_ref,
    d_q_ref,
    d_k_ref,
    d_v_ref,
    bias,
):
    @pl.when(pl.program_id(2) == 0)
    def _():
        mask_tile(bias, k_place.at[0], k_segment.at[0], q_place, q_segment)

    @pl.when((pl.program_id(1) == 0) & (pl.program_id(2) == 0))
    def _():
        d_k_ref[...] = jnp.zeros_like(d_k_ref)
        d_v_ref[...] = jnp.zeros_like(d_v_ref)

    query, d_mixed = q_ref[0], d_mixed_ref[0]
    probs = jnp.exp(dot_nt(k_ref[0], query) * scale + bias[...] - total_ref[0, 0])
    d_probs = dot_nt(v_ref[0], d_mixed)
    row_dot = jnp.sum(probs * d_probs, axis=0, keepdims=True)
    d_scores = (probs * (d_probs - row_dot)).astype(low)
    d_v_ref[0] += dot(probs.astype(low), d_mixed)
    d_k_ref[0] += dot(d_scores, query)
    d_q_ref[0] = (dot(kt_ref[0], d_scores) * scale).T.astype(low)


def attention_call(kernel, marks, arrays, kinds, outs, width, scale, work):
    place, segment = marks
    seqs, length = place.shape
    tile = min(256, length)
    heads = arrays[0].shape[2] // width
    specs = {
        "query": pl.BlockSpec((1, tile, width), lambda s, i, h: (s, i, h)),
        "keys": pl.BlockSpec((1, length, width), lambda s, i, h: (s, 0, 0)),
        "flat": pl.BlockSpec((1, width, length), lambda s, i, h: (s, 0, 0)),
        "total": pl.BlockSpec((1, 1, 1, tile), lambda s, i, h: (s, h, 0, i)),
    }
    column = pl.BlockSpec((1, length, 1), lambda s, i, h: (s, 0, 0))
    row = pl.BlockSpec((1, 1, tile), lambda s, i, h: (s, 0, i))
    return pl.pallas_call(
        functools.partial(kernel, scale),
        grid=(seqs, length // tile, heads),
        in_specs=[column, column, row, row] + [specs[kind] for kind in kinds],
        out_specs=[specs[kind] for kind, _ in outs],
        out_shape=[shape for _, shape in outs],
        scratch_shapes=[pltpu.VMEM((length, tile), wide)],
        compiler_params=pltpu.CompilerParams(vmem_limit_bytes=48 * MIB),
        cost_estimate=BRIEF,
    )(place[:, :, None], segment[:, :, None], place[:, None, :], segment[:, None, :], *arrays)


def per_device(
    g_axes,
    c_axes,
    f_axes,
    tokens,
    places,
    segments,
    routes,
    w_query,
    w_key,
    w_value,
    w_out,
    w_router,
    w_gate,
    w_up,
    w_down,
    gain_attn,
    gain_ffn,
    gain_query,
    gain_key,
    cotangent,
):
    groups, parts_c, parts_f = 1 << len(g_axes), 1 << len(c_axes), 1 << len(f_axes)
    count = tokens.shape[1]
    width = gain_query.shape[0]
    model_width = tokens.shape[2]
    kv_heads = w_key.shape[1] // width // parts_c
    assert kv_heads == 1
    heads = w_query.shape[1] // width // parts_c // groups
    experts = w_gate.shape[0]
    hidden_width = w_gate.shape[2]
    scale = 1.0 / math.sqrt(width)
    rows_d = w_query.shape[0]
    rows_o = w_out.shape[0]
    rows_f = w_down.shape[1]
    pair_count = experts.bit_length() - 1 - len(g_axes) - len(c_axes)
    assert 0 <= pair_count <= len(f_axes)
    far_axes = f_axes[: len(f_axes) - pair_count]
    near_axes = f_axes[len(f_axes) - pair_count :]
    parts_near = 1 << len(near_axes)
    team_axes = c_axes + near_axes
    team = parts_c * parts_near
    own_axes = c_axes + f_axes
    plane_axes = g_axes + c_axes
    cluster_axes = g_axes + team_axes
    all_axes = g_axes + c_axes + f_axes
    all_axes_but_core = c_axes[:-1] + f_axes[::-1] + g_axes
    g_here = flat_index(g_axes)
    core = c_axes[-1:]
    plane_shape = (2,) * len(plane_axes) + (count, model_width)
    cluster_shape = (2,) * len(cluster_axes) + (count, model_width)
    turn = g_axes + c_axes[:-1]
    half = count // 2
    plane_parts = [(0, half, turn), (half, count, turn[1:] + turn[:1])]
    turn = turn + near_axes
    third = (count // 3) // ROW_TILE * ROW_TILE
    cuts = [0, count - 2 * third, count - third, count]
    cluster_parts = [
        (cuts[step], cuts[step + 1], turn[step:] + turn[:step]) for step in range(len(cuts) - 1)
    ]
    def core_last(parts):
        return [(lo, hi, order + core) for lo, hi, order in parts]

    def core_first(parts):
        return [(lo, hi, core + order) for lo, hi, order in parts]

    q_cols = heads * width
    qkv_cols = q_cols + 2 * width
    even = rows_o % (groups * width) == 0
    if even:
        own_query = w_query.reshape(rows_d, parts_c, parts_f, groups, q_cols // parts_f)
        own_query = own_query.transpose(3, 1, 0, 2, 4)
    else:
        own_query = w_query.reshape(rows_d, parts_c, groups, q_cols).transpose(2, 1, 0, 3)
    own_query = take(own_query.reshape(groups, parts_c, rows_d, q_cols), g_here)
    mine_qkv = jnp.concatenate(
        [
            own_query,
            w_key.reshape(rows_d, parts_c, width).transpose(1, 0, 2),
            w_value.reshape(rows_d, parts_c, width).transpose(1, 0, 2),
        ],
        axis=2,
    )
    wide_router = jnp.pad(w_router, ((0, 0), (0, width - experts)))
    resid = tokens[0].astype(jnp.float32)
    norm_one, back_one = jax.vjp(normed, resid, gain_attn)

    def own_expert(place):
        return flat_index(g_axes) * team + place

    mine_out = take(w_out.reshape(groups, -1, model_width), g_here) if even else w_out
    grad_parts = [(lo, hi, near_axes + order) for lo, hi, order in plane_parts]
    all_one, w_qkv, own_grads, pieces_down, w_mix, got_gate, got_up, full_router, marks = transfer(
        1,
        [
            Gather(plane_axes, norm_one.astype(low), core_last(plane_parts)),
            Spread(c_axes, f_axes, mine_qkv, (rows_d, qkv_cols)),
            Gather(turn, cotangent[0], grad_parts),
            Spread(team_axes, far_axes, w_down, w_down.shape[1:], own_expert),
            Gather(f_axes, mine_out, [(0, mine_out.shape[0], f_axes)]),
            Direct(team_axes, w_gate, w_gate.shape[1:], own_expert),
            Direct(team_axes, w_up, w_up.shape[1:], own_expert),
            Direct(own_axes, wide_router[None], wide_router.shape, lambda place: 0),
            Direct(
                g_axes,
                jnp.stack([places[0], segments[0]])[None],
                (2,) + places.shape[1:],
                lambda place: 0,
            ),
        ],
        (1, 0, 2, 3, 0, 2, 4, 1, 0),
    )
    blocks = 1 << len(turn)
    own_grads = own_grads.reshape(blocks, count, model_width)
    far_grads = lax.ppermute(own_grads, core[0], SWAP)
    w_qkv = w_qkv.reshape(model_width, qkv_cols)
    all_one = all_one.reshape(-1, model_width)
    full_router = full_router.reshape(model_width, width)[:, :experts]

    w_mix = w_mix.reshape(-1, model_width)
    if not even:
        w_mix = take(w_mix.reshape(groups, q_cols, model_width), g_here)

    def from_far(got):
        return lax.all_gather(got, far_axes, axis=0, tiled=False) if far_axes else got[None]

    pieces_gate, pieces_up = from_far(got_gate), from_far(got_up)
    pieces_down = pieces_down.reshape((team, -1) + w_down.shape[1:]).transpose(1, 0, 2, 3)
    if rows_f % ROW_TILE:
        pieces_down = pieces_down.reshape((-1, parts_c, parts_near) + w_down.shape[1:])
        pieces_down = pieces_down.transpose(1, 0, 2, 3, 4).reshape(1, 1, hidden_width, model_width)

    place, segment = marks[:, 0], marks[:, 1]
    length = place.shape[1]
    rows = groups * length
    steps = jnp.arange(width // 2).astype(wide)
    inverse = jnp.exp(steps * (-2.0 * math.log(1000000.0) / width))
    inverse = jnp.concatenate([inverse, inverse])[None]
    sign = jnp.where(jnp.arange(width) < width // 2, -1.0, 1.0)[None]
    head_gains = (gain_query[None], gain_key[None])
    lin, query_low, keyed_low, value_low, cosine, sine = row_call(
        functools.partial(prep_kernel, heads),
        rows,
        (all_one, w_qkv, place.reshape(rows, 1), inverse, sign) + head_gains,
        (1, 3, 4, 5, 6),
        [(q_cols + width, wide), (q_cols, low), (width, low), (width, low), (width, wide), (width, wide)],
        [],
    )
    query_low = query_low.reshape(groups, length, q_cols)
    keyed_low = keyed_low.reshape(groups, length, width)
    value_low = value_low.reshape(groups, length, width)
    total_shape = jax.ShapeDtypeStruct((groups, heads, 1, length), wide)
    mixed_low, log_total = attention_call(
        ahead_kernel,
        (place, segment),
        (query_low, keyed_low, value_low.transpose(0, 2, 1)),
        ("query", "keys", "flat"),
        [("query", jax.ShapeDtypeStruct(query_low.shape, low)), ("total", total_shape)],
        width,
        scale,
        4,
    )
    mixed_rows = mixed_low.reshape(groups * length, q_cols)
    branch = dot(mixed_rows, w_mix).astype(low).reshape(plane_shape)
    (branch,) = transfer(2, [Reduce(plane_axes, branch, core_first(plane_parts))])
    resid_one = resid + branch

    norm_two, back_two = jax.vjp(normed, resid_one, gain_ffn)
    normed_two = norm_two.astype(low)
    logits = dot(normed_two, full_router)
    labels = jnp.arange(experts, dtype=jnp.int32)
    chosen = jnp.any(routes[0][:, :, None] == labels[None, None, :], axis=1)
    logits = jnp.where(chosen, logits, -1e30)
    powers = jnp.where(chosen, jnp.exp(logits - jnp.max(logits, axis=-1, keepdims=True)), 0.0)
    gates = powers / jnp.sum(powers, axis=-1, keepdims=True)

    own_two, all_gates = transfer(
        3,
        [
            Gather(turn, normed_two, cluster_parts),
            Gather(cluster_axes, gates.T, [(0, experts, turn + core)]),
        ],
    )
    own_two = own_two.reshape(blocks, count, model_width)
    far_two = lax.ppermute(own_two, core[0], SWAP)
    gate_stack = take_at(all_gates, flat_index(cluster_axes), len(cluster_axes))
    core_here, core_spot = lax.axis_index(core[0]), cluster_axes.index(core[0])
    ids = jnp.bitwise_xor(jnp.arange(blocks), flat_index(turn)).astype(jnp.int32)
    sides = []
    pieces = (pieces_gate, pieces_up, pieces_down)
    for side, side_rows, side_grads in (
        (core_here, own_two, own_grads),
        (1 - core_here, far_two, far_grads),
    ):
        gate = take_at(gate_stack, side, core_spot).reshape(-1, 1)
        sides.append(expert_rows(side_rows, side_grads, gate, pieces, parts_near, ids))
        ids = ids + zero_of(sides[0][2]).astype(jnp.int32)
    hiddens, d_ins, d_gate_parts, made_parts, back_parts = zip(*sides)
    half_shape = (2,) * len(turn) + (count, model_width)
    far_back = lax.ppermute(back_parts[1], core[0], SWAP)
    far_made = lax.ppermute(made_parts[1], core[0], SWAP)
    far_parts = 1 << len(far_axes)
    straight = parts_near * rows_d == TILE
    d_gates = jnp.stack(d_gate_parts).reshape(experts, 1, count)
    hiddens = [part.reshape(blocks, count, hidden_width) for part in hiddens]
    d_ins = [part.reshape(blocks, count, 2 * hidden_width) for part in d_ins]
    back = [part.reshape(half_shape) for part in (back_parts[0], far_back)]
    d_rows_two, d_gates, part_down, part_in = transfer(
        4,
        [
            ReduceBoth(turn, *back, cluster_parts),
            Direct(core + turn, d_gates, (1, count)),
            WeightGrad(hiddens, [own_grads, far_grads]),
            WeightGrad([own_two, far_two], d_ins, far_parts if straight else 1),
        ],
        (-1, 0, -2),
    )
    d_gates = d_gates.reshape((2,) * len(cluster_axes) + (count,))
    spots = [(core + turn).index(axis) for axis in cluster_axes]
    d_gates = d_gates.transpose(spots + [len(spots)]).reshape(experts, count).T

    reduced = zero_of(d_rows_two).astype(low)

    def to_far(part, rows, done=False):
        stack = part
        if not done:
            stack = part.reshape(parts_c, -1, parts_near, rows, part.shape[1]) + reduced
            stack = stack.transpose(1, 0, 2, 3, 4)
        stack = stack.reshape(-1, team, rows, part.shape[1])
        if not far_axes:
            return stack[0]
        return lax.psum_scatter(stack, far_axes, scatter_dimension=0, tiled=False)

    share_in, share_down = to_far(part_in, rows_d, straight), to_far(part_down, rows_f)

    d_logits = (gates * (d_gates - jnp.sum(gates * d_gates, axis=-1, keepdims=True))).astype(low)
    part_router = dot_tn(normed_two, d_logits)
    d_normed_two = d_rows_two + dot_nt(d_logits, full_router)
    d_resid_one, d_gain_ffn = back_two(d_normed_two)
    d_resid_one = d_resid_one + cotangent[0].astype(jnp.float32)
    wide_part = jnp.pad(part_router.astype(low), ((0, 0), (0, width - experts)))

    made_axes = turn[: len(turn) - len(near_axes)]
    made_shape = (2,) * len(made_axes) + (parts_near * count, model_width)
    made = (made_parts[0].reshape(made_shape), far_made.reshape(made_shape))
    made_spans = [(lo * parts_near, hi * parts_near, order) for lo, hi, order in plane_parts]
    d_branch, made = transfer(
        5,
        [
            Gather(plane_axes, d_resid_one.astype(low), core_last(plane_parts)),
            ReduceBoth(made_axes, *made, made_spans),
        ],
    )
    d_branch = d_branch.reshape(-1, model_width)
    d_mixed = dot_nt(d_branch, w_mix).astype(low).reshape(query_low.shape)
    shapes = [
        jax.ShapeDtypeStruct(query_low.shape, low),
        jax.ShapeDtypeStruct(keyed_low.shape, wide),
        jax.ShapeDtypeStruct(keyed_low.shape, wide),
    ]
    d_query, d_keyed, d_value = attention_call(
        behind_kernel,
        (place, segment),
        (query_low, d_mixed, keyed_low, value_low, keyed_low.transpose(0, 2, 1), log_total),
        ("query", "query", "keys", "keys", "flat", "total"),
        list(zip(("query", "keys", "keys"), shapes)),
        width,
        scale,
        10,
    )
    d_lin, d_one, d_gain_query, d_gain_key, d_gain_attn = row_call(
        functools.partial(unprep_kernel, heads, scale),
        rows,
        (
            d_query.reshape(rows, q_cols),
            d_keyed.reshape(rows, width),
            d_value.reshape(rows, width),
            lin,
            w_qkv,
            cosine,
            sine,
        )
        + head_gains
        + (all_one, gain_attn[None]),
        (4, 7, 8, 10),
        [(qkv_cols, low), (model_width, low)],
        [width, width, model_width],
    )
    d_one = d_one.reshape(plane_shape)
    part_out = weight_grad([mixed_rows], [d_branch]).reshape(q_cols, model_width)
    part_qkv = weight_grad([all_one], [d_lin], parts_c, parts_f)

    turn_back = plane_axes[len(g_axes) : -1] + g_axes
    def over_groups(shape):
        return Gather(g_axes, shape, [(0, shape.shape[0], g_axes)])

    def to_column_owners(shape):
        return Spread(c_axes, g_axes, shape, shape.shape[1:])

    flows = [
        Spread(team_axes, g_axes, share_down, share_down.shape[1:]),
        Spread(team_axes, g_axes, share_in, share_in.shape[1:]),
        Reduce(plane_axes, d_one, core_first([(lo, hi, turn_back) for lo, hi, _ in plane_parts])),
        Reduce(
            f_axes,
            part_qkv.reshape((2,) * len(f_axes) + (parts_c * rows_d, qkv_cols)),
            [(0, parts_c * rows_d, f_axes[::-1])],
            jax.ShapeDtypeStruct((parts_c, rows_d, qkv_cols), low),
            to_column_owners,
        ),
        Reduce(
            own_axes,
            wide_part.reshape((2,) * len(own_axes) + (rows_d, width)),
            [(0, rows_d, own_axes)],
            jax.ShapeDtypeStruct((rows_d, width), low),
            over_groups,
        ),
    ]
    if even:
        rows = q_cols // parts_f
        stack = part_out.reshape((2,) * len(f_axes) + (rows, model_width))
        shape = jax.ShapeDtypeStruct((rows, model_width), low)
        flows.append(Reduce(f_axes, stack, [(0, rows, f_axes[::-1])], shape, over_groups))
    if near_axes:
        near_shape = (2,) * len(near_axes) + (count, model_width)
        near_flow = Reduce(
            near_axes, made.astype(low).reshape(near_shape), [(0, count, near_axes)], by_distance=True
        )
        flows.append(near_flow)
    gains = jnp.concatenate([d_gain_attn[0], d_gain_ffn, d_gain_query[0], d_gain_key[0]])
    lines = -(-gains.size // (8 * width)) * 8
    gains = jnp.pad(gains, (0, lines * width - gains.size)).reshape(lines, width)
    flows.insert(5, Gather(all_axes, gains, [(0, lines, core + all_axes_but_core)]))
    all_down, all_in, d_one, all_qkv, share_router, gains, *rest = transfer(
        7, flows, (2, 0, 1, 2, 3, 7, 6, 4, 5, 3, 3, 6, 6, 4, 5, 3, 4, 5)
    )
    gains = jnp.sum(gains.reshape(-1, lines * width), axis=0)
    share_router = share_router.reshape(groups, rows_d, width)[:, :, :experts]
    grad_router = jnp.sum(share_router.astype(wide), axis=0)
    if near_axes:
        made = rest.pop()
    output = (resid_one + made).astype(low)[None]
    d_resid = back_one(d_one)[0]
    grad_tokens = (d_resid + d_resid_one)[None]
    grad_down, = by_expert(all_down, 1)
    grad_gate, grad_up = by_expert(all_in, 2)
    if even:
        grad_out = rest[0].astype(wide).reshape(rows_o, model_width)
    else:
        stack = jnp.where(jnp.arange(groups)[:, None, None] == g_here, part_out[None], 0)
        share_out = lax.psum_scatter(
            stack.reshape(groups * q_cols, model_width), f_axes, scatter_dimension=0, tiled=True
        )
        grad_out = lax.psum(share_out.astype(wide), g_axes)
    grad_query, grad_key, grad_value = by_head(
        all_qkv.reshape(parts_c, groups, rows_d, qkv_cols), parts_f if even else 1, width
    )
    return (
        output,
        grad_tokens,
        grad_query,
        grad_key,
        grad_value,
        grad_out,
        grad_router,
        grad_gate,
        grad_up,
        grad_down,
        gains[:model_width],
        gains[model_width : 2 * model_width],
        gains[2 * model_width : 2 * model_width + width],
        gains[2 * model_width + width : 2 * model_width + 2 * width],
    )


def solution(mesh):
    def binary(letter, size):
        return tuple(letter + str(step) for step in range(size.bit_length() - 1))

    g_axes = binary("g", mesh.shape["grp"])
    c_axes = binary("c", mesh.shape["ctx"])
    f_axes = binary("f", mesh.shape["fsdp"])
    names = g_axes + c_axes + f_axes
    fine = Mesh(mesh.devices.reshape((2,) * len(names)), names)
    rows = P(g_axes + f_axes, c_axes, None)
    line = P(g_axes + f_axes, None)
    split = P(c_axes + f_axes, None)
    expert = P(None, c_axes + f_axes, None)
    whole = P()
    in_specs = (
        (rows, line, line, rows)
        + (split,) * 5
        + (expert,) * 3
        + (whole,) * 4
        + (rows,)
    )
    out_specs = (rows, rows) + (split,) * 5 + (expert,) * 3 + (whole,) * 4

    def device_part(*arrays):
        return per_device(g_axes, c_axes, f_axes, *arrays)

    return jax.shard_map(
        device_part, mesh=fine, in_specs=in_specs, out_specs=out_specs, check_vma=False
    )
```

```python
import functools
import math

import jax
import jax.numpy as jnp
from jax import lax
from jax.experimental import pallas as pl
from jax.experimental.pallas import tpu as pltpu
from jax.sharding import Mesh
from jax.sharding import PartitionSpec as P

epsilon = 1e-06
low = jnp.bfloat16
wide = jnp.float32
SWAP = [(0, 1), (1, 0)]
ROW_TILE = 16
MIB = 1 << 20
TILE = 256
WAIT_LAST = 8
LONG = 16
BRIEF = pl.CostEstimate(flops=0, bytes_accessed=0, transcendentals=0)


def normed(values, gain):
    return values * lax.rsqrt(jnp.mean(values * values, axis=-1, keepdims=True) + epsilon) * gain


def dot(left, right):
    return jnp.dot(left, right, preferred_element_type=jnp.float32)


def dot_nt(left, right):
    return lax.dot_general(left, right, (((1,), (1,)), ((), ())), preferred_element_type=jnp.float32)


def dot_tn(left, right):
    return lax.dot_general(left, right, (((0,), (0,)), ((), ())), preferred_element_type=jnp.float32)


def zero_of(anchor):
    return jnp.minimum(jnp.abs(anchor[(0,) * anchor.ndim].astype(wide)), 0.0)


def flat_index(axes):
    index = 0
    for axis in axes:
        index = index * 2 + lax.axis_index(axis)
    return index


def take(stack, index):
    return lax.dynamic_index_in_dim(stack, index, 0, keepdims=False)


def take_at(stack, index, at):
    return lax.dynamic_index_in_dim(stack, index, at, keepdims=False)


def sems(amount):
    return pltpu.SemaphoreType.DMA((amount,))


def toward(flips):
    return {axis: 1 - lax.axis_index(axis) for axis in flips}


def remote(src, dst, send, recv, flips):
    return pltpu.make_async_remote_copy(
        src_ref=src,
        dst_ref=dst,
        send_sem=send,
        recv_sem=recv,
        device_id=toward(flips),
        device_id_type=pl.DeviceIdType.MESH,
    )


class Direct:
    def __init__(self, axes, operand, block, pick=None, rounds=0):
        self.axes, self.block, self.pick, self.rounds = axes, block, pick, rounds
        self.amount = 1 << len(axes)
        self.operands = [operand]
        self.results = [jax.ShapeDtypeStruct((self.amount,) + block, operand.dtype)]
        self.scratch = [
            sems(self.amount),
            sems(self.amount),
            sems(2),
            pltpu.VMEM(block, operand.dtype),
        ]
        self.steps = [
            tuple(axis for bit, axis in enumerate(reversed(axes)) if step >> bit & 1)
            for step in range(self.amount)
        ]
        self.flips = self.steps[1:]

    def begin(self, operands, target, send, recv):
        copies = []
        for step in range(1, self.amount):
            other = 0
            for axis in self.axes:
                place = lax.axis_index(axis)
                other = other * 2 + (1 - place if axis in self.steps[step] else place)
            copy = remote(
                operands[0].at[step if self.pick is None else self.pick(other)],
                target,
                send.at[step],
                recv.at[step],
                self.steps[step],
            )
            copy.start()
            copies.append(copy)
        return copies

    def keep(self, operands, target, local, held):
        own = 0 if self.pick is None else self.pick(flat_index(self.axes))
        load = pltpu.make_async_copy(operands[0].at[own], held, local.at[0])
        load.start()
        load.wait()
        store = pltpu.make_async_copy(held, target, local.at[1])
        store.start()
        store.wait()

    def run(self, operands, results, scratch):
        send, recv, local, held = scratch
        for _ in range(self.rounds):
            yield
        target = results[0].at[flat_index(self.axes)]
        copies = self.begin(operands, target, send, recv)
        self.keep(operands, target, local, held)
        for _ in range(WAIT_LAST):
            yield
        for copy in copies:
            copy.wait()


class Spread(Direct):
    def __init__(self, axes, others, operand, block, pick=lambda place: place):
        super().__init__(axes, operand, block, pick)
        self.others = others
        self.results = [
            jax.ShapeDtypeStruct((self.amount,) + (2,) * len(others) + block, operand.dtype)
        ]
        self.scratch += [sems(max(1, len(others))), sems(max(1, len(others)))]
        self.flips = self.flips + [(axis,) for axis in others]

    def run(self, operands, results, scratch):
        send, recv, local, held, next_send, next_recv = scratch
        here = flat_index(self.axes)
        place = {axis: lax.axis_index(axis) for axis in self.others}
        spot = tuple(place[axis] for axis in self.others)
        copies = self.begin(operands, results[0].at[(here,) + spot], send, recv)
        self.keep(operands, results[0].at[(here,) + spot], local, held)
        yield
        for copy in copies:
            copy.wait_recv()
        for stage, axis in enumerate(self.others):
            region = tuple(
                slice(None) if other in self.others[:stage] else place[other]
                for other in self.others
            )
            region = results[0].at[(slice(None),) + region]
            copy = remote(region, region, next_send.at[stage], next_recv.at[stage], (axis,))
            copy.start()
            yield
            copy.wait()
        for copy in copies:
            copy.wait_send()


class Gather:
    def __init__(self, axes, operand, parts):
        self.axes, self.parts = axes, parts
        self.operands = [operand]
        self.results = [
            jax.ShapeDtypeStruct((2,) * len(axes) + operand.shape, operand.dtype)
        ]
        amount = len(parts) * len(axes)
        self.scratch = [sems(amount), sems(amount), sems(2), pltpu.VMEM(operand.shape, operand.dtype)]
        self.flips = [(axis,) for axis in axes]

    def run(self, operands, results, scratch):
        send, recv, local, held = scratch
        place = {axis: lax.axis_index(axis) for axis in self.axes}
        load = pltpu.make_async_copy(operands[0], held, local.at[0])
        load.start()
        load.wait()
        spot = tuple(place[axis] for axis in self.axes)
        store = pltpu.make_async_copy(held, results[0].at[spot], local.at[1])
        store.start()
        store.wait()
        copies = {}

        def start(number, stage):
            lo, hi, order = self.parts[number]
            region = tuple(
                slice(None) if axis in order[:stage] else place[axis] for axis in self.axes
            )
            region = results[0].at[region + (pl.ds(lo, hi - lo),)]
            slot = number * len(self.axes) + stage
            copies[number, stage] = remote(
                region, region, send.at[slot], recv.at[slot], (order[stage],)
            )
            copies[number, stage].start()

        for number in range(len(self.parts)):
            start(number, 0)
        yield
        for stage in range(1, len(self.axes)):
            for number in range(len(self.parts)):
                copies[number, stage - 1].wait_recv()
                start(number, stage)
            yield
        for number in range(len(self.parts)):
            copies[number, len(self.axes) - 1].wait_recv()
        for copy in copies.values():
            copy.wait_send()


class Reduce:
    def __init__(self, axes, operand, parts, ready=None, last=None, by_distance=False):
        self.axes, self.parts, self.by_distance = axes, parts, by_distance
        count, columns = operand.shape[-2:]
        self.operands = [operand]
        self.results = [jax.ShapeDtypeStruct((count, columns), wide)]
        self.scratch = []
        for lo, hi, order in parts:
            for stage in range(len(axes)):
                left = len(axes) - 1 - stage
                self.scratch.append(pltpu.VMEM((2,) * left + (hi - lo, columns), low))
            self.scratch.append(pltpu.VMEM((2,) * (len(axes) - 1) + (hi - lo, columns), low))
        self.scratch.append(pltpu.VMEM((count, columns), wide))
        amount = len(parts) * len(axes)
        self.flips = [(axis,) for axis in axes]
        self.last = None
        if last is not None:
            self.last = last(ready)
            self.results = self.last.results
            self.flips = self.flips + self.last.flips
            self.scratch += [pltpu.VMEM(ready.shape, low)] + self.last.scratch
        self.scratch += [sems(amount), sems(amount), sems(len(parts) + 1)]

    def run(self, operands, results, scratch):
        stages = len(self.axes)
        send, recv, local = scratch[-3:]
        total = scratch[len(self.parts) * (stages + 1)]
        place = {axis: 0 if self.by_distance else lax.axis_index(axis) for axis in self.axes}
        copies, loads = {}, []

        def buffers(number):
            base = number * (stages + 1)
            return scratch[base : base + stages], scratch[base + stages]

        def start(number, stage):
            lo, hi, order = self.parts[number]
            slots, held = buffers(number)
            slot = number * stages + stage
            axis = order[stage]
            if stage == 0:
                spot = tuple(
                    1 - place[other] if other == axis else slice(None) for other in self.axes
                )
                source = operands[0].at[spot + (pl.ds(lo, hi - lo),)]
            else:
                rest = [other for other in self.axes if other != order[0]]
                spot = tuple(
                    place[other]
                    if other in order[:stage]
                    else 1 - place[other]
                    if other == axis
                    else slice(None)
                    for other in rest
                )
                source = held.at[spot]
            copies[number, stage] = remote(
                source, slots[stage], send.at[slot], recv.at[slot], (axis,)
            )
            copies[number, stage].start()

        for number, (lo, hi, order) in enumerate(self.parts):
            start(number, 0)
            spot = tuple(
                place[other] if other == order[0] else slice(None) for other in self.axes
            )
            load = pltpu.make_async_copy(
                operands[0].at[spot + (pl.ds(lo, hi - lo),)], buffers(number)[1], local.at[number]
            )
            load.start()
            loads.append(load)
        yield
        for stage in range(stages):
            for number, (lo, hi, order) in enumerate(self.parts):
                slots, held = buffers(number)
                if stage == 0:
                    loads[number].wait()
                copies[number, stage].wait_recv()
                rest = [other for other in self.axes if other != order[0]]
                gone = order[: stage + 1]
                free = [other for other in rest if other not in gone]
                for code in range(1 << len(free)):
                    bits = {axis: code >> bit & 1 for bit, axis in enumerate(free)}
                    spot = tuple(bits[axis] if axis in bits else place[axis] for axis in rest)
                    slot_spot = tuple(bits[axis] for axis in free)
                    last = stage == stages - 1

                    def add(step, carry, spot=spot, slot_spot=slot_spot, last=last):
                        rows = pl.ds(pl.multiple_of(step * ROW_TILE, ROW_TILE), ROW_TILE)
                        value = held[spot + (rows,)].astype(wide)
                        value = value + slots[stage][slot_spot + (rows,)].astype(wide)
                        if last:
                            at = pl.multiple_of(step * ROW_TILE + lo, ROW_TILE)
                            total[pl.ds(at, ROW_TILE)] = value
                        else:
                            held[spot + (rows,)] = value.astype(low)
                        return carry

                    lax.fori_loop(0, (hi - lo) // ROW_TILE, add, 0)
                if stage + 1 < stages:
                    start(number, stage + 1)
            yield
        if self.last is None:
            store = pltpu.make_async_copy(total, results[0], local.at[len(self.parts)])
            store.start()
            store.wait()
        else:
            ready, *others = scratch[len(self.parts) * (stages + 1) + 1 : -3]
            ready[...] = total[...].astype(low).reshape(ready.shape)
            yield from self.last.run([ready], results, others)
        for copy in copies.values():
            copy.wait_send()


class ReduceBoth(Reduce):
    def __init__(self, axes, operand, other, parts, first=()):
        super().__init__(axes, operand, parts, by_distance=True)
        self.first = first
        self.flips = self.flips + [(axis,) for axis in first]
        self.operands = [operand, other]
        shape = operand.shape
        self.scratch = [pltpu.VMEM(shape, low), pltpu.VMEM(shape, low)]
        for lo, hi, order in parts:
            for stage in range(len(axes)):
                left = len(axes) - 1 - stage
                self.scratch.append(pltpu.VMEM((2,) * left + (hi - lo, shape[-1]), low))
        self.scratch.append(pltpu.VMEM(shape[-2:], wide))
        amount = len(parts) * len(axes)
        self.scratch += [sems(amount), sems(amount), sems(2 * len(parts) + 1), sems(len(parts))]

    def run(self, operands, results, scratch):
        stages = len(self.axes)
        held, added, *slots = scratch[:-5]
        total, send, recv, local, far = scratch[-5:]
        copies, loads = {}, []
        every = (slice(None),) * stages

        def start(number, stage):
            lo, hi, order = self.parts[number]
            spot = tuple(
                0 if axis in order[:stage] else 1 if axis == order[stage] else slice(None)
                for axis in self.axes
            )
            slot = number * stages + stage
            copies[number, stage] = remote(
                held.at[spot + (pl.ds(lo, hi - lo),)],
                slots[slot],
                send.at[slot],
                recv.at[slot],
                (order[stage],),
            )
            copies[number, stage].start()

        def add_all(lo, hi, free, spot_of, source, last):
            for code in range(1 << len(free)):
                bits = {axis: code >> bit & 1 for bit, axis in enumerate(free)}
                spot = tuple(bits.get(axis, 0) for axis in self.axes)
                source_spot = spot_of(bits)

                def add(step, carry, spot=spot, source_spot=source_spot):
                    at = pl.multiple_of(step * ROW_TILE, ROW_TILE)
                    rows = pl.ds(pl.multiple_of(at + lo, ROW_TILE), ROW_TILE)
                    value = held[spot + (rows,)].astype(wide)
                    shift = rows if source is added else pl.ds(at, ROW_TILE)
                    value = value + source[source_spot + (shift,)].astype(wide)
                    if last:
                        total[rows] = value
                    else:
                        held[spot + (rows,)] = value.astype(low)
                    return carry

                lax.fori_loop(0, (hi - lo) // ROW_TILE, add, 0)

        for number, (lo, hi, order) in enumerate(self.parts):
            span = every + (pl.ds(lo, hi - lo),)
            for which, (operand, buffer) in enumerate(zip(operands, (held, added))):
                if which and self.first:
                    load = remote(
                        operand.at[span],
                        added.at[span],
                        far.at[number],
                        local.at[2 * number + which],
                        self.first,
                    )
                else:
                    load = pltpu.make_async_copy(
                        operand.at[span], buffer.at[span], local.at[2 * number + which]
                    )
                load.start()
                loads.append(load)
        if self.first:
            yield
        for number, (lo, hi, order) in enumerate(self.parts):
            loads[2 * number].wait()
            loads[2 * number + 1].wait()
            add_all(
                lo, hi, self.axes, lambda bits: tuple(bits[axis] for axis in self.axes), added, False
            )
            start(number, 0)
        yield
        for stage in range(stages):
            for number, (lo, hi, order) in enumerate(self.parts):
                copies[number, stage].wait_recv()
                free = [axis for axis in self.axes if axis not in order[: stage + 1]]
                add_all(
                    lo,
                    hi,
                    free,
                    lambda bits, free=free: tuple(bits[axis] for axis in free),
                    slots[number * stages + stage],
                    stage == stages - 1,
                )
                if stage + 1 < stages:
                    start(number, stage + 1)
            yield
        store = pltpu.make_async_copy(total, results[0], local.at[2 * len(self.parts)])
        store.start()
        store.wait()
        for copy in copies.values():
            copy.wait_send()


class Later:
    def __init__(self, flow):
        self.flow, self.flips = flow, flow.flips
        self.operands, self.results, self.scratch = flow.operands, flow.results, flow.scratch

    def run(self, *parts):
        yield
        yield from self.flow.run(*parts)


class Fed(Later):
    def __init__(self, flow, source):
        super().__init__(flow)
        self.source, self.operands = source, []

    def run(self, operands, results, scratch):
        yield
        yield from self.flow.run([self.source()], results, scratch)


class PairSum:
    def __init__(self, axis, task, groups, rows):
        self.axis, self.task, self.groups, self.rows = axis, task, groups, rows
        shape = (groups, rows, task.width)
        self.operands, self.flips = [], [(axis,)]
        self.results = [jax.ShapeDtypeStruct(shape, low)]
        self.scratch = [pltpu.VMEM(shape, low), pltpu.VMEM(shape, low)]
        self.scratch += [sems(groups), sems(groups), sems(groups + 1)]

    def run(self, operands, results, scratch):
        held, added, send, recv, local = scratch
        source, place = self.task.refs[1][0], lax.axis_index(self.axis)
        yield

        def part(group, whose):
            at = pl.multiple_of((group * 2 + whose) * self.rows, self.rows)
            return source.at[pl.ds(at, self.rows)]

        copies = []
        for group in range(self.groups):
            copy = remote(
                part(group, 1 - place), added.at[group], send.at[group], recv.at[group], (self.axis,)
            )
            load = pltpu.make_async_copy(part(group, place), held.at[group], local.at[group])
            copy.start()
            load.start()
            copies += [copy, load]
        yield
        for copy in copies:
            copy.wait()
        for group in range(self.groups):

            def add(step, carry, group=group):
                at = pl.ds(pl.multiple_of(step * ROW_TILE, ROW_TILE), ROW_TILE)
                value = held[group, at].astype(wide) + added[group, at].astype(wide)
                held[group, at] = value.astype(low)
                return carry

            lax.fori_loop(0, self.rows // ROW_TILE, add, 0)
        store = pltpu.make_async_copy(held, results[0], local.at[self.groups])
        store.start()
        store.wait()


class Task:
    flips = ()


class WeightGrad(Task):
    def __init__(self, lefts, rights, turns=1, pieces=1, source=None, out=None, room=None):
        self.amount, self.turns, self.pieces, self.calls = len(lefts), turns, pieces, 0
        self.source, self.room = source, room
        self.operands = list(lefts) + (list(rights) if source is None else [])
        self.blocks, self.rows, self.columns = lefts[0].shape
        self.width = rights[0].shape[-1]
        self.out = out or ((self.columns, self.width), (TILE, self.width), self.place)
        self.results = [jax.ShapeDtypeStruct(self.out[0], low)]
        shape = (self.amount, self.blocks, self.rows, self.width)
        self.scratch = [sems(self.amount)] + ([] if room else [pltpu.VMEM(shape, low)])

    def run(self, operands, results, scratch):
        done = scratch[0]
        held = self.room.refs[2][1] if self.room else scratch[1]
        span = slice(0, self.width)
        if self.calls == 0:
            rights = operands[self.amount :] if self.source is None else [self.source()]
            copies = [
                pltpu.make_async_copy(
                    right, held.at[number, :, :, pl.ds(0, self.width)], done.at[number]
                )
                for number, right in enumerate(rights)
            ]
            for copy in copies:
                copy.start()
            for copy in copies:
                copy.wait()
        share = self.columns // TILE // self.pieces
        first = self.calls * share
        self.calls = (self.calls + 1) % self.pieces

        def body(*refs):
            total = 0.0
            for number, left_ref in enumerate(refs[:-1]):
                right = held[number, :, :, span].reshape(-1, self.width)
                total = total + dot_tn(left_ref[...].reshape(-1, TILE), right)
            refs[-1][...] = total.astype(low).reshape(refs[-1].shape)

        block = pl.BlockSpec((self.blocks, self.rows, TILE), lambda step: (0, 0, step + first))
        pltpu.emit_pipeline(
            body,
            grid=(share,),
            in_specs=[block] * self.amount,
            out_specs=[pl.BlockSpec(self.out[1], lambda step: self.out[2](step + first))],
        )(*operands[: self.amount], results[0])

    def place(self, step):
        steps = self.columns // TILE
        return (step % self.turns * (steps // self.turns) + step // self.turns, 0)


class HeadsBack(Task):
    def __init__(self, heads, scale, tiled, w_qkv, gains, ffn_lines, axes):
        self.heads, self.scale, self.axes = heads, scale, axes
        self.operands = list(tiled) + [w_qkv, ffn_lines] + list(gains)
        self.tiled = len(tiled)
        self.rows, self.width = tiled[1].shape
        self.model_width, self.columns = w_qkv.shape
        self.blocks = 1 << len(axes)
        self.tile = self.rows // self.blocks
        self.results = [
            jax.ShapeDtypeStruct((self.blocks, self.tile, self.columns), low),
            jax.ShapeDtypeStruct((2,) * len(axes) + (self.tile, self.model_width), low),
        ]
        own, ffn = self.model_width // self.width, ffn_lines.shape[0]
        self.lines = -(-(own + ffn + 2) // 8) * 8
        row = pltpu.VMEM((1, self.width), wide)
        long_row = pltpu.VMEM((1, self.model_width), wide)
        self.scratch = [pltpu.VMEM((self.lines, self.width), wide), pltpu.VMEM(w_qkv.shape, low)]
        self.scratch += [row, row, long_row, row, row, long_row, sems(5)]

    def run(self, operands, results, scratch):
        lines, w_ref, gain_q, gain_k, gain, d_gain_q, d_gain_k, d_gain, done = scratch
        w_hbm, ffn, *gains = operands[self.tiled :]
        own, count = self.model_width // self.width, ffn.shape[0]
        lines[...] = jnp.zeros_like(lines)
        targets = [w_ref, lines.at[pl.ds(own, count)], gain_q, gain_k, gain]
        copies = [
            pltpu.make_async_copy(source, target, done.at[number])
            for number, (source, target) in enumerate(zip([w_hbm, ffn] + gains, targets))
        ]
        for copy in copies:
            copy.start()
        for copy in copies:
            copy.wait()
        for total in (d_gain_q, d_gain_k, d_gain):
            total[...] = jnp.zeros_like(total)

        def body(
            d_query_ref,
            d_keyed_ref,
            d_value_ref,
            lin_ref,
            cosine_ref,
            sine_ref,
            rows_ref,
            d_lin_ref,
            d_one_ref,
        ):
            cosine, sine = cosine_ref[...], sine_ref[...]
            for head in range(self.heads + 1):
                span = slice(head * self.width, (head + 1) * self.width)
                values = lin_ref[:, span]
                if head < self.heads:
                    grads, own_gain, d_head = d_query_ref[:, span].astype(wide), gain_q, d_gain_q
                else:
                    grads, own_gain, d_head = d_keyed_ref[...] * self.scale, gain_k, d_gain_k
                grads = turned_back(grads, cosine, sine)
                factor = head_scale(values)
                plain = values * factor
                d_head[...] += jnp.sum(grads * plain, axis=0, keepdims=True)
                grads = grads * own_gain[...]
                mean = jnp.mean(grads * plain, axis=1, keepdims=True)
                d_lin_ref[:, span] = (factor * (grads - plain * mean)).astype(low)
            d_lin_ref[:, (self.heads + 1) * self.width :] = d_value_ref[...].astype(low)
            d_one = dot_nt(d_lin_ref[...], w_ref[...])
            d_one_ref[...] = d_one.astype(low)
            share = jnp.sum(d_one * rows_ref[...].astype(wide), axis=0, keepdims=True)
            d_gain[...] += share / gain[...]

        def by_bits(step):
            bits = [step // (self.blocks >> (bit + 1)) % 2 for bit in range(len(self.axes))]
            return tuple(bits) + (0, 0)

        pltpu.emit_pipeline(
            body,
            grid=(self.blocks,),
            in_specs=[
                pl.BlockSpec((self.tile, array.shape[1]), lambda step: (step, 0))
                for array in operands[: self.tiled]
            ],
            out_specs=[
                pl.BlockSpec((None, self.tile, self.columns), lambda step: (step, 0, 0)),
                pl.BlockSpec((None,) * len(self.axes) + (self.tile, self.model_width), by_bits),
            ],
        )(*operands[: self.tiled], *results)
        for line in range(own):
            lines[line : line + 1] = d_gain[:, line * self.width : (line + 1) * self.width]
        lines[own + count : own + count + 1] = d_gain_q[...]
        lines[own + count + 1 : own + count + 2] = d_gain_k[...]


def flow_kernel(flows, plan, *refs):
    refs = list(refs)

    def cut(amount):
        part = refs[:amount]
        del refs[:amount]
        return part

    operands = [cut(len(flow.operands)) for flow in flows]
    results = [cut(len(flow.results)) for flow in flows]
    scratch = [cut(len(flow.scratch)) for flow in flows]
    partners = []
    for flow in flows:
        partners += [flips for flips in flow.flips if flips not in partners]
    barrier = pltpu.get_barrier_semaphore()
    for flips in partners:
        pl.semaphore_signal(
            barrier, inc=1, device_id=toward(flips), device_id_type=pl.DeviceIdType.MESH
        )
    pl.semaphore_wait(barrier, len(partners))
    for flow, *parts in zip(flows, operands, results, scratch):
        flow.refs = parts
    tasks = [part for part in zip(flows, operands, results, scratch) if isinstance(part[0], Task)]
    runs = [
        flow.run(*parts)
        for flow, *parts in zip(flows, operands, results, scratch)
        if not isinstance(flow, Task)
    ]
    for run in runs:
        next(run)
    for number in plan:
        if number < 0:
            flow, *parts = tasks[-1 - number]
            flow.run(*parts)
        elif number < len(runs):
            next(runs[number], None)
    while runs:
        runs = [run for run in runs if next(run, run) is not run]


def transfer(number, flows, plan=()):
    arrays = [array for flow in flows for array in flow.operands]
    shapes = [shape for flow in flows for shape in flow.results]
    anywhere = pl.BlockSpec(memory_space=pl.ANY)
    return pl.pallas_call(
        functools.partial(flow_kernel, flows, plan),
        out_shape=shapes,
        in_specs=[anywhere] * len(arrays),
        out_specs=[anywhere] * len(shapes),
        scratch_shapes=[one for flow in flows for one in flow.scratch],
        compiler_params=pltpu.CompilerParams(
            collective_id=number, has_side_effects=True, vmem_limit_bytes=60 * MIB
        ),
        cost_estimate=BRIEF,
    )(*arrays)


def tile_of(rows, most):
    steps = -(-rows // most)
    while rows % steps or (rows // steps) % ROW_TILE:
        steps += 1
    return rows // steps


def whole_block(shape):
    return pl.BlockSpec(shape, lambda *ids: (0,) * len(shape), pipeline_mode=pl.Buffered(1))


def expert_kernel(
    near,
    ids_ref,
    rows_ref,
    grad_ref,
    gate_ref,
    pieces_gate,
    pieces_up,
    pieces_down,
    hidden_ref,
    d_in_ref,
    d_gate_ref,
    made_ref,
    back_ref,
    in_ref,
    down_ref,
    done,
):
    @pl.when(pl.program_id(0) == 0)
    def _():
        copies = []
        half = pieces_gate.shape[3]
        for pieces, held, lo in (
            (pieces_gate, in_ref, 0),
            (pieces_up, in_ref, half),
            (pieces_down, down_ref, 0),
        ):
            amount, parts, rows, columns = pieces.shape
            for spot in range(amount):
                for part in range(parts):
                    block = (part // near * amount + spot) * near + part % near
                    copy = pltpu.make_async_copy(
                        pieces.at[spot, part],
                        held.at[pl.ds(block * rows, rows), pl.ds(lo, columns)],
                        done.at[len(copies)],
                    )
                    copy.start()
                    copies.append(copy)
        for copy in copies:
            copy.wait()

    hidden_width = down_ref.shape[0]
    gate = gate_ref[...]
    acts = dot(rows_ref[...], in_ref[...])
    d_plain = dot_nt(grad_ref[...], down_ref[...])
    act_gate, act_up = acts[:, :hidden_width], acts[:, hidden_width:]
    sigmoid = 1.0 / (1.0 + jnp.exp(-act_gate))
    silu_gate = act_gate * sigmoid
    hidden = silu_gate * act_up
    d_gate_ref[...] = jnp.sum(hidden * d_plain, axis=1, keepdims=True)
    d_hidden = d_plain * gate
    hidden_low = (hidden * gate).astype(low)
    d_act_gate = d_hidden * act_up * (sigmoid * (1.0 + act_gate * (1.0 - sigmoid)))
    d_in = jnp.concatenate([d_act_gate.astype(low), (d_hidden * silu_gate).astype(low)], axis=1)
    hidden_ref[...] = hidden_low
    d_in_ref[...] = d_in
    back_ref[...] = dot_nt(d_in, in_ref[...]).astype(low)
    made_ref[...] = dot(hidden_low, down_ref[...]).astype(low)


def expert_rows(rows, grad_rows, gate, pieces, near, ids):
    blocks, tile, model_width = rows.shape
    amount = blocks * tile
    hidden_width = pieces[0].shape[3]

    block = pl.BlockSpec((None, tile, model_width), lambda step, ids: (ids[step], 0, 0))

    def by_place(columns):
        return pl.BlockSpec((tile, columns), lambda step, ids: (ids[step], 0))

    def by_distance(columns):
        return pl.BlockSpec((tile, columns), lambda step, ids: (step, 0))

    outs = [
        (by_place, hidden_width, low),
        (by_place, 2 * hidden_width, low),
        (by_distance, 1, wide),
        (by_distance, model_width, low),
        (by_distance, model_width, low),
    ]
    anywhere = pl.BlockSpec(memory_space=pl.ANY)
    return pl.pallas_call(
        functools.partial(expert_kernel, near),
        grid_spec=pltpu.PrefetchScalarGridSpec(
            num_scalar_prefetch=1,
            grid=(blocks,),
            in_specs=[block, block, by_place(1)]
            + [anywhere] * len(pieces),
            out_specs=[spec(columns) for spec, columns, _ in outs],
            scratch_shapes=[
                pltpu.VMEM((model_width, 2 * hidden_width), low),
                pltpu.VMEM((hidden_width, model_width), low),
                sems(sum(piece.shape[0] * piece.shape[1] for piece in pieces)),
            ],
        ),
        out_shape=[jax.ShapeDtypeStruct((amount, columns), kind) for _, columns, kind in outs],
        compiler_params=pltpu.CompilerParams(vmem_limit_bytes=52 * MIB),
        cost_estimate=pl.CostEstimate(
            flops=LONG * 18 * amount * model_width * hidden_width,
            bytes_accessed=14 * amount * model_width,
            transcendentals=0,
        ),
    )(ids, rows, grad_rows, gate, *pieces)


def weight_kernel(amount, *refs):
    total = 0.0
    for left, right in zip(refs[:amount], refs[amount:-1]):
        total = total + dot_tn(left[...], right[...])
    refs[-1][...] = total.astype(low).reshape(refs[-1].shape)


def weight_grad(lefts, rights, groups=1, parts=1, tile=256):
    amount = len(lefts)
    columns, out_columns = lefts[0].shape[1], rights[0].shape[1]
    piece = columns // (groups * parts)
    tile = min(tile, piece * parts)
    if tile < piece:
        groups, parts, piece = columns // tile, 1, tile
    runs = piece * parts // tile
    return pl.pallas_call(
        functools.partial(weight_kernel, amount),
        grid=(columns // tile,),
        in_specs=[pl.BlockSpec((left.shape[0], tile), lambda step: (0, step)) for left in lefts]
        + [whole_block(right.shape) for right in rights],
        out_specs=pl.BlockSpec(
            (tile // piece, 1, piece, out_columns), lambda step: (step % runs, step // runs, 0, 0)
        ),
        out_shape=jax.ShapeDtypeStruct((parts, groups, piece, out_columns), low),
        compiler_params=pltpu.CompilerParams(vmem_limit_bytes=52 * MIB),
        cost_estimate=BRIEF,
    )(*lefts, *rights)


def widen_kernel(pieces_ref, *out_refs):
    columns = out_refs[0].shape[2]
    for number, out_ref in enumerate(out_refs):
        span = slice(number * columns, (number + 1) * columns)
        out_ref[...] = pieces_ref[:, :, span].astype(wide)


def widen_heads_kernel(parts, piece_ref, query_ref, key_ref, value_ref):
    groups, width = piece_ref.shape[0], key_ref.shape[1]
    columns = piece_ref.shape[2] - 2 * width
    piece = columns // parts
    for part in range(parts):
        for group in range(groups):
            at = (part * groups + group) * piece
            span = slice(part * piece, (part + 1) * piece)
            query_ref[:, at : at + piece] = piece_ref[group, :, span].astype(wide)
    for number, out_ref in enumerate((key_ref, value_ref)):
        span = slice(columns + number * width, columns + (number + 1) * width)
        total = piece_ref[0, :, span].astype(wide)
        for group in range(1, groups):
            total = total + piece_ref[group, :, span].astype(wide)
        out_ref[...] = total


def by_head(pieces, parts, width):
    owners, groups, rows, columns = pieces.shape
    spans = [groups * (columns - 2 * width), width, width]
    return pl.pallas_call(
        functools.partial(widen_heads_kernel, parts),
        grid=(owners,),
        in_specs=[pl.BlockSpec((None, groups, rows, columns), lambda step: (step, 0, 0, 0))],
        out_specs=[pl.BlockSpec((rows, span), lambda step: (0, step)) for span in spans],
        out_shape=[jax.ShapeDtypeStruct((rows, owners * span), wide) for span in spans],
        cost_estimate=BRIEF,
    )(pieces)


def by_expert(pieces, amount):
    team, rows, columns = pieces.shape[0], pieces.shape[-2], pieces.shape[-1]
    pieces = pieces.reshape(team, -1, rows, columns)
    groups = pieces.shape[1]
    out = (groups * team, rows, columns // amount)
    return pl.pallas_call(
        widen_kernel,
        grid=(groups, team // 4),
        in_specs=[pl.BlockSpec((4, None, rows, columns), lambda group, place: (place, group, 0, 0))],
        out_specs=[
            pl.BlockSpec((4,) + out[1:], lambda group, place: (group * (team // 4) + place, 0, 0))
        ]
        * amount,
        out_shape=[jax.ShapeDtypeStruct(out, wide)] * amount,
        cost_estimate=BRIEF,
    )(pieces)


def turned(values, cosine, sine):
    return values * cosine + pltpu.roll(values, values.shape[1] // 2, 1) * sine


def turned_back(grads, cosine, sine):
    return grads * cosine + pltpu.roll(grads * sine, grads.shape[1] // 2, 1)


def head_scale(values):
    return lax.rsqrt(jnp.mean(values * values, axis=1, keepdims=True) + epsilon)


def prep_kernel(
    heads,
    rows_ref,
    w_ref,
    place_ref,
    inverse_ref,
    sign_ref,
    gain_q,
    gain_k,
    lin_ref,
    query_ref,
    keyed_ref,
    value_ref,
    cosine_ref,
    sine_ref,
):
    width = gain_q.shape[1]
    angle = place_ref[...].astype(wide) * inverse_ref[...]
    cosine, sine = jnp.cos(angle), jnp.sin(angle) * sign_ref[...]
    cosine_ref[...] = cosine
    sine_ref[...] = sine
    lin = dot(rows_ref[...], w_ref[...])
    lin_ref[...] = lin[:, : (heads + 1) * width]
    for head in range(heads + 1):
        span = slice(head * width, (head + 1) * width)
        values = lin[:, span]
        gain = gain_q[...] if head < heads else gain_k[...]
        made = turned(values * head_scale(values) * gain, cosine, sine).astype(low)
        if head < heads:
            query_ref[:, span] = made
        else:
            keyed_ref[...] = made
    value_ref[...] = lin[:, (heads + 1) * width :].astype(low)


def row_call(kernel, rows, tiled, fixed, outs, sums):
    tile = tile_of(rows, 256)

    def by_rows(columns):
        return pl.BlockSpec((tile, columns), lambda step: (step, 0))

    return pl.pallas_call(
        kernel,
        grid=(rows // tile,),
        in_specs=[
            whole_block(array.shape) if number in fixed else by_rows(array.shape[1])
            for number, array in enumerate(tiled)
        ],
        out_specs=[by_rows(columns) for columns, _ in outs]
        + [pl.BlockSpec((1, columns), lambda step: (0, 0)) for columns in sums],
        out_shape=[jax.ShapeDtypeStruct((rows, columns), kind) for columns, kind in outs]
        + [jax.ShapeDtypeStruct((1, columns), wide) for columns in sums],
        compiler_params=pltpu.CompilerParams(vmem_limit_bytes=48 * MIB),
        cost_estimate=BRIEF,
    )(*tiled)


def mask_tile(bias, k_place, k_segment, q_place, q_segment):
    allowed = (k_segment[...] == q_segment[0]) & (k_place[...] <= q_place[0])
    bias[...] = jnp.where(allowed, 0.0, -1e30)


def ahead_kernel(
    scale, k_place, k_segment, q_place, q_segment, q_ref, k_ref, vt_ref, mixed_ref, total_ref, bias
):
    @pl.when(pl.program_id(2) == 0)
    def _():
        mask_tile(bias, k_place.at[0], k_segment.at[0], q_place, q_segment)

    scores = dot_nt(k_ref[0], q_ref[0]) * scale + bias[...]
    row_max = jnp.max(scores, axis=0, keepdims=True)
    expd = jnp.exp(scores - row_max)
    row_total = jnp.sum(expd, axis=0, keepdims=True)
    mixed = dot(vt_ref[0], expd.astype(low)) / row_total
    mixed_ref[0] = mixed.T.astype(low)
    total_ref[0, 0] = row_max + jnp.log(row_total)


def behind_kernel(
    scale,
    k_place,
    k_segment,
    q_place,
    q_segment,
    q_ref,
    d_mixed_ref,
    k_ref,
    v_ref,
    kt_ref,
    total_ref,
    d_q_ref,
    d_k_ref,
    d_v_ref,
    bias,
):
    @pl.when(pl.program_id(2) == 0)
    def _():
        mask_tile(bias, k_place.at[0], k_segment.at[0], q_place, q_segment)

    @pl.when((pl.program_id(1) == 0) & (pl.program_id(2) == 0))
    def _():
        d_k_ref[...] = jnp.zeros_like(d_k_ref)
        d_v_ref[...] = jnp.zeros_like(d_v_ref)

    query, d_mixed = q_ref[0], d_mixed_ref[0]
    probs = jnp.exp(dot_nt(k_ref[0], query) * scale + bias[...] - total_ref[0, 0])
    d_probs = dot_nt(v_ref[0], d_mixed)
    row_dot = jnp.sum(probs * d_probs, axis=0, keepdims=True)
    d_scores = (probs * (d_probs - row_dot)).astype(low)
    d_v_ref[0] += dot(probs.astype(low), d_mixed)
    d_k_ref[0] += dot(d_scores, query)
    d_q_ref[0] = (dot(kt_ref[0], d_scores) * scale).T.astype(low)


def attention_call(kernel, marks, arrays, kinds, outs, width, scale, work):
    place, segment = marks
    seqs, length = place.shape
    tile = min(256, length)
    heads = arrays[0].shape[2] // width
    specs = {
        "query": pl.BlockSpec((1, tile, width), lambda s, i, h: (s, i, h)),
        "keys": pl.BlockSpec((1, length, width), lambda s, i, h: (s, 0, 0)),
        "flat": pl.BlockSpec((1, width, length), lambda s, i, h: (s, 0, 0)),
        "total": pl.BlockSpec((1, 1, 1, tile), lambda s, i, h: (s, h, 0, i)),
    }
    column = pl.BlockSpec((1, length, 1), lambda s, i, h: (s, 0, 0))
    row = pl.BlockSpec((1, 1, tile), lambda s, i, h: (s, 0, i))
    return pl.pallas_call(
        functools.partial(kernel, scale),
        grid=(seqs, length // tile, heads),
        in_specs=[column, column, row, row] + [specs[kind] for kind in kinds],
        out_specs=[specs[kind] for kind, _ in outs],
        out_shape=[shape for _, shape in outs],
        scratch_shapes=[pltpu.VMEM((length, tile), wide)],
        compiler_params=pltpu.CompilerParams(vmem_limit_bytes=48 * MIB),
        cost_estimate=BRIEF,
    )(place[:, :, None], segment[:, :, None], place[:, None, :], segment[:, None, :], *arrays)


def per_device(
    g_axes,
    c_axes,
    f_axes,
    tokens,
    places,
    segments,
    routes,
    w_query,
    w_key,
    w_value,
    w_out,
    w_router,
    w_gate,
    w_up,
    w_down,
    gain_attn,
    gain_ffn,
    gain_query,
    gain_key,
    cotangent,
):
    groups, parts_c, parts_f = 1 << len(g_axes), 1 << len(c_axes), 1 << len(f_axes)
    count = tokens.shape[1]
    width = gain_query.shape[0]
    model_width = tokens.shape[2]
    kv_heads = w_key.shape[1] // width // parts_c
    assert kv_heads == 1
    heads = w_query.shape[1] // width // parts_c // groups
    experts = w_gate.shape[0]
    hidden_width = w_gate.shape[2]
    scale = 1.0 / math.sqrt(width)
    rows_d = w_query.shape[0]
    rows_o = w_out.shape[0]
    rows_f = w_down.shape[1]
    pair_count = experts.bit_length() - 1 - len(g_axes) - len(c_axes)
    assert 0 <= pair_count <= len(f_axes)
    far_axes = f_axes[: len(f_axes) - pair_count]
    near_axes = f_axes[len(f_axes) - pair_count :]
    parts_near = 1 << len(near_axes)
    team_axes = c_axes + near_axes
    team = parts_c * parts_near
    own_axes = c_axes + f_axes
    plane_axes = g_axes + c_axes
    cluster_axes = g_axes + team_axes
    all_axes = g_axes + c_axes + f_axes
    all_axes_but_core = c_axes[:-1] + f_axes[::-1] + g_axes
    g_here = flat_index(g_axes)
    core = c_axes[-1:]
    plane_shape = (2,) * len(plane_axes) + (count, model_width)
    cluster_shape = (2,) * len(cluster_axes) + (count, model_width)
    turn = g_axes + c_axes[:-1]
    half = count // 2
    plane_parts = [(0, half, turn), (half, count, turn[1:] + turn[:1])]
    turn = turn + near_axes
    third = (count // 3) // ROW_TILE * ROW_TILE
    cuts = [0, count - 2 * third, count - third, count]
    cluster_parts = [
        (cuts[step], cuts[step + 1], turn[step:] + turn[:step]) for step in range(len(cuts) - 1)
    ]
    def core_last(parts):
        return [(lo, hi, order + core) for lo, hi, order in parts]

    def core_first(parts):
        return [(lo, hi, core + order) for lo, hi, order in parts]

    q_cols = heads * width
    qkv_cols = q_cols + 2 * width
    even = rows_o % (groups * width) == 0
    if even:
        own_query = w_query.reshape(rows_d, parts_c, parts_f, groups, q_cols // parts_f)
        own_query = own_query.transpose(3, 1, 0, 2, 4)
    else:
        own_query = w_query.reshape(rows_d, parts_c, groups, q_cols).transpose(2, 1, 0, 3)
    own_query = take(own_query.reshape(groups, parts_c, rows_d, q_cols), g_here)
    mine_qkv = jnp.concatenate(
        [
            own_query,
            w_key.reshape(rows_d, parts_c, width).transpose(1, 0, 2),
            w_value.reshape(rows_d, parts_c, width).transpose(1, 0, 2),
        ],
        axis=2,
    )
    wide_router = jnp.pad(w_router, ((0, 0), (0, width - experts)))
    resid = tokens[0].astype(jnp.float32)
    norm_one, back_one = jax.vjp(normed, resid, gain_attn)

    def own_expert(place):
        return flat_index(g_axes) * team + place

    mine_out = take(w_out.reshape(groups, -1, model_width), g_here) if even else w_out
    grad_parts = [(lo, hi, near_axes + order) for lo, hi, order in plane_parts]
    all_one, w_qkv, own_grads, pieces_down, w_mix, got_gate, got_up, full_router, marks = transfer(
        1,
        [
            Gather(plane_axes, norm_one.astype(low), core_last(plane_parts)),
            Spread(c_axes, f_axes, mine_qkv, (rows_d, qkv_cols)),
            Gather(turn, cotangent[0], grad_parts),
            Spread(team_axes, far_axes, w_down, w_down.shape[1:], own_expert),
            Gather(f_axes, mine_out, [(0, mine_out.shape[0], f_axes)]),
            Direct(team_axes, w_gate, w_gate.shape[1:], own_expert),
            Direct(team_axes, w_up, w_up.shape[1:], own_expert),
            Direct(own_axes, wide_router[None], wide_router.shape, lambda place: 0),
            Direct(
                g_axes,
                jnp.stack([places[0], segments[0]])[None],
                (2,) + places.shape[1:],
                lambda place: 0,
            ),
        ],
        (1, 0, 2, 3, 0, 2, 4, 1, 0),
    )
    blocks = 1 << len(turn)
    own_grads = own_grads.reshape(blocks, count, model_width)
    far_grads = lax.ppermute(own_grads, core[0], SWAP)
    w_qkv = w_qkv.reshape(model_width, qkv_cols)
    all_one = all_one.reshape(-1, model_width)
    full_router = full_router.reshape(model_width, width)[:, :experts]

    w_mix = w_mix.reshape(-1, model_width)
    if not even:
        w_mix = take(w_mix.reshape(groups, q_cols, model_width), g_here)

    def from_far(got):
        return lax.all_gather(got, far_axes, axis=0, tiled=False) if far_axes else got[None]

    pieces_gate, pieces_up = from_far(got_gate), from_far(got_up)
    pieces_down = pieces_down.reshape((team, -1) + w_down.shape[1:]).transpose(1, 0, 2, 3)
    if rows_f % ROW_TILE:
        pieces_down = pieces_down.reshape((-1, parts_c, parts_near) + w_down.shape[1:])
        pieces_down = pieces_down.transpose(1, 0, 2, 3, 4).reshape(1, 1, hidden_width, model_width)

    place, segment = marks[:, 0], marks[:, 1]
    length = place.shape[1]
    rows = groups * length
    steps = jnp.arange(width // 2).astype(wide)
    inverse = jnp.exp(steps * (-2.0 * math.log(1000000.0) / width))
    inverse = jnp.concatenate([inverse, inverse])[None]
    sign = jnp.where(jnp.arange(width) < width // 2, -1.0, 1.0)[None]
    head_gains = (gain_query[None], gain_key[None])
    lin, query_low, keyed_low, value_low, cosine, sine = row_call(
        functools.partial(prep_kernel, heads),
        rows,
        (all_one, w_qkv, place.reshape(rows, 1), inverse, sign) + head_gains,
        (1, 3, 4, 5, 6),
        [(q_cols + width, wide), (q_cols, low), (width, low), (width, low), (width, wide), (width, wide)],
        [],
    )
    query_low = query_low.reshape(groups, length, q_cols)
    keyed_low = keyed_low.reshape(groups, length, width)
    value_low = value_low.reshape(groups, length, width)
    total_shape = jax.ShapeDtypeStruct((groups, heads, 1, length), wide)
    mixed_low, log_total = attention_call(
        ahead_kernel,
        (place, segment),
        (query_low, keyed_low, value_low.transpose(0, 2, 1)),
        ("query", "keys", "flat"),
        [("query", jax.ShapeDtypeStruct(query_low.shape, low)), ("total", total_shape)],
        width,
        scale,
        4,
    )
    mixed_rows = mixed_low.reshape(groups * length, q_cols)
    branch = dot(mixed_rows, w_mix).astype(low).reshape(plane_shape)
    (branch,) = transfer(2, [Reduce(plane_axes, branch, core_first(plane_parts))])
    resid_one = resid + branch

    norm_two, back_two = jax.vjp(normed, resid_one, gain_ffn)
    normed_two = norm_two.astype(low)
    logits = dot(normed_two, full_router)
    labels = jnp.arange(experts, dtype=jnp.int32)
    chosen = jnp.any(routes[0][:, :, None] == labels[None, None, :], axis=1)
    logits = jnp.where(chosen, logits, -1e30)
    powers = jnp.where(chosen, jnp.exp(logits - jnp.max(logits, axis=-1, keepdims=True)), 0.0)
    gates = powers / jnp.sum(powers, axis=-1, keepdims=True)

    own_two, all_gates = transfer(
        3,
        [
            Gather(turn, normed_two, cluster_parts),
            Gather(cluster_axes, gates.T, [(0, experts, turn + core)]),
        ],
    )
    own_two = own_two.reshape(blocks, count, model_width)
    far_two = lax.ppermute(own_two, core[0], SWAP)
    gate_stack = take_at(all_gates, flat_index(cluster_axes), len(cluster_axes))
    core_here, core_spot = lax.axis_index(core[0]), cluster_axes.index(core[0])
    ids = jnp.bitwise_xor(jnp.arange(blocks), flat_index(turn)).astype(jnp.int32)
    sides = []
    pieces = (pieces_gate, pieces_up, pieces_down)
    for side, side_rows, side_grads in (
        (core_here, own_two, own_grads),
        (1 - core_here, far_two, far_grads),
    ):
        gate = take_at(gate_stack, side, core_spot).reshape(-1, 1)
        sides.append(expert_rows(side_rows, side_grads, gate, pieces, parts_near, ids))
        ids = ids + zero_of(sides[0][2]).astype(jnp.int32)
    hiddens, d_ins, d_gate_parts, made_parts, back_parts = zip(*sides)
    half_shape = (2,) * len(turn) + (count, model_width)
    far_made = lax.ppermute(made_parts[1], core[0], SWAP)
    far_parts = 1 << len(far_axes)
    straight = parts_near * rows_d == TILE
    d_gates = jnp.stack(d_gate_parts).reshape(experts, 1, count)
    hiddens = [part.reshape(blocks, count, hidden_width) for part in hiddens]
    d_ins = [part.reshape(blocks, count, 2 * hidden_width) for part in d_ins]
    back = [part.reshape(half_shape) for part in back_parts]
    down_task = WeightGrad(hiddens, [own_grads, far_grads])
    in_task = WeightGrad(
        [own_two, far_two], d_ins, far_parts if straight else 1, 2, room=down_task
    )
    flows = [
        ReduceBoth(turn, *back, cluster_parts, core),
        Direct(core + turn, d_gates, (1, count)),
        down_task,
        in_task,
    ]
    in_pair = len(far_axes) == 1 and parts_near * rows_f % ROW_TILE == 0
    if in_pair:
        flows.append(PairSum(far_axes[0], down_task, parts_c, parts_near * rows_f))
    d_rows_two, d_gates, part_down, part_in, *sums = transfer(4, flows, (-1, 2, 0, -2, 0, -2, 0))
    d_gates = d_gates.reshape((2,) * len(cluster_axes) + (count,))
    spots = [(core + turn).index(axis) for axis in cluster_axes]
    d_gates = d_gates.transpose(spots + [len(spots)]).reshape(experts, count).T

    reduced = zero_of(d_rows_two).astype(low)

    def to_far(part, rows, done=False):
        stack = part
        if not done:
            stack = part.reshape(parts_c, -1, parts_near, rows, part.shape[1]) + reduced
            stack = stack.transpose(1, 0, 2, 3, 4)
        stack = stack.reshape(-1, team, rows, part.shape[1])
        if not far_axes:
            return stack[0]
        return lax.psum_scatter(stack, far_axes, scatter_dimension=0, tiled=False)

    share_in = to_far(part_in, rows_d, straight)
    if in_pair:
        share_down = sums[0].reshape(team, rows_f, model_width)
    else:
        share_down = to_far(part_down, rows_f)

    d_logits = (gates * (d_gates - jnp.sum(gates * d_gates, axis=-1, keepdims=True))).astype(low)
    part_router = dot_tn(normed_two, d_logits)
    d_normed_two = d_rows_two + dot_nt(d_logits, full_router)
    d_resid_one, d_gain_ffn = back_two(d_normed_two)
    d_resid_one = d_resid_one + cotangent[0].astype(jnp.float32)
    wide_part = jnp.pad(part_router.astype(low), ((0, 0), (0, width - experts)))

    made_axes = turn[: len(turn) - len(near_axes)]
    made_shape = (2,) * len(made_axes) + (parts_near * count, model_width)
    made = (made_parts[0].reshape(made_shape), far_made.reshape(made_shape))
    made_spans = [(lo * parts_near, hi * parts_near, order) for lo, hi, order in plane_parts]
    d_branch, made = transfer(
        5,
        [
            Gather(plane_axes, d_resid_one.astype(low), core_last(plane_parts)),
            ReduceBoth(made_axes, *made, made_spans),
        ],
    )
    d_branch = d_branch.reshape(-1, model_width)
    d_mixed = dot_nt(d_branch, w_mix).astype(low).reshape(query_low.shape)
    shapes = [
        jax.ShapeDtypeStruct(query_low.shape, low),
        jax.ShapeDtypeStruct(keyed_low.shape, wide),
        jax.ShapeDtypeStruct(keyed_low.shape, wide),
    ]
    d_query, d_keyed, d_value = attention_call(
        behind_kernel,
        (place, segment),
        (query_low, d_mixed, keyed_low, value_low, keyed_low.transpose(0, 2, 1), log_total),
        ("query", "query", "keys", "keys", "flat", "total"),
        list(zip(("query", "keys", "keys"), shapes)),
        width,
        scale,
        10,
    )
    heads_back = HeadsBack(
        heads,
        scale,
        (
            d_query.reshape(rows, q_cols),
            d_keyed.reshape(rows, width),
            d_value.reshape(rows, width),
            lin,
            cosine,
            sine,
            all_one,
        ),
        w_qkv,
        head_gains + (gain_attn[None],),
        d_gain_ffn.reshape(-1, width),
        plane_axes,
    )
    part_out = weight_grad([mixed_rows], [d_branch]).reshape(q_cols, model_width)
    pieces_tile = TILE // rows_d
    runs = parts_f // pieces_tile
    spare = len(f_axes) - (pieces_tile.bit_length() - 1)
    qkv_shape = (2,) * len(f_axes) + (parts_c * rows_d, qkv_cols)

    def qkv_place(step):
        bits = [step % runs // (runs >> (bit + 1)) % 2 for bit in range(spare)]
        return tuple(bits) + (0,) * (len(f_axes) - spare) + (step // runs, 0)

    qkv_block = (None,) * spare + (2,) * (len(f_axes) - spare) + (rows_d, qkv_cols)
    stack = (1 << len(plane_axes), count)
    qkv_task = WeightGrad(
        [all_one.reshape(stack + (model_width,))],
        [jax.ShapeDtypeStruct(stack + (qkv_cols,), low)],
        source=lambda: heads_back.refs[1][0],
        out=(qkv_shape, qkv_block, qkv_place),
    )

    turn_back = plane_axes[len(g_axes) : -1] + g_axes
    def over_groups(shape):
        return Gather(g_axes, shape, [(0, shape.shape[0], g_axes)])

    def to_column_owners(shape):
        return Spread(c_axes, g_axes, shape, shape.shape[1:])

    flows = [
        Spread(team_axes, g_axes, share_down, share_down.shape[1:]),
        Spread(team_axes, g_axes, share_in, share_in.shape[1:]),
        Fed(
            Reduce(
                plane_axes,
                heads_back.results[1],
                core_first([(lo, hi, turn_back) for lo, hi, _ in plane_parts]),
            ),
            lambda: heads_back.refs[1][1],
        ),
        Fed(
            Reduce(
                f_axes,
                qkv_task.results[0],
                [(0, parts_c * rows_d, f_axes[::-1])],
                jax.ShapeDtypeStruct((parts_c, rows_d, qkv_cols), low),
                to_column_owners,
            ),
            lambda: qkv_task.refs[1][0],
        ),
        Reduce(
            own_axes,
            wide_part.reshape((2,) * len(own_axes) + (rows_d, width)),
            [(0, rows_d, own_axes)],
            jax.ShapeDtypeStruct((rows_d, width), low),
            over_groups,
        ),
    ]
    if even:
        rows = q_cols // parts_f
        stack = part_out.reshape((2,) * len(f_axes) + (rows, model_width))
        shape = jax.ShapeDtypeStruct((rows, model_width), low)
        flows.append(Later(Reduce(f_axes, stack, [(0, rows, f_axes[::-1])], shape, over_groups)))
    if near_axes:
        near_shape = (2,) * len(near_axes) + (count, model_width)
        near_flow = Reduce(
            near_axes, made.astype(low).reshape(near_shape), [(0, count, near_axes)], by_distance=True
        )
        flows.append(Later(near_flow))
    lines = jax.ShapeDtypeStruct((heads_back.lines, width), wide)
    gains_flow = Gather(all_axes, lines, [(0, heads_back.lines, core + all_axes_but_core)])
    flows.insert(5, Fed(gains_flow, lambda: heads_back.refs[2][0]))
    flows += [heads_back, qkv_task]
    all_down, all_in, d_one, all_qkv, share_router, gains, *rest = transfer(
        7,
        flows,
        (-1, 0, 2, -2, 2, 3, 1, 6, 5, 3, 2, 6, 7, 3, 3, 6, 6, 3, 4, 5, 4, 5, 4, 5, 4, 5),
    )
    rest = rest[:-3]
    gains = jnp.sum(gains.reshape(-1, heads_back.lines * width), axis=0)
    share_router = share_router.reshape(groups, rows_d, width)[:, :, :experts]
    grad_router = jnp.sum(share_router.astype(wide), axis=0)
    if near_axes:
        made = rest.pop()
    output = (resid_one + made).astype(low)[None]
    d_resid = back_one(d_one)[0]
    grad_tokens = (d_resid + d_resid_one)[None]
    grad_down, = by_expert(all_down, 1)
    grad_gate, grad_up = by_expert(all_in, 2)
    if even:
        grad_out = rest[0].astype(wide).reshape(rows_o, model_width)
    else:
        stack = jnp.where(jnp.arange(groups)[:, None, None] == g_here, part_out[None], 0)
        share_out = lax.psum_scatter(
            stack.reshape(groups * q_cols, model_width), f_axes, scatter_dimension=0, tiled=True
        )
        grad_out = lax.psum(share_out.astype(wide), g_axes)
    grad_query, grad_key, grad_value = by_head(
        all_qkv.reshape(parts_c, groups, rows_d, qkv_cols), parts_f if even else 1, width
    )
    return (
        output,
        grad_tokens,
        grad_query,
        grad_key,
        grad_value,
        grad_out,
        grad_router,
        grad_gate,
        grad_up,
        grad_down,
        gains[:model_width],
        gains[model_width : 2 * model_width],
        gains[2 * model_width : 2 * model_width + width],
        gains[2 * model_width + width : 2 * model_width + 2 * width],
    )


def solution(mesh):
    def binary(letter, size):
        return tuple(letter + str(step) for step in range(size.bit_length() - 1))

    g_axes = binary("g", mesh.shape["grp"])
    c_axes = binary("c", mesh.shape["ctx"])
    f_axes = binary("f", mesh.shape["fsdp"])
    names = g_axes + c_axes + f_axes
    fine = Mesh(mesh.devices.reshape((2,) * len(names)), names)
    rows = P(g_axes + f_axes, c_axes, None)
    line = P(g_axes + f_axes, None)
    split = P(c_axes + f_axes, None)
    expert = P(None, c_axes + f_axes, None)
    whole = P()
    in_specs = (
        (rows, line, line, rows)
        + (split,) * 5
        + (expert,) * 3
        + (whole,) * 4
        + (rows,)
    )
    out_specs = (rows, rows) + (split,) * 5 + (expert,) * 3 + (whole,) * 4

    def device_part(*arrays):
        return per_device(g_axes, c_axes, f_axes, *arrays)

    return jax.shard_map(
        device_part, mesh=fine, in_specs=in_specs, out_specs=out_specs, check_vma=False
    )
```

```python
import functools
import itertools
import math

import jax
import jax.numpy as jnp
from jax import lax
from jax.experimental import pallas as pl
from jax.experimental.pallas import tpu as pltpu
from jax.sharding import Mesh
from jax.sharding import PartitionSpec as P

epsilon = 1e-06
low = jnp.bfloat16
wide = jnp.float32
SWAP = [(0, 1), (1, 0)]
ROW_TILE = 16
MIB = 1 << 20
TILE = 256
WAIT_LAST = 8
LONG = 16
BRIEF = pl.CostEstimate(flops=0, bytes_accessed=0, transcendentals=0)


def normed(values, gain):
    return values * lax.rsqrt(jnp.mean(values * values, axis=-1, keepdims=True) + epsilon) * gain


def dot(left, right):
    return jnp.dot(left, right, preferred_element_type=jnp.float32)


def dot_nt(left, right):
    return lax.dot_general(left, right, (((1,), (1,)), ((), ())), preferred_element_type=jnp.float32)


def dot_tn(left, right):
    return lax.dot_general(left, right, (((0,), (0,)), ((), ())), preferred_element_type=jnp.float32)


def zero_of(anchor):
    return jnp.minimum(jnp.abs(anchor[(0,) * anchor.ndim].astype(wide)), 0.0)


def flat_index(axes):
    index = 0
    for axis in axes:
        index = index * 2 + lax.axis_index(axis)
    return index


def take(stack, index):
    return lax.dynamic_index_in_dim(stack, index, 0, keepdims=False)


def take_at(stack, index, at):
    return lax.dynamic_index_in_dim(stack, index, at, keepdims=False)


def sems(amount):
    return pltpu.SemaphoreType.DMA((amount,))


def toward(flips):
    return {axis: 1 - lax.axis_index(axis) for axis in flips}


def remote(src, dst, send, recv, flips):
    return pltpu.make_async_remote_copy(
        src_ref=src,
        dst_ref=dst,
        send_sem=send,
        recv_sem=recv,
        device_id=toward(flips),
        device_id_type=pl.DeviceIdType.MESH,
    )


class Direct:
    def __init__(self, axes, operand, block, pick=None, rounds=0):
        self.axes, self.block, self.pick, self.rounds = axes, block, pick, rounds
        self.amount = 1 << len(axes)
        self.operands = [operand]
        self.results = [jax.ShapeDtypeStruct((self.amount,) + block, operand.dtype)]
        self.scratch = [
            sems(self.amount),
            sems(self.amount),
            sems(2),
            pltpu.VMEM(block, operand.dtype),
        ]
        self.steps = [
            tuple(axis for bit, axis in enumerate(reversed(axes)) if step >> bit & 1)
            for step in range(self.amount)
        ]
        self.flips = self.steps[1:]

    def begin(self, operands, target, send, recv):
        copies = []
        for step in range(1, self.amount):
            other = 0
            for axis in self.axes:
                place = lax.axis_index(axis)
                other = other * 2 + (1 - place if axis in self.steps[step] else place)
            copy = remote(
                operands[0].at[step if self.pick is None else self.pick(other)],
                target,
                send.at[step],
                recv.at[step],
                self.steps[step],
            )
            copy.start()
            copies.append(copy)
        return copies

    def keep(self, operands, target, local, held):
        own = 0 if self.pick is None else self.pick(flat_index(self.axes))
        load = pltpu.make_async_copy(operands[0].at[own], held, local.at[0])
        load.start()
        load.wait()
        store = pltpu.make_async_copy(held, target, local.at[1])
        store.start()
        store.wait()

    def run(self, operands, results, scratch):
        send, recv, local, held = scratch
        for _ in range(self.rounds):
            yield
        target = results[0].at[flat_index(self.axes)]
        copies = self.begin(operands, target, send, recv)
        self.keep(operands, target, local, held)
        for _ in range(WAIT_LAST):
            yield
        for copy in copies:
            copy.wait()


class Spread(Direct):
    def __init__(self, axes, others, operand, block, pick=lambda place: place):
        super().__init__(axes, operand, block, pick)
        self.others = others
        self.results = [
            jax.ShapeDtypeStruct((self.amount,) + (2,) * len(others) + block, operand.dtype)
        ]
        self.scratch += [sems(max(1, len(others))), sems(max(1, len(others)))]
        self.flips = self.flips + [(axis,) for axis in others]

    def run(self, operands, results, scratch):
        send, recv, local, held, next_send, next_recv = scratch
        here = flat_index(self.axes)
        place = {axis: lax.axis_index(axis) for axis in self.others}
        spot = tuple(place[axis] for axis in self.others)
        copies = self.begin(operands, results[0].at[(here,) + spot], send, recv)
        self.keep(operands, results[0].at[(here,) + spot], local, held)
        yield
        for copy in copies:
            copy.wait_recv()
        for stage, axis in enumerate(self.others):
            region = tuple(
                slice(None) if other in self.others[:stage] else place[other]
                for other in self.others
            )
            region = results[0].at[(slice(None),) + region]
            copy = remote(region, region, next_send.at[stage], next_recv.at[stage], (axis,))
            copy.start()
            yield
            copy.wait()
        for copy in copies:
            copy.wait_send()


class Gather:
    def __init__(self, axes, operand, parts):
        self.axes, self.parts = axes, parts
        self.operands = [operand]
        self.results = [
            jax.ShapeDtypeStruct((2,) * len(axes) + operand.shape, operand.dtype)
        ]
        amount = len(parts) * len(axes)
        self.scratch = [sems(amount), sems(amount), sems(2), pltpu.VMEM(operand.shape, operand.dtype)]
        self.flips = [(axis,) for axis in axes]

    def run(self, operands, results, scratch):
        send, recv, local, held = scratch
        place = {axis: lax.axis_index(axis) for axis in self.axes}
        load = pltpu.make_async_copy(operands[0], held, local.at[0])
        load.start()
        load.wait()
        spot = tuple(place[axis] for axis in self.axes)
        store = pltpu.make_async_copy(held, results[0].at[spot], local.at[1])
        store.start()
        store.wait()
        copies = {}

        def start(number, stage):
            lo, hi, order = self.parts[number]
            region = tuple(
                slice(None) if axis in order[:stage] else place[axis] for axis in self.axes
            )
            region = results[0].at[region + (pl.ds(lo, hi - lo),)]
            slot = number * len(self.axes) + stage
            copies[number, stage] = remote(
                region, region, send.at[slot], recv.at[slot], (order[stage],)
            )
            copies[number, stage].start()

        for number in range(len(self.parts)):
            start(number, 0)
        yield
        for stage in range(1, len(self.axes)):
            for number in range(len(self.parts)):
                copies[number, stage - 1].wait_recv()
                start(number, stage)
            yield
        for number in range(len(self.parts)):
            copies[number, len(self.axes) - 1].wait_recv()
        for copy in copies.values():
            copy.wait_send()


class Reduce:
    def __init__(self, axes, operand, parts, ready=None, last=None, by_distance=False):
        self.axes, self.parts, self.by_distance = axes, parts, by_distance
        count, columns = operand.shape[-2:]
        self.operands = [operand]
        self.results = [jax.ShapeDtypeStruct((count, columns), wide)]
        self.scratch = []
        for lo, hi, order in parts:
            for stage in range(len(axes)):
                left = len(axes) - 1 - stage
                self.scratch.append(pltpu.VMEM((2,) * left + (hi - lo, columns), low))
            self.scratch.append(pltpu.VMEM((2,) * (len(axes) - 1) + (hi - lo, columns), low))
        self.scratch.append(pltpu.VMEM((count, columns), wide))
        amount = len(parts) * len(axes)
        self.flips = [(axis,) for axis in axes]
        self.last = None
        if last is not None:
            self.last = last(ready)
            self.results = self.last.results
            self.flips = self.flips + self.last.flips
            self.scratch += [pltpu.VMEM(ready.shape, low)] + self.last.scratch
        self.scratch += [sems(amount), sems(amount), sems(len(parts) + 1)]

    def run(self, operands, results, scratch):
        stages = len(self.axes)
        send, recv, local = scratch[-3:]
        total = scratch[len(self.parts) * (stages + 1)]
        place = {axis: 0 if self.by_distance else lax.axis_index(axis) for axis in self.axes}
        copies, loads = {}, []

        def buffers(number):
            base = number * (stages + 1)
            return scratch[base : base + stages], scratch[base + stages]

        def start(number, stage):
            lo, hi, order = self.parts[number]
            slots, held = buffers(number)
            slot = number * stages + stage
            axis = order[stage]
            if stage == 0:
                spot = tuple(
                    1 - place[other] if other == axis else slice(None) for other in self.axes
                )
                source = operands[0].at[spot + (pl.ds(lo, hi - lo),)]
            else:
                rest = [other for other in self.axes if other != order[0]]
                spot = tuple(
                    place[other]
                    if other in order[:stage]
                    else 1 - place[other]
                    if other == axis
                    else slice(None)
                    for other in rest
                )
                source = held.at[spot]
            copies[number, stage] = remote(
                source, slots[stage], send.at[slot], recv.at[slot], (axis,)
            )
            copies[number, stage].start()

        for number, (lo, hi, order) in enumerate(self.parts):
            start(number, 0)
            spot = tuple(
                place[other] if other == order[0] else slice(None) for other in self.axes
            )
            load = pltpu.make_async_copy(
                operands[0].at[spot + (pl.ds(lo, hi - lo),)], buffers(number)[1], local.at[number]
            )
            load.start()
            loads.append(load)
        yield
        for stage in range(stages):
            for number, (lo, hi, order) in enumerate(self.parts):
                slots, held = buffers(number)
                if stage == 0:
                    loads[number].wait()
                copies[number, stage].wait_recv()
                rest = [other for other in self.axes if other != order[0]]
                gone = order[: stage + 1]
                free = [other for other in rest if other not in gone]
                for code in range(1 << len(free)):
                    bits = {axis: code >> bit & 1 for bit, axis in enumerate(free)}
                    spot = tuple(bits[axis] if axis in bits else place[axis] for axis in rest)
                    slot_spot = tuple(bits[axis] for axis in free)
                    last = stage == stages - 1

                    def add(step, carry, spot=spot, slot_spot=slot_spot, last=last):
                        rows = pl.ds(pl.multiple_of(step * ROW_TILE, ROW_TILE), ROW_TILE)
                        value = held[spot + (rows,)].astype(wide)
                        value = value + slots[stage][slot_spot + (rows,)].astype(wide)
                        if last:
                            at = pl.multiple_of(step * ROW_TILE + lo, ROW_TILE)
                            total[pl.ds(at, ROW_TILE)] = value
                        else:
                            held[spot + (rows,)] = value.astype(low)
                        return carry

                    lax.fori_loop(0, (hi - lo) // ROW_TILE, add, 0)
                if stage + 1 < stages:
                    start(number, stage + 1)
            yield
        if self.last is None:
            store = pltpu.make_async_copy(total, results[0], local.at[len(self.parts)])
            store.start()
            store.wait()
        else:
            ready, *others = scratch[len(self.parts) * (stages + 1) + 1 : -3]
            ready[...] = total[...].astype(low).reshape(ready.shape)
            yield from self.last.run([ready], results, others)
        for copy in copies.values():
            copy.wait_send()


class ReduceBoth(Reduce):
    def __init__(self, axes, operand, other, parts, first=(), hold=False):
        super().__init__(axes, operand, parts, by_distance=True)
        self.first, self.hold = first, hold
        self.flips = self.flips + [(axis,) for axis in first]
        self.operands = [operand, other]
        shape = operand.shape
        self.scratch = [pltpu.VMEM(shape, low), pltpu.VMEM(shape, low)]
        for lo, hi, order in parts:
            for stage in range(len(axes)):
                left = len(axes) - 1 - stage
                self.scratch.append(pltpu.VMEM((2,) * left + (hi - lo, shape[-1]), low))
        self.scratch.append(pltpu.VMEM(shape[-2:], wide))
        amount = len(parts) * len(axes)
        self.scratch += [sems(amount), sems(amount), sems(2 * len(parts) + 1), sems(len(parts))]

    def run(self, operands, results, scratch):
        stages = len(self.axes)
        held, added, *slots = scratch[:-5]
        total, send, recv, local, far = scratch[-5:]
        copies, loads = {}, []
        every = (slice(None),) * stages

        def start(number, stage):
            lo, hi, order = self.parts[number]
            spot = tuple(
                0 if axis in order[:stage] else 1 if axis == order[stage] else slice(None)
                for axis in self.axes
            )
            slot = number * stages + stage
            copies[number, stage] = remote(
                held.at[spot + (pl.ds(lo, hi - lo),)],
                slots[slot],
                send.at[slot],
                recv.at[slot],
                (order[stage],),
            )
            copies[number, stage].start()

        def add_all(lo, hi, free, spot_of, source, last):
            for code in range(1 << len(free)):
                bits = {axis: code >> bit & 1 for bit, axis in enumerate(free)}
                spot = tuple(bits.get(axis, 0) for axis in self.axes)
                source_spot = spot_of(bits)

                def add(step, carry, spot=spot, source_spot=source_spot):
                    at = pl.multiple_of(step * ROW_TILE, ROW_TILE)
                    rows = pl.ds(pl.multiple_of(at + lo, ROW_TILE), ROW_TILE)
                    value = held[spot + (rows,)].astype(wide)
                    shift = rows if source is added else pl.ds(at, ROW_TILE)
                    value = value + source[source_spot + (shift,)].astype(wide)
                    if last:
                        total[rows] = value
                    else:
                        held[spot + (rows,)] = value.astype(low)
                    return carry

                lax.fori_loop(0, (hi - lo) // ROW_TILE, add, 0)

        for number, (lo, hi, order) in enumerate(self.parts):
            span = every + (pl.ds(lo, hi - lo),)
            for which, (operand, buffer) in enumerate(zip(operands, (held, added))):
                if which and self.first:
                    load = remote(
                        operand.at[span],
                        added.at[span],
                        far.at[number],
                        local.at[2 * number + which],
                        self.first,
                    )
                else:
                    load = pltpu.make_async_copy(
                        operand.at[span], buffer.at[span], local.at[2 * number + which]
                    )
                load.start()
                loads.append(load)
        if self.first:
            yield
        for number, (lo, hi, order) in enumerate(self.parts):
            loads[2 * number].wait()
            loads[2 * number + 1].wait()
            add_all(
                lo, hi, self.axes, lambda bits: tuple(bits[axis] for axis in self.axes), added, False
            )
            if not self.hold:
                start(number, 0)
        yield
        if self.hold:
            for number in range(len(self.parts)):
                start(number, 0)
            yield
        for stage in range(stages):
            for number, (lo, hi, order) in enumerate(self.parts):
                copies[number, stage].wait_recv()
                free = [axis for axis in self.axes if axis not in order[: stage + 1]]
                add_all(
                    lo,
                    hi,
                    free,
                    lambda bits, free=free: tuple(bits[axis] for axis in free),
                    slots[number * stages + stage],
                    stage == stages - 1,
                )
                if stage + 1 < stages:
                    start(number, stage + 1)
            yield
        store = pltpu.make_async_copy(total, results[0], local.at[2 * len(self.parts)])
        store.start()
        store.wait()
        for copy in copies.values():
            copy.wait_send()


class Later:
    def __init__(self, flow):
        self.flow, self.flips = flow, flow.flips
        self.operands, self.results, self.scratch = flow.operands, flow.results, flow.scratch

    def run(self, *parts):
        yield
        yield from self.flow.run(*parts)


class Fed(Later):
    def __init__(self, flow, source):
        super().__init__(flow)
        self.source, self.operands = source, []

    def run(self, operands, results, scratch):
        yield
        yield from self.flow.run([self.source()], results, scratch)


class PairSum:
    def __init__(self, axis, task, groups, rows):
        self.axis, self.task, self.groups, self.rows = axis, task, groups, rows
        shape = (groups, rows, task.width)
        self.operands, self.flips = [], [(axis,)]
        self.results = [jax.ShapeDtypeStruct(shape, low)]
        self.scratch = [pltpu.VMEM(shape, low), pltpu.VMEM(shape, low)]
        self.scratch += [sems(groups), sems(groups), sems(groups + 1)]

    def run(self, operands, results, scratch):
        held, added, send, recv, local = scratch
        source, place = self.task.refs[1][0], lax.axis_index(self.axis)
        yield

        def part(group, whose):
            at = pl.multiple_of((group * 2 + whose) * self.rows, self.rows)
            return source.at[pl.ds(at, self.rows)]

        copies = []
        for group in range(self.groups):
            copy = remote(
                part(group, 1 - place), added.at[group], send.at[group], recv.at[group], (self.axis,)
            )
            load = pltpu.make_async_copy(part(group, place), held.at[group], local.at[group])
            copy.start()
            load.start()
            copies += [copy, load]
        yield
        for copy in copies:
            copy.wait()
        for group in range(self.groups):

            def add(step, carry, group=group):
                at = pl.ds(pl.multiple_of(step * ROW_TILE, ROW_TILE), ROW_TILE)
                value = held[group, at].astype(wide) + added[group, at].astype(wide)
                held[group, at] = value.astype(low)
                return carry

            lax.fori_loop(0, self.rows // ROW_TILE, add, 0)
        store = pltpu.make_async_copy(held, results[0], local.at[self.groups])
        store.start()
        store.wait()


class Task:
    flips = ()


def bit_spots(blocks):
    return list(itertools.product((0, 1), repeat=blocks.bit_length() - 1))


def bits_of(step, blocks):
    amount = blocks.bit_length() - 1
    return tuple(step // (blocks >> (bit + 1)) % 2 for bit in range(amount))


class Branch(Task):
    def __init__(self, source, w_mix, seqs, blocks, count):
        self.source, self.seqs, self.blocks, self.count = source, seqs, blocks, count
        self.columns, self.model_width = w_mix.shape
        self.operands = [w_mix]
        shape = (seqs, blocks // seqs * count, self.columns)
        self.results = [jax.ShapeDtypeStruct(shape, low)]
        self.scratch = [pltpu.VMEM(w_mix.shape, low), sems(1)]

    def run(self, operands, results, scratch):
        w_ref, done = scratch
        copy = pltpu.make_async_copy(operands[0], w_ref, done.at[0])
        copy.start()
        copy.wait()
        each = self.blocks // self.seqs

        def body(rows_ref, out_ref):
            out_ref[...] = dot_nt(rows_ref[...], w_ref[...]).astype(low)

        free = (None,) * (self.blocks.bit_length() - 1)
        pltpu.emit_pipeline(
            body,
            grid=(self.blocks,),
            in_specs=[
                pl.BlockSpec(
                    free + (self.count, self.model_width),
                    lambda step: bits_of(step, self.blocks) + (0, 0),
                )
            ],
            out_specs=[
                pl.BlockSpec(
                    (None, self.count, self.columns), lambda step: (step // each, step % each, 0)
                )
            ],
        )(self.source(), results[0])


class HeadsBehind(Task):
    def __init__(self, source, marks, arrays, scale, tile=256):
        self.source, self.scale, self.tile, self.calls = source, scale, tile, 0
        place, segment = marks
        query, keyed = arrays[:2]
        self.seqs, self.length, columns = query.shape
        self.width = keyed.shape[2]
        self.heads = columns // self.width
        self.operands = [place[:, :, None], segment[:, :, None], place[:, None], segment[:, None]]
        self.operands += list(arrays)
        self.results = [
            jax.ShapeDtypeStruct(query.shape, low),
            jax.ShapeDtypeStruct(keyed.shape, wide),
            jax.ShapeDtypeStruct(keyed.shape, wide),
        ]
        total = pltpu.VMEM((self.length, self.width), wide)
        self.scratch = [pltpu.VMEM((self.length, tile), wide), total, total]

    def run(self, operands, results, scratch):
        bias, d_k_total, d_v_total = scratch
        seq = self.calls
        self.calls = (self.calls + 1) % self.seqs
        tiles = self.length // self.tile
        d_k_total[...] = jnp.zeros_like(d_k_total)
        d_v_total[...] = jnp.zeros_like(d_v_total)

        def body(
            k_place,
            k_segment,
            q_place,
            q_segment,
            q_ref,
            k_ref,
            v_ref,
            kt_ref,
            total_ref,
            d_mixed_ref,
            d_q_ref,
            d_k_ref,
            d_v_ref,
        ):
            at, head = pl.program_id(0), pl.program_id(1)

            @pl.when(head == 0)
            def _():
                allowed = (k_segment[...] == q_segment[...]) & (k_place[...] <= q_place[...])
                bias[...] = jnp.where(allowed, 0.0, -1e30)

            query, d_mixed = q_ref[...], d_mixed_ref[...]
            probs = jnp.exp(dot_nt(k_ref[...], query) * self.scale + bias[...] - total_ref[...])
            d_probs = dot_nt(v_ref[...], d_mixed)
            row_dot = jnp.sum(probs * d_probs, axis=0, keepdims=True)
            d_scores = (probs * (d_probs - row_dot)).astype(low)
            d_v_total[...] += dot(probs.astype(low), d_mixed)
            d_k_total[...] += dot(d_scores, query)
            d_q_ref[...] = (dot(kt_ref[...], d_scores) * self.scale).T.astype(low)

            @pl.when((at == tiles - 1) & (head == self.heads - 1))
            def _():
                d_k_ref[...] = d_k_total[...]
                d_v_ref[...] = d_v_total[...]

        column = pl.BlockSpec((None, self.length, 1), lambda i, h: (seq, 0, 0))
        row = pl.BlockSpec((None, 1, self.tile), lambda i, h: (seq, 0, i))
        query = pl.BlockSpec((None, self.tile, self.width), lambda i, h: (seq, i, h))
        keys = pl.BlockSpec((None, self.length, self.width), lambda i, h: (seq, 0, 0))
        flat = pl.BlockSpec((None, self.width, self.length), lambda i, h: (seq, 0, 0))
        total = pl.BlockSpec((None, None, 1, self.tile), lambda i, h: (seq, h, 0, i))
        pltpu.emit_pipeline(
            body,
            grid=(tiles, self.heads),
            in_specs=[column, column, row, row, query, keys, keys, flat, total, query],
            out_specs=[query, keys, keys],
        )(*operands, self.source(), *results)


class WeightGrad(Task):
    def __init__(self, lefts, rights, turns=1, pieces=1, source=None, out=None, room=None):
        self.amount, self.turns, self.pieces, self.calls = len(lefts), turns, pieces, 0
        self.source, self.room = source, room
        self.operands = list(lefts) + (list(rights) if source is None else [])
        self.blocks, self.rows, self.columns = lefts[0].shape
        self.width = rights[0].shape[-1]
        self.out = out or ((self.columns, self.width), (TILE, self.width), self.place)
        self.results = [jax.ShapeDtypeStruct(self.out[0], low)]
        shape = (self.amount, self.blocks, self.rows, self.width)
        self.scratch = [sems(max(self.amount, self.blocks))] + ([] if room else [pltpu.VMEM(shape, low)])

    def run(self, operands, results, scratch):
        done = scratch[0]
        held = self.room.refs[2][1] if self.room else scratch[1]
        span = slice(0, self.width)
        if self.calls == 0:
            rights = operands[self.amount :] if self.source is None else [self.source()]
            copies = [
                pltpu.make_async_copy(
                    right, held.at[number, :, :, pl.ds(0, self.width)], done.at[number]
                )
                for number, right in enumerate(rights)
                if len(right.shape) == 3
            ]
            if not copies:
                copies = [
                    pltpu.make_async_copy(rights[0].at[bits], held.at[0, number], done.at[number])
                    for number, bits in enumerate(bit_spots(self.blocks))
                ]
            for copy in copies:
                copy.start()
            for copy in copies:
                copy.wait()
        share = self.columns // TILE // self.pieces
        first = self.calls * share
        self.calls = (self.calls + 1) % self.pieces

        def body(*refs):
            total = 0.0
            for number, left_ref in enumerate(refs[:-1]):
                right = held[number, :, :, span].reshape(-1, self.width)
                total = total + dot_tn(left_ref[...].reshape(-1, TILE), right)
            refs[-1][...] = total.astype(low).reshape(refs[-1].shape)

        block = pl.BlockSpec((self.blocks, self.rows, TILE), lambda step: (0, 0, step + first))
        pltpu.emit_pipeline(
            body,
            grid=(share,),
            in_specs=[block] * self.amount,
            out_specs=[pl.BlockSpec(self.out[1], lambda step: self.out[2](step + first))],
        )(*operands[: self.amount], results[0])

    def place(self, step):
        steps = self.columns // TILE
        return (step % self.turns * (steps // self.turns) + step // self.turns, 0)


class HeadsBack(Task):
    def __init__(self, heads, scale, tiled, w_qkv, gains, ffn_lines, axes):
        self.heads, self.scale, self.axes = heads, scale, axes
        self.operands = list(tiled) + [w_qkv, ffn_lines] + list(gains)
        self.tiled = len(tiled)
        self.rows, self.width = tiled[1].shape
        self.model_width, self.columns = w_qkv.shape
        self.blocks = 1 << len(axes)
        self.tile = self.rows // self.blocks
        self.results = [
            jax.ShapeDtypeStruct((self.blocks, self.tile, self.columns), low),
            jax.ShapeDtypeStruct((2,) * len(axes) + (self.tile, self.model_width), low),
        ]
        own, ffn = self.model_width // self.width, ffn_lines.shape[0]
        self.lines = -(-(own + ffn + 2) // 8) * 8
        row = pltpu.VMEM((1, self.width), wide)
        long_row = pltpu.VMEM((1, self.model_width), wide)
        self.scratch = [pltpu.VMEM((self.lines, self.width), wide), pltpu.VMEM(w_qkv.shape, low)]
        self.scratch += [row, row, long_row, row, row, long_row, sems(5)]

    def run(self, operands, results, scratch):
        lines, w_ref, gain_q, gain_k, gain, d_gain_q, d_gain_k, d_gain, done = scratch
        w_hbm, ffn, *gains = operands[self.tiled :]
        own, count = self.model_width // self.width, ffn.shape[0]
        lines[...] = jnp.zeros_like(lines)
        targets = [w_ref, lines.at[pl.ds(own, count)], gain_q, gain_k, gain]
        copies = [
            pltpu.make_async_copy(source, target, done.at[number])
            for number, (source, target) in enumerate(zip([w_hbm, ffn] + gains, targets))
        ]
        for copy in copies:
            copy.start()
        for copy in copies:
            copy.wait()
        for total in (d_gain_q, d_gain_k, d_gain):
            total[...] = jnp.zeros_like(total)

        def body(
            d_query_ref,
            d_keyed_ref,
            d_value_ref,
            lin_ref,
            cosine_ref,
            sine_ref,
            rows_ref,
            d_lin_ref,
            d_one_ref,
        ):
            cosine, sine = cosine_ref[...], sine_ref[...]
            for head in range(self.heads + 1):
                span = slice(head * self.width, (head + 1) * self.width)
                values = lin_ref[:, span]
                if head < self.heads:
                    grads, own_gain, d_head = d_query_ref[:, span].astype(wide), gain_q, d_gain_q
                else:
                    grads, own_gain, d_head = d_keyed_ref[...] * self.scale, gain_k, d_gain_k
                grads = turned_back(grads, cosine, sine)
                factor = head_scale(values)
                plain = values * factor
                d_head[...] += jnp.sum(grads * plain, axis=0, keepdims=True)
                grads = grads * own_gain[...]
                mean = jnp.mean(grads * plain, axis=1, keepdims=True)
                d_lin_ref[:, span] = (factor * (grads - plain * mean)).astype(low)
            d_lin_ref[:, (self.heads + 1) * self.width :] = d_value_ref[...].astype(low)
            d_one = dot_nt(d_lin_ref[...], w_ref[...])
            d_one_ref[...] = d_one.astype(low)
            share = jnp.sum(d_one * rows_ref[...].astype(wide), axis=0, keepdims=True)
            d_gain[...] += share / gain[...]

        def by_bits(step):
            bits = [step // (self.blocks >> (bit + 1)) % 2 for bit in range(len(self.axes))]
            return tuple(bits) + (0, 0)

        pltpu.emit_pipeline(
            body,
            grid=(self.blocks,),
            in_specs=[
                pl.BlockSpec((self.tile, array.shape[1]), lambda step: (step, 0))
                for array in operands[: self.tiled]
            ],
            out_specs=[
                pl.BlockSpec((None, self.tile, self.columns), lambda step: (step, 0, 0)),
                pl.BlockSpec((None,) * len(self.axes) + (self.tile, self.model_width), by_bits),
            ],
        )(*operands[: self.tiled], *results)
        for line in range(own):
            lines[line : line + 1] = d_gain[:, line * self.width : (line + 1) * self.width]
        lines[own + count : own + count + 1] = d_gain_q[...]
        lines[own + count + 1 : own + count + 2] = d_gain_k[...]


def flow_kernel(flows, plan, *refs):
    refs = list(refs)

    def cut(amount):
        part = refs[:amount]
        del refs[:amount]
        return part

    operands = [cut(len(flow.operands)) for flow in flows]
    results = [cut(len(flow.results)) for flow in flows]
    scratch = [cut(len(flow.scratch)) for flow in flows]
    partners = []
    for flow in flows:
        partners += [flips for flips in flow.flips if flips not in partners]
    barrier = pltpu.get_barrier_semaphore()
    for flips in partners:
        pl.semaphore_signal(
            barrier, inc=1, device_id=toward(flips), device_id_type=pl.DeviceIdType.MESH
        )
    pl.semaphore_wait(barrier, len(partners))
    for flow, *parts in zip(flows, operands, results, scratch):
        flow.refs = parts
    tasks = [part for part in zip(flows, operands, results, scratch) if isinstance(part[0], Task)]
    runs = [
        flow.run(*parts)
        for flow, *parts in zip(flows, operands, results, scratch)
        if not isinstance(flow, Task)
    ]
    for run in runs:
        next(run)
    for number in plan:
        if number < 0:
            flow, *parts = tasks[-1 - number]
            flow.run(*parts)
        elif number < len(runs):
            next(runs[number], None)
    while runs:
        runs = [run for run in runs if next(run, run) is not run]


def transfer(number, flows, plan=()):
    arrays = [array for flow in flows for array in flow.operands]
    shapes = [shape for flow in flows for shape in flow.results]
    anywhere = pl.BlockSpec(memory_space=pl.ANY)
    return pl.pallas_call(
        functools.partial(flow_kernel, flows, plan),
        out_shape=shapes,
        in_specs=[anywhere] * len(arrays),
        out_specs=[anywhere] * len(shapes),
        scratch_shapes=[one for flow in flows for one in flow.scratch],
        compiler_params=pltpu.CompilerParams(
            collective_id=number, has_side_effects=True, vmem_limit_bytes=60 * MIB
        ),
        cost_estimate=BRIEF,
    )(*arrays)


def tile_of(rows, most):
    steps = -(-rows // most)
    while rows % steps or (rows // steps) % ROW_TILE:
        steps += 1
    return rows // steps


def whole_block(shape):
    return pl.BlockSpec(shape, lambda *ids: (0,) * len(shape), pipeline_mode=pl.Buffered(1))


def expert_kernel(
    near,
    ids_ref,
    rows_ref,
    grad_ref,
    gate_ref,
    pieces_gate,
    pieces_up,
    pieces_down,
    hidden_ref,
    d_in_ref,
    d_gate_ref,
    made_ref,
    back_ref,
    in_ref,
    down_ref,
    done,
):
    @pl.when(pl.program_id(0) == 0)
    def _():
        copies = []
        half = pieces_gate.shape[3]
        for pieces, held, lo in (
            (pieces_gate, in_ref, 0),
            (pieces_up, in_ref, half),
            (pieces_down, down_ref, 0),
        ):
            amount, parts, rows, columns = pieces.shape
            for spot in range(amount):
                for part in range(parts):
                    block = (part // near * amount + spot) * near + part % near
                    copy = pltpu.make_async_copy(
                        pieces.at[spot, part],
                        held.at[pl.ds(block * rows, rows), pl.ds(lo, columns)],
                        done.at[len(copies)],
                    )
                    copy.start()
                    copies.append(copy)
        for copy in copies:
            copy.wait()

    hidden_width = down_ref.shape[0]
    gate = gate_ref[...]
    acts = dot(rows_ref[...], in_ref[...])
    d_plain = dot_nt(grad_ref[...], down_ref[...])
    act_gate, act_up = acts[:, :hidden_width], acts[:, hidden_width:]
    sigmoid = 1.0 / (1.0 + jnp.exp(-act_gate))
    silu_gate = act_gate * sigmoid
    hidden = silu_gate * act_up
    d_gate_ref[...] = jnp.sum(hidden * d_plain, axis=1, keepdims=True)
    d_hidden = d_plain * gate
    hidden_low = (hidden * gate).astype(low)
    d_act_gate = d_hidden * act_up * (sigmoid * (1.0 + act_gate * (1.0 - sigmoid)))
    d_in = jnp.concatenate([d_act_gate.astype(low), (d_hidden * silu_gate).astype(low)], axis=1)
    hidden_ref[...] = hidden_low
    d_in_ref[...] = d_in
    back_ref[...] = dot_nt(d_in, in_ref[...]).astype(low)
    made_ref[...] = dot(hidden_low, down_ref[...]).astype(low)


def expert_rows(rows, grad_rows, gate, pieces, near, ids):
    blocks, tile, model_width = rows.shape
    amount = blocks * tile
    hidden_width = pieces[0].shape[3]

    block = pl.BlockSpec((None, tile, model_width), lambda step, ids: (ids[step], 0, 0))

    def by_place(columns):
        return pl.BlockSpec((tile, columns), lambda step, ids: (ids[step], 0))

    def by_distance(columns):
        return pl.BlockSpec((tile, columns), lambda step, ids: (step, 0))

    outs = [
        (by_place, hidden_width, low),
        (by_place, 2 * hidden_width, low),
        (by_distance, 1, wide),
        (by_distance, model_width, low),
        (by_distance, model_width, low),
    ]
    anywhere = pl.BlockSpec(memory_space=pl.ANY)
    return pl.pallas_call(
        functools.partial(expert_kernel, near),
        grid_spec=pltpu.PrefetchScalarGridSpec(
            num_scalar_prefetch=1,
            grid=(blocks,),
            in_specs=[block, block, by_place(1)]
            + [anywhere] * len(pieces),
            out_specs=[spec(columns) for spec, columns, _ in outs],
            scratch_shapes=[
                pltpu.VMEM((model_width, 2 * hidden_width), low),
                pltpu.VMEM((hidden_width, model_width), low),
                sems(sum(piece.shape[0] * piece.shape[1] for piece in pieces)),
            ],
        ),
        out_shape=[jax.ShapeDtypeStruct((amount, columns), kind) for _, columns, kind in outs],
        compiler_params=pltpu.CompilerParams(vmem_limit_bytes=52 * MIB),
        cost_estimate=pl.CostEstimate(
            flops=LONG * 18 * amount * model_width * hidden_width,
            bytes_accessed=14 * amount * model_width,
            transcendentals=0,
        ),
    )(ids, rows, grad_rows, gate, *pieces)


def weight_kernel(amount, *refs):
    total = 0.0
    for left, right in zip(refs[:amount], refs[amount:-1]):
        total = total + dot_tn(left[...], right[...])
    refs[-1][...] = total.astype(low).reshape(refs[-1].shape)


def weight_grad(lefts, rights, groups=1, parts=1, tile=256):
    amount = len(lefts)
    columns, out_columns = lefts[0].shape[1], rights[0].shape[1]
    piece = columns // (groups * parts)
    tile = min(tile, piece * parts)
    if tile < piece:
        groups, parts, piece = columns // tile, 1, tile
    runs = piece * parts // tile
    return pl.pallas_call(
        functools.partial(weight_kernel, amount),
        grid=(columns // tile,),
        in_specs=[pl.BlockSpec((left.shape[0], tile), lambda step: (0, step)) for left in lefts]
        + [whole_block(right.shape) for right in rights],
        out_specs=pl.BlockSpec(
            (tile // piece, 1, piece, out_columns), lambda step: (step % runs, step // runs, 0, 0)
        ),
        out_shape=jax.ShapeDtypeStruct((parts, groups, piece, out_columns), low),
        compiler_params=pltpu.CompilerParams(vmem_limit_bytes=52 * MIB),
        cost_estimate=BRIEF,
    )(*lefts, *rights)


def widen_kernel(pieces_ref, *out_refs):
    columns = out_refs[0].shape[2]
    for number, out_ref in enumerate(out_refs):
        span = slice(number * columns, (number + 1) * columns)
        out_ref[...] = pieces_ref[:, :, span].astype(wide)


def widen_heads_kernel(parts, piece_ref, query_ref, key_ref, value_ref):
    groups, width = piece_ref.shape[0], key_ref.shape[1]
    columns = piece_ref.shape[2] - 2 * width
    piece = columns // parts
    for part in range(parts):
        for group in range(groups):
            at = (part * groups + group) * piece
            span = slice(part * piece, (part + 1) * piece)
            query_ref[:, at : at + piece] = piece_ref[group, :, span].astype(wide)
    for number, out_ref in enumerate((key_ref, value_ref)):
        span = slice(columns + number * width, columns + (number + 1) * width)
        total = piece_ref[0, :, span].astype(wide)
        for group in range(1, groups):
            total = total + piece_ref[group, :, span].astype(wide)
        out_ref[...] = total


def by_head(pieces, parts, width):
    owners, groups, rows, columns = pieces.shape
    spans = [groups * (columns - 2 * width), width, width]
    return pl.pallas_call(
        functools.partial(widen_heads_kernel, parts),
        grid=(owners,),
        in_specs=[pl.BlockSpec((None, groups, rows, columns), lambda step: (step, 0, 0, 0))],
        out_specs=[pl.BlockSpec((rows, span), lambda step: (0, step)) for span in spans],
        out_shape=[jax.ShapeDtypeStruct((rows, owners * span), wide) for span in spans],
        cost_estimate=BRIEF,
    )(pieces)


def by_expert(pieces, amount):
    team, rows, columns = pieces.shape[0], pieces.shape[-2], pieces.shape[-1]
    pieces = pieces.reshape(team, -1, rows, columns)
    groups = pieces.shape[1]
    out = (groups * team, rows, columns // amount)
    return pl.pallas_call(
        widen_kernel,
        grid=(groups, team // 4),
        in_specs=[pl.BlockSpec((4, None, rows, columns), lambda group, place: (place, group, 0, 0))],
        out_specs=[
            pl.BlockSpec((4,) + out[1:], lambda group, place: (group * (team // 4) + place, 0, 0))
        ]
        * amount,
        out_shape=[jax.ShapeDtypeStruct(out, wide)] * amount,
        cost_estimate=BRIEF,
    )(pieces)


def turned(values, cosine, sine):
    return values * cosine + pltpu.roll(values, values.shape[1] // 2, 1) * sine


def turned_back(grads, cosine, sine):
    return grads * cosine + pltpu.roll(grads * sine, grads.shape[1] // 2, 1)


def head_scale(values):
    return lax.rsqrt(jnp.mean(values * values, axis=1, keepdims=True) + epsilon)


def prep_kernel(
    heads,
    rows_ref,
    w_ref,
    place_ref,
    inverse_ref,
    sign_ref,
    gain_q,
    gain_k,
    lin_ref,
    query_ref,
    keyed_ref,
    value_ref,
    cosine_ref,
    sine_ref,
):
    width = gain_q.shape[1]
    angle = place_ref[...].astype(wide) * inverse_ref[...]
    cosine, sine = jnp.cos(angle), jnp.sin(angle) * sign_ref[...]
    cosine_ref[...] = cosine
    sine_ref[...] = sine
    lin = dot(rows_ref[...], w_ref[...])
    lin_ref[...] = lin[:, : (heads + 1) * width]
    for head in range(heads + 1):
        span = slice(head * width, (head + 1) * width)
        values = lin[:, span]
        gain = gain_q[...] if head < heads else gain_k[...]
        made = turned(values * head_scale(values) * gain, cosine, sine).astype(low)
        if head < heads:
            query_ref[:, span] = made
        else:
            keyed_ref[...] = made
    value_ref[...] = lin[:, (heads + 1) * width :].astype(low)


def row_call(kernel, rows, tiled, fixed, outs, sums):
    tile = tile_of(rows, 256)

    def by_rows(columns):
        return pl.BlockSpec((tile, columns), lambda step: (step, 0))

    return pl.pallas_call(
        kernel,
        grid=(rows // tile,),
        in_specs=[
            whole_block(array.shape) if number in fixed else by_rows(array.shape[1])
            for number, array in enumerate(tiled)
        ],
        out_specs=[by_rows(columns) for columns, _ in outs]
        + [pl.BlockSpec((1, columns), lambda step: (0, 0)) for columns in sums],
        out_shape=[jax.ShapeDtypeStruct((rows, columns), kind) for columns, kind in outs]
        + [jax.ShapeDtypeStruct((1, columns), wide) for columns in sums],
        compiler_params=pltpu.CompilerParams(vmem_limit_bytes=48 * MIB),
        cost_estimate=BRIEF,
    )(*tiled)


def mask_tile(bias, k_place, k_segment, q_place, q_segment):
    allowed = (k_segment[...] == q_segment[0]) & (k_place[...] <= q_place[0])
    bias[...] = jnp.where(allowed, 0.0, -1e30)


def ahead_kernel(
    scale, k_place, k_segment, q_place, q_segment, q_ref, k_ref, vt_ref, mixed_ref, total_ref, bias
):
    @pl.when(pl.program_id(2) == 0)
    def _():
        mask_tile(bias, k_place.at[0], k_segment.at[0], q_place, q_segment)

    scores = dot_nt(k_ref[0], q_ref[0]) * scale + bias[...]
    row_max = jnp.max(scores, axis=0, keepdims=True)
    expd = jnp.exp(scores - row_max)
    row_total = jnp.sum(expd, axis=0, keepdims=True)
    mixed = dot(vt_ref[0], expd.astype(low)) / row_total
    mixed_ref[0] = mixed.T.astype(low)
    total_ref[0, 0] = row_max + jnp.log(row_total)


def behind_kernel(
    scale,
    k_place,
    k_segment,
    q_place,
    q_segment,
    q_ref,
    d_mixed_ref,
    k_ref,
    v_ref,
    kt_ref,
    total_ref,
    d_q_ref,
    d_k_ref,
    d_v_ref,
    bias,
):
    @pl.when(pl.program_id(2) == 0)
    def _():
        mask_tile(bias, k_place.at[0], k_segment.at[0], q_place, q_segment)

    @pl.when((pl.program_id(1) == 0) & (pl.program_id(2) == 0))
    def _():
        d_k_ref[...] = jnp.zeros_like(d_k_ref)
        d_v_ref[...] = jnp.zeros_like(d_v_ref)

    query, d_mixed = q_ref[0], d_mixed_ref[0]
    probs = jnp.exp(dot_nt(k_ref[0], query) * scale + bias[...] - total_ref[0, 0])
    d_probs = dot_nt(v_ref[0], d_mixed)
    row_dot = jnp.sum(probs * d_probs, axis=0, keepdims=True)
    d_scores = (probs * (d_probs - row_dot)).astype(low)
    d_v_ref[0] += dot(probs.astype(low), d_mixed)
    d_k_ref[0] += dot(d_scores, query)
    d_q_ref[0] = (dot(kt_ref[0], d_scores) * scale).T.astype(low)


def attention_call(kernel, marks, arrays, kinds, outs, width, scale, work):
    place, segment = marks
    seqs, length = place.shape
    tile = min(256, length)
    heads = arrays[0].shape[2] // width
    specs = {
        "query": pl.BlockSpec((1, tile, width), lambda s, i, h: (s, i, h)),
        "keys": pl.BlockSpec((1, length, width), lambda s, i, h: (s, 0, 0)),
        "flat": pl.BlockSpec((1, width, length), lambda s, i, h: (s, 0, 0)),
        "total": pl.BlockSpec((1, 1, 1, tile), lambda s, i, h: (s, h, 0, i)),
    }
    column = pl.BlockSpec((1, length, 1), lambda s, i, h: (s, 0, 0))
    row = pl.BlockSpec((1, 1, tile), lambda s, i, h: (s, 0, i))
    return pl.pallas_call(
        functools.partial(kernel, scale),
        grid=(seqs, length // tile, heads),
        in_specs=[column, column, row, row] + [specs[kind] for kind in kinds],
        out_specs=[specs[kind] for kind, _ in outs],
        out_shape=[shape for _, shape in outs],
        scratch_shapes=[pltpu.VMEM((length, tile), wide)],
        compiler_params=pltpu.CompilerParams(vmem_limit_bytes=48 * MIB),
        cost_estimate=BRIEF,
    )(place[:, :, None], segment[:, :, None], place[:, None, :], segment[:, None, :], *arrays)


def per_device(
    g_axes,
    c_axes,
    f_axes,
    tokens,
    places,
    segments,
    routes,
    w_query,
    w_key,
    w_value,
    w_out,
    w_router,
    w_gate,
    w_up,
    w_down,
    gain_attn,
    gain_ffn,
    gain_query,
    gain_key,
    cotangent,
):
    groups, parts_c, parts_f = 1 << len(g_axes), 1 << len(c_axes), 1 << len(f_axes)
    count = tokens.shape[1]
    width = gain_query.shape[0]
    model_width = tokens.shape[2]
    kv_heads = w_key.shape[1] // width // parts_c
    assert kv_heads == 1
    heads = w_query.shape[1] // width // parts_c // groups
    experts = w_gate.shape[0]
    hidden_width = w_gate.shape[2]
    scale = 1.0 / math.sqrt(width)
    rows_d = w_query.shape[0]
    rows_o = w_out.shape[0]
    rows_f = w_down.shape[1]
    pair_count = experts.bit_length() - 1 - len(g_axes) - len(c_axes)
    assert 0 <= pair_count <= len(f_axes)
    far_axes = f_axes[: len(f_axes) - pair_count]
    near_axes = f_axes[len(f_axes) - pair_count :]
    parts_near = 1 << len(near_axes)
    team_axes = c_axes + near_axes
    team = parts_c * parts_near
    own_axes = c_axes + f_axes
    plane_axes = g_axes + c_axes
    cluster_axes = g_axes + team_axes
    all_axes = g_axes + c_axes + f_axes
    all_axes_but_core = c_axes[:-1] + f_axes[::-1] + g_axes
    g_here = flat_index(g_axes)
    core = c_axes[-1:]
    plane_shape = (2,) * len(plane_axes) + (count, model_width)
    cluster_shape = (2,) * len(cluster_axes) + (count, model_width)
    turn = g_axes + c_axes[:-1]
    half = count // 2
    plane_parts = [(0, half, turn), (half, count, turn[1:] + turn[:1])]
    turn = turn + near_axes
    third = (count // 3) // ROW_TILE * ROW_TILE
    cuts = [0, count - 2 * third, count - third, count]
    cluster_parts = [
        (cuts[step], cuts[step + 1], turn[step:] + turn[:step]) for step in range(len(cuts) - 1)
    ]
    def core_last(parts):
        return [(lo, hi, order + core) for lo, hi, order in parts]

    def core_first(parts):
        return [(lo, hi, core + order) for lo, hi, order in parts]

    q_cols = heads * width
    qkv_cols = q_cols + 2 * width
    even = rows_o % (groups * width) == 0
    if even:
        own_query = w_query.reshape(rows_d, parts_c, parts_f, groups, q_cols // parts_f)
        own_query = own_query.transpose(3, 1, 0, 2, 4)
    else:
        own_query = w_query.reshape(rows_d, parts_c, groups, q_cols).transpose(2, 1, 0, 3)
    own_query = take(own_query.reshape(groups, parts_c, rows_d, q_cols), g_here)
    mine_qkv = jnp.concatenate(
        [
            own_query,
            w_key.reshape(rows_d, parts_c, width).transpose(1, 0, 2),
            w_value.reshape(rows_d, parts_c, width).transpose(1, 0, 2),
        ],
        axis=2,
    )
    wide_router = jnp.pad(w_router, ((0, 0), (0, width - experts)))
    resid = tokens[0].astype(jnp.float32)
    norm_one, back_one = jax.vjp(normed, resid, gain_attn)

    def own_expert(place):
        return flat_index(g_axes) * team + place

    mine_out = take(w_out.reshape(groups, -1, model_width), g_here) if even else w_out
    grad_parts = [(lo, hi, near_axes + order) for lo, hi, order in plane_parts]
    all_one, w_qkv, own_grads, pieces_down, w_mix, got_gate, got_up, full_router, marks = transfer(
        1,
        [
            Gather(plane_axes, norm_one.astype(low), core_last(plane_parts)),
            Spread(c_axes, f_axes, mine_qkv, (rows_d, qkv_cols)),
            Gather(turn, cotangent[0], grad_parts),
            Spread(team_axes, far_axes, w_down, w_down.shape[1:], own_expert),
            Gather(f_axes, mine_out, [(0, mine_out.shape[0], f_axes)]),
            Direct(team_axes, w_gate, w_gate.shape[1:], own_expert),
            Direct(team_axes, w_up, w_up.shape[1:], own_expert),
            Direct(own_axes, wide_router[None], wide_router.shape, lambda place: 0),
            Direct(
                g_axes,
                jnp.stack([places[0], segments[0]])[None],
                (2,) + places.shape[1:],
                lambda place: 0,
            ),
        ],
        (1, 0, 2, 3, 0, 2, 4, 1, 0),
    )
    blocks = 1 << len(turn)
    own_grads = own_grads.reshape(blocks, count, model_width)
    far_grads = lax.ppermute(own_grads, core[0], SWAP)
    w_qkv = w_qkv.reshape(model_width, qkv_cols)
    all_one = all_one.reshape(-1, model_width)
    full_router = full_router.reshape(model_width, width)[:, :experts]

    w_mix = w_mix.reshape(-1, model_width)
    if not even:
        w_mix = take(w_mix.reshape(groups, q_cols, model_width), g_here)

    def from_far(got):
        return lax.all_gather(got, far_axes, axis=0, tiled=False) if far_axes else got[None]

    pieces_gate, pieces_up = from_far(got_gate), from_far(got_up)
    pieces_down = pieces_down.reshape((team, -1) + w_down.shape[1:]).transpose(1, 0, 2, 3)
    if rows_f % ROW_TILE:
        pieces_down = pieces_down.reshape((-1, parts_c, parts_near) + w_down.shape[1:])
        pieces_down = pieces_down.transpose(1, 0, 2, 3, 4).reshape(1, 1, hidden_width, model_width)

    place, segment = marks[:, 0], marks[:, 1]
    length = place.shape[1]
    rows = groups * length
    steps = jnp.arange(width // 2).astype(wide)
    inverse = jnp.exp(steps * (-2.0 * math.log(1000000.0) / width))
    inverse = jnp.concatenate([inverse, inverse])[None]
    sign = jnp.where(jnp.arange(width) < width // 2, -1.0, 1.0)[None]
    head_gains = (gain_query[None], gain_key[None])
    lin, query_low, keyed_low, value_low, cosine, sine = row_call(
        functools.partial(prep_kernel, heads),
        rows,
        (all_one, w_qkv, place.reshape(rows, 1), inverse, sign) + head_gains,
        (1, 3, 4, 5, 6),
        [(q_cols + width, wide), (q_cols, low), (width, low), (width, low), (width, wide), (width, wide)],
        [],
    )
    query_low = query_low.reshape(groups, length, q_cols)
    keyed_low = keyed_low.reshape(groups, length, width)
    value_low = value_low.reshape(groups, length, width)
    total_shape = jax.ShapeDtypeStruct((groups, heads, 1, length), wide)
    mixed_low, log_total = attention_call(
        ahead_kernel,
        (place, segment),
        (query_low, keyed_low, value_low.transpose(0, 2, 1)),
        ("query", "keys", "flat"),
        [("query", jax.ShapeDtypeStruct(query_low.shape, low)), ("total", total_shape)],
        width,
        scale,
        4,
    )
    mixed_rows = mixed_low.reshape(groups * length, q_cols)
    branch = dot(mixed_rows, w_mix).astype(low).reshape(plane_shape)
    (branch,) = transfer(2, [Reduce(plane_axes, branch, core_first(plane_parts))])
    resid_one = resid + branch

    norm_two, back_two = jax.vjp(normed, resid_one, gain_ffn)
    normed_two = norm_two.astype(low)
    logits = dot(normed_two, full_router)
    labels = jnp.arange(experts, dtype=jnp.int32)
    chosen = jnp.any(routes[0][:, :, None] == labels[None, None, :], axis=1)
    logits = jnp.where(chosen, logits, -1e30)
    powers = jnp.where(chosen, jnp.exp(logits - jnp.max(logits, axis=-1, keepdims=True)), 0.0)
    gates = powers / jnp.sum(powers, axis=-1, keepdims=True)

    own_two, all_gates = transfer(
        3,
        [
            Gather(turn, normed_two, cluster_parts),
            Gather(cluster_axes, gates.T, [(0, experts, turn + core)]),
        ],
    )
    own_two = own_two.reshape(blocks, count, model_width)
    far_two = lax.ppermute(own_two, core[0], SWAP)
    gate_stack = take_at(all_gates, flat_index(cluster_axes), len(cluster_axes))
    core_here, core_spot = lax.axis_index(core[0]), cluster_axes.index(core[0])
    ids = jnp.bitwise_xor(jnp.arange(blocks), flat_index(turn)).astype(jnp.int32)
    sides = []
    pieces = (pieces_gate, pieces_up, pieces_down)
    for side, side_rows, side_grads in (
        (core_here, own_two, own_grads),
        (1 - core_here, far_two, far_grads),
    ):
        gate = take_at(gate_stack, side, core_spot).reshape(-1, 1)
        sides.append(expert_rows(side_rows, side_grads, gate, pieces, parts_near, ids))
        ids = ids + zero_of(sides[0][2]).astype(jnp.int32)
    hiddens, d_ins, d_gate_parts, made_parts, back_parts = zip(*sides)
    half_shape = (2,) * len(turn) + (count, model_width)
    far_made = lax.ppermute(made_parts[1], core[0], SWAP)
    far_parts = 1 << len(far_axes)
    straight = parts_near * rows_d == TILE
    d_gates = jnp.stack(d_gate_parts).reshape(experts, 1, count)
    hiddens = [part.reshape(blocks, count, hidden_width) for part in hiddens]
    d_ins = [part.reshape(blocks, count, 2 * hidden_width) for part in d_ins]
    back = [part.reshape(half_shape) for part in back_parts]
    down_task = WeightGrad(hiddens, [own_grads, far_grads])
    in_task = WeightGrad(
        [own_two, far_two], d_ins, far_parts if straight else 1, 2, room=down_task
    )
    flows = [
        ReduceBoth(turn, *back, cluster_parts, core),
        Direct(core + turn, d_gates, (1, count)),
        down_task,
        in_task,
    ]
    in_pair = len(far_axes) == 1 and parts_near * rows_f % ROW_TILE == 0
    if in_pair:
        flows.append(PairSum(far_axes[0], down_task, parts_c, parts_near * rows_f))
    d_rows_two, d_gates, part_down, part_in, *sums = transfer(4, flows, (-1, 2, 0, -2, 0, -2, 0))
    d_gates = d_gates.reshape((2,) * len(cluster_axes) + (count,))
    spots = [(core + turn).index(axis) for axis in cluster_axes]
    d_gates = d_gates.transpose(spots + [len(spots)]).reshape(experts, count).T

    reduced = zero_of(d_rows_two).astype(low)

    def to_far(part, rows, done=False):
        stack = part
        if not done:
            stack = part.reshape(parts_c, -1, parts_near, rows, part.shape[1]) + reduced
            stack = stack.transpose(1, 0, 2, 3, 4)
        stack = stack.reshape(-1, team, rows, part.shape[1])
        if not far_axes:
            return stack[0]
        return lax.psum_scatter(stack, far_axes, scatter_dimension=0, tiled=False)

    share_in = to_far(part_in, rows_d, straight)
    if in_pair:
        share_down = sums[0].reshape(team, rows_f, model_width)
    else:
        share_down = to_far(part_down, rows_f)

    d_logits = (gates * (d_gates - jnp.sum(gates * d_gates, axis=-1, keepdims=True))).astype(low)
    part_router = dot_tn(normed_two, d_logits)
    d_normed_two = d_rows_two + dot_nt(d_logits, full_router)
    d_resid_one, d_gain_ffn = back_two(d_normed_two)
    d_resid_one = d_resid_one + cotangent[0].astype(jnp.float32)
    wide_part = jnp.pad(part_router.astype(low), ((0, 0), (0, width - experts)))

    made_axes = turn[: len(turn) - len(near_axes)]
    made_shape = (2,) * len(made_axes) + (parts_near * count, model_width)
    made = (made_parts[0].reshape(made_shape), far_made.reshape(made_shape))
    made_spans = [(lo * parts_near, hi * parts_near, order) for lo, hi, order in plane_parts]
    branch_flow = Gather(plane_axes, d_resid_one.astype(low), core_last(plane_parts))
    planes = 1 << len(plane_axes)
    branch_task = Branch(lambda: branch_flow.refs[1][0], w_mix, groups, planes, count)
    behind_task = HeadsBehind(
        lambda: branch_task.refs[1][0],
        (place, segment),
        (query_low, keyed_low, value_low, keyed_low.transpose(0, 2, 1), log_total),
        scale,
    )
    out_task = WeightGrad(
        [mixed_rows.reshape(planes, count, q_cols)],
        [jax.ShapeDtypeStruct((planes, count, model_width), low)],
        source=lambda: branch_flow.refs[1][0],
    )
    _, made, _, d_query, d_keyed, d_value, part_out = transfer(
        5,
        [
            branch_flow,
            ReduceBoth(made_axes, *made, made_spans, hold=True),
            branch_task,
            behind_task,
            out_task,
        ],
        (0,) * (len(plane_axes) - 1) + (1, 0, -1) + (-2,) * groups + (1, -3, 1),
    )
    heads_back = HeadsBack(
        heads,
        scale,
        (
            d_query.reshape(rows, q_cols),
            d_keyed.reshape(rows, width),
            d_value.reshape(rows, width),
            lin,
            cosine,
            sine,
            all_one,
        ),
        w_qkv,
        head_gains + (gain_attn[None],),
        d_gain_ffn.reshape(-1, width),
        plane_axes,
    )
    pieces_tile = TILE // rows_d
    runs = parts_f // pieces_tile
    spare = len(f_axes) - (pieces_tile.bit_length() - 1)
    qkv_shape = (2,) * len(f_axes) + (parts_c * rows_d, qkv_cols)

    def qkv_place(step):
        bits = [step % runs // (runs >> (bit + 1)) % 2 for bit in range(spare)]
        return tuple(bits) + (0,) * (len(f_axes) - spare) + (step // runs, 0)

    qkv_block = (None,) * spare + (2,) * (len(f_axes) - spare) + (rows_d, qkv_cols)
    stack = (1 << len(plane_axes), count)
    qkv_task = WeightGrad(
        [all_one.reshape(stack + (model_width,))],
        [jax.ShapeDtypeStruct(stack + (qkv_cols,), low)],
        source=lambda: heads_back.refs[1][0],
        out=(qkv_shape, qkv_block, qkv_place),
    )

    turn_back = plane_axes[len(g_axes) : -1] + g_axes
    def over_groups(shape):
        return Gather(g_axes, shape, [(0, shape.shape[0], g_axes)])

    def to_column_owners(shape):
        return Spread(c_axes, g_axes, shape, shape.shape[1:])

    flows = [
        Spread(team_axes, g_axes, share_down, share_down.shape[1:]),
        Spread(team_axes, g_axes, share_in, share_in.shape[1:]),
        Fed(
            Reduce(
                plane_axes,
                heads_back.results[1],
                core_first([(lo, hi, turn_back) for lo, hi, _ in plane_parts]),
            ),
            lambda: heads_back.refs[1][1],
        ),
        Fed(
            Reduce(
                f_axes,
                qkv_task.results[0],
                [(0, parts_c * rows_d, f_axes[::-1])],
                jax.ShapeDtypeStruct((parts_c, rows_d, qkv_cols), low),
                to_column_owners,
            ),
            lambda: qkv_task.refs[1][0],
        ),
        Reduce(
            own_axes,
            wide_part.reshape((2,) * len(own_axes) + (rows_d, width)),
            [(0, rows_d, own_axes)],
            jax.ShapeDtypeStruct((rows_d, width), low),
            over_groups,
        ),
    ]
    if even:
        rows = q_cols // parts_f
        stack = part_out.reshape((2,) * len(f_axes) + (rows, model_width))
        shape = jax.ShapeDtypeStruct((rows, model_width), low)
        flows.append(Later(Reduce(f_axes, stack, [(0, rows, f_axes[::-1])], shape, over_groups)))
    if near_axes:
        near_shape = (2,) * len(near_axes) + (count, model_width)
        near_flow = Reduce(
            near_axes, made.astype(low).reshape(near_shape), [(0, count, near_axes)], by_distance=True
        )
        flows.append(Later(near_flow))
    lines = jax.ShapeDtypeStruct((heads_back.lines, width), wide)
    gains_flow = Gather(all_axes, lines, [(0, heads_back.lines, core + all_axes_but_core)])
    flows.insert(5, Fed(gains_flow, lambda: heads_back.refs[2][0]))
    flows += [heads_back, qkv_task]
    all_down, all_in, d_one, all_qkv, share_router, gains, *rest = transfer(
        7,
        flows,
        (-1, 0, 2, -2, 2, 3, 1, 6, 5, 3, 2, 6, 7, 3, 3, 6, 6, 3, 4, 5, 4, 5, 4, 5, 4, 5),
    )
    rest = rest[:-3]
    gains = jnp.sum(gains.reshape(-1, heads_back.lines * width), axis=0)
    share_router = share_router.reshape(groups, rows_d, width)[:, :, :experts]
    grad_router = jnp.sum(share_router.astype(wide), axis=0)
    if near_axes:
        made = rest.pop()
    output = (resid_one + made).astype(low)[None]
    d_resid = back_one(d_one)[0]
    grad_tokens = (d_resid + d_resid_one)[None]
    grad_down, = by_expert(all_down, 1)
    grad_gate, grad_up = by_expert(all_in, 2)
    if even:
        grad_out = rest[0].astype(wide).reshape(rows_o, model_width)
    else:
        stack = jnp.where(jnp.arange(groups)[:, None, None] == g_here, part_out[None], 0)
        share_out = lax.psum_scatter(
            stack.reshape(groups * q_cols, model_width), f_axes, scatter_dimension=0, tiled=True
        )
        grad_out = lax.psum(share_out.astype(wide), g_axes)
    grad_query, grad_key, grad_value = by_head(
        all_qkv.reshape(parts_c, groups, rows_d, qkv_cols), parts_f if even else 1, width
    )
    return (
        output,
        grad_tokens,
        grad_query,
        grad_key,
        grad_value,
        grad_out,
        grad_router,
        grad_gate,
        grad_up,
        grad_down,
        gains[:model_width],
        gains[model_width : 2 * model_width],
        gains[2 * model_width : 2 * model_width + width],
        gains[2 * model_width + width : 2 * model_width + 2 * width],
    )


def solution(mesh):
    def binary(letter, size):
        return tuple(letter + str(step) for step in range(size.bit_length() - 1))

    g_axes = binary("g", mesh.shape["grp"])
    c_axes = binary("c", mesh.shape["ctx"])
    f_axes = binary("f", mesh.shape["fsdp"])
    names = g_axes + c_axes + f_axes
    fine = Mesh(mesh.devices.reshape((2,) * len(names)), names)
    rows = P(g_axes + f_axes, c_axes, None)
    line = P(g_axes + f_axes, None)
    split = P(c_axes + f_axes, None)
    expert = P(None, c_axes + f_axes, None)
    whole = P()
    in_specs = (
        (rows, line, line, rows)
        + (split,) * 5
        + (expert,) * 3
        + (whole,) * 4
        + (rows,)
    )
    out_specs = (rows, rows) + (split,) * 5 + (expert,) * 3 + (whole,) * 4

    def device_part(*arrays):
        return per_device(g_axes, c_axes, f_axes, *arrays)

    return jax.shard_map(
        device_part, mesh=fine, in_specs=in_specs, out_specs=out_specs, check_vma=False
    )
```

```python
import functools
import itertools
import math

import jax
import jax.numpy as jnp
from jax import lax
from jax.experimental import pallas as pl
from jax.experimental.pallas import tpu as pltpu
from jax.sharding import Mesh
from jax.sharding import PartitionSpec as P

epsilon = 1e-06
low = jnp.bfloat16
wide = jnp.float32
SWAP = [(0, 1), (1, 0)]
ROW_TILE = 16
MIB = 1 << 20
TILE = 256
WAIT_LAST = 8
LONG = 16
BRIEF = pl.CostEstimate(flops=0, bytes_accessed=0, transcendentals=0)


def normed(values, gain):
    return values * lax.rsqrt(jnp.mean(values * values, axis=-1, keepdims=True) + epsilon) * gain


def dot(left, right):
    return jnp.dot(left, right, preferred_element_type=jnp.float32)


def dot_nt(left, right):
    return lax.dot_general(left, right, (((1,), (1,)), ((), ())), preferred_element_type=jnp.float32)


def dot_tn(left, right):
    return lax.dot_general(left, right, (((0,), (0,)), ((), ())), preferred_element_type=jnp.float32)


def zero_of(anchor):
    return jnp.minimum(jnp.abs(anchor[(0,) * anchor.ndim].astype(wide)), 0.0)


def flat_index(axes):
    index = 0
    for axis in axes:
        index = index * 2 + lax.axis_index(axis)
    return index


def take(stack, index):
    return lax.dynamic_index_in_dim(stack, index, 0, keepdims=False)


def take_at(stack, index, at):
    return lax.dynamic_index_in_dim(stack, index, at, keepdims=False)


def sems(amount):
    return pltpu.SemaphoreType.DMA((amount,))


def toward(flips):
    return {axis: 1 - lax.axis_index(axis) for axis in flips}


def remote(src, dst, send, recv, flips):
    return pltpu.make_async_remote_copy(
        src_ref=src,
        dst_ref=dst,
        send_sem=send,
        recv_sem=recv,
        device_id=toward(flips),
        device_id_type=pl.DeviceIdType.MESH,
    )


class Direct:
    def __init__(self, axes, operand, block, pick=None, rounds=0):
        self.axes, self.block, self.pick, self.rounds = axes, block, pick, rounds
        self.amount = 1 << len(axes)
        self.operands = [operand]
        self.results = [jax.ShapeDtypeStruct((self.amount,) + block, operand.dtype)]
        self.scratch = [
            sems(self.amount),
            sems(self.amount),
            sems(2),
            pltpu.VMEM(block, operand.dtype),
        ]
        self.steps = [
            tuple(axis for bit, axis in enumerate(reversed(axes)) if step >> bit & 1)
            for step in range(self.amount)
        ]
        self.flips = self.steps[1:]

    def begin(self, operands, target, send, recv):
        copies = []
        for step in range(1, self.amount):
            other = 0
            for axis in self.axes:
                place = lax.axis_index(axis)
                other = other * 2 + (1 - place if axis in self.steps[step] else place)
            copy = remote(
                operands[0].at[step if self.pick is None else self.pick(other)],
                target,
                send.at[step],
                recv.at[step],
                self.steps[step],
            )
            copy.start()
            copies.append(copy)
        return copies

    def keep(self, operands, target, local, held):
        own = 0 if self.pick is None else self.pick(flat_index(self.axes))
        load = pltpu.make_async_copy(operands[0].at[own], held, local.at[0])
        load.start()
        load.wait()
        store = pltpu.make_async_copy(held, target, local.at[1])
        store.start()
        store.wait()

    def run(self, operands, results, scratch):
        send, recv, local, held = scratch
        for _ in range(self.rounds):
            yield
        target = results[0].at[flat_index(self.axes)]
        copies = self.begin(operands, target, send, recv)
        self.keep(operands, target, local, held)
        for _ in range(WAIT_LAST):
            yield
        for copy in copies:
            copy.wait()


class Spread(Direct):
    def __init__(self, axes, others, operand, block, pick=lambda place: place):
        super().__init__(axes, operand, block, pick)
        self.others = others
        self.results = [
            jax.ShapeDtypeStruct((self.amount,) + (2,) * len(others) + block, operand.dtype)
        ]
        self.scratch += [sems(max(1, len(others))), sems(max(1, len(others)))]
        self.flips = self.flips + [(axis,) for axis in others]

    def run(self, operands, results, scratch):
        send, recv, local, held, next_send, next_recv = scratch
        here = flat_index(self.axes)
        place = {axis: lax.axis_index(axis) for axis in self.others}
        spot = tuple(place[axis] for axis in self.others)
        copies = self.begin(operands, results[0].at[(here,) + spot], send, recv)
        self.keep(operands, results[0].at[(here,) + spot], local, held)
        yield
        for copy in copies:
            copy.wait_recv()
        for stage, axis in enumerate(self.others):
            region = tuple(
                slice(None) if other in self.others[:stage] else place[other]
                for other in self.others
            )
            region = results[0].at[(slice(None),) + region]
            copy = remote(region, region, next_send.at[stage], next_recv.at[stage], (axis,))
            copy.start()
            yield
            copy.wait()
        for copy in copies:
            copy.wait_send()


class Gather:
    def __init__(self, axes, operand, parts):
        self.axes, self.parts = axes, parts
        self.operands = [operand]
        self.results = [
            jax.ShapeDtypeStruct((2,) * len(axes) + operand.shape, operand.dtype)
        ]
        amount = len(parts) * len(axes)
        self.scratch = [sems(amount), sems(amount), sems(2), pltpu.VMEM(operand.shape, operand.dtype)]
        self.flips = [(axis,) for axis in axes]

    def run(self, operands, results, scratch):
        send, recv, local, held = scratch
        place = {axis: lax.axis_index(axis) for axis in self.axes}
        load = pltpu.make_async_copy(operands[0], held, local.at[0])
        load.start()
        load.wait()
        spot = tuple(place[axis] for axis in self.axes)
        store = pltpu.make_async_copy(held, results[0].at[spot], local.at[1])
        store.start()
        store.wait()
        copies = {}

        def start(number, stage):
            lo, hi, order = self.parts[number]
            region = tuple(
                slice(None) if axis in order[:stage] else place[axis] for axis in self.axes
            )
            region = results[0].at[region + (pl.ds(lo, hi - lo),)]
            slot = number * len(self.axes) + stage
            copies[number, stage] = remote(
                region, region, send.at[slot], recv.at[slot], (order[stage],)
            )
            copies[number, stage].start()

        for number in range(len(self.parts)):
            start(number, 0)
        yield
        for stage in range(1, len(self.axes)):
            for number in range(len(self.parts)):
                copies[number, stage - 1].wait_recv()
                start(number, stage)
            yield
        for number in range(len(self.parts)):
            copies[number, len(self.axes) - 1].wait_recv()
        for copy in copies.values():
            copy.wait_send()


class Reduce:
    def __init__(self, axes, operand, parts, ready=None, last=None, by_distance=False):
        self.axes, self.parts, self.by_distance = axes, parts, by_distance
        count, columns = operand.shape[-2:]
        self.operands = [operand]
        self.results = [jax.ShapeDtypeStruct((count, columns), wide)]
        self.scratch = []
        for lo, hi, order in parts:
            for stage in range(len(axes)):
                left = len(axes) - 1 - stage
                self.scratch.append(pltpu.VMEM((2,) * left + (hi - lo, columns), low))
            self.scratch.append(pltpu.VMEM((2,) * (len(axes) - 1) + (hi - lo, columns), low))
        self.scratch.append(pltpu.VMEM((count, columns), wide))
        amount = len(parts) * len(axes)
        self.flips = [(axis,) for axis in axes]
        self.last = None
        if last is not None:
            self.last = last(ready)
            self.results = self.last.results
            self.flips = self.flips + self.last.flips
            self.scratch += [pltpu.VMEM(ready.shape, low)] + self.last.scratch
        self.scratch += [sems(amount), sems(amount), sems(len(parts) + 1)]

    def run(self, operands, results, scratch):
        stages = len(self.axes)
        send, recv, local = scratch[-3:]
        total = scratch[len(self.parts) * (stages + 1)]
        place = {axis: 0 if self.by_distance else lax.axis_index(axis) for axis in self.axes}
        copies, loads = {}, []

        def buffers(number):
            base = number * (stages + 1)
            return scratch[base : base + stages], scratch[base + stages]

        def start(number, stage):
            lo, hi, order = self.parts[number]
            slots, held = buffers(number)
            slot = number * stages + stage
            axis = order[stage]
            if stage == 0:
                spot = tuple(
                    1 - place[other] if other == axis else slice(None) for other in self.axes
                )
                source = operands[0].at[spot + (pl.ds(lo, hi - lo),)]
            else:
                rest = [other for other in self.axes if other != order[0]]
                spot = tuple(
                    place[other]
                    if other in order[:stage]
                    else 1 - place[other]
                    if other == axis
                    else slice(None)
                    for other in rest
                )
                source = held.at[spot]
            copies[number, stage] = remote(
                source, slots[stage], send.at[slot], recv.at[slot], (axis,)
            )
            copies[number, stage].start()

        for number, (lo, hi, order) in enumerate(self.parts):
            start(number, 0)
            spot = tuple(
                place[other] if other == order[0] else slice(None) for other in self.axes
            )
            load = pltpu.make_async_copy(
                operands[0].at[spot + (pl.ds(lo, hi - lo),)], buffers(number)[1], local.at[number]
            )
            load.start()
            loads.append(load)
        yield
        for stage in range(stages):
            for number, (lo, hi, order) in enumerate(self.parts):
                slots, held = buffers(number)
                if stage == 0:
                    loads[number].wait()
                copies[number, stage].wait_recv()
                rest = [other for other in self.axes if other != order[0]]
                gone = order[: stage + 1]
                free = [other for other in rest if other not in gone]
                for code in range(1 << len(free)):
                    bits = {axis: code >> bit & 1 for bit, axis in enumerate(free)}
                    spot = tuple(bits[axis] if axis in bits else place[axis] for axis in rest)
                    slot_spot = tuple(bits[axis] for axis in free)
                    last = stage == stages - 1

                    def add(step, carry, spot=spot, slot_spot=slot_spot, last=last):
                        rows = pl.ds(pl.multiple_of(step * ROW_TILE, ROW_TILE), ROW_TILE)
                        value = held[spot + (rows,)].astype(wide)
                        value = value + slots[stage][slot_spot + (rows,)].astype(wide)
                        if last:
                            at = pl.multiple_of(step * ROW_TILE + lo, ROW_TILE)
                            total[pl.ds(at, ROW_TILE)] = value
                        else:
                            held[spot + (rows,)] = value.astype(low)
                        return carry

                    lax.fori_loop(0, (hi - lo) // ROW_TILE, add, 0)
                if stage + 1 < stages:
                    start(number, stage + 1)
            yield
        if self.last is None:
            store = pltpu.make_async_copy(total, results[0], local.at[len(self.parts)])
            store.start()
            store.wait()
        else:
            ready, *others = scratch[len(self.parts) * (stages + 1) + 1 : -3]
            ready[...] = total[...].astype(low).reshape(ready.shape)
            yield from self.last.run([ready], results, others)
        for copy in copies.values():
            copy.wait_send()


class ReduceBoth(Reduce):
    def __init__(self, axes, operand, other, parts, first=(), hold=False):
        super().__init__(axes, operand, parts, by_distance=True)
        self.first, self.hold = first, hold
        self.flips = self.flips + [(axis,) for axis in first]
        self.operands = [operand, other]
        shape = operand.shape
        self.scratch = [pltpu.VMEM(shape, low), pltpu.VMEM(shape, low)]
        for lo, hi, order in parts:
            for stage in range(len(axes)):
                left = len(axes) - 1 - stage
                self.scratch.append(pltpu.VMEM((2,) * left + (hi - lo, shape[-1]), low))
        self.scratch.append(pltpu.VMEM(shape[-2:], wide))
        amount = len(parts) * len(axes)
        self.scratch += [sems(amount), sems(amount), sems(2 * len(parts) + 1), sems(len(parts))]

    def run(self, operands, results, scratch):
        stages = len(self.axes)
        held, added, *slots = scratch[:-5]
        total, send, recv, local, far = scratch[-5:]
        copies, loads = {}, []
        every = (slice(None),) * stages

        def start(number, stage):
            lo, hi, order = self.parts[number]
            spot = tuple(
                0 if axis in order[:stage] else 1 if axis == order[stage] else slice(None)
                for axis in self.axes
            )
            slot = number * stages + stage
            copies[number, stage] = remote(
                held.at[spot + (pl.ds(lo, hi - lo),)],
                slots[slot],
                send.at[slot],
                recv.at[slot],
                (order[stage],),
            )
            copies[number, stage].start()

        def add_all(lo, hi, free, spot_of, source, last):
            for code in range(1 << len(free)):
                bits = {axis: code >> bit & 1 for bit, axis in enumerate(free)}
                spot = tuple(bits.get(axis, 0) for axis in self.axes)
                source_spot = spot_of(bits)

                def add(step, carry, spot=spot, source_spot=source_spot):
                    at = pl.multiple_of(step * ROW_TILE, ROW_TILE)
                    rows = pl.ds(pl.multiple_of(at + lo, ROW_TILE), ROW_TILE)
                    value = held[spot + (rows,)].astype(wide)
                    shift = rows if source is added else pl.ds(at, ROW_TILE)
                    value = value + source[source_spot + (shift,)].astype(wide)
                    if last:
                        total[rows] = value
                    else:
                        held[spot + (rows,)] = value.astype(low)
                    return carry

                lax.fori_loop(0, (hi - lo) // ROW_TILE, add, 0)

        for number, (lo, hi, order) in enumerate(self.parts):
            span = every + (pl.ds(lo, hi - lo),)
            for which, (operand, buffer) in enumerate(zip(operands, (held, added))):
                if which and self.first:
                    load = remote(
                        operand.at[span],
                        added.at[span],
                        far.at[number],
                        local.at[2 * number + which],
                        self.first,
                    )
                else:
                    load = pltpu.make_async_copy(
                        operand.at[span], buffer.at[span], local.at[2 * number + which]
                    )
                load.start()
                loads.append(load)
        if self.first:
            yield
        for number, (lo, hi, order) in enumerate(self.parts):
            loads[2 * number].wait()
            loads[2 * number + 1].wait()
            add_all(
                lo, hi, self.axes, lambda bits: tuple(bits[axis] for axis in self.axes), added, False
            )
            if not self.hold:
                start(number, 0)
        yield
        if self.hold:
            for number in range(len(self.parts)):
                start(number, 0)
            yield
        for stage in range(stages):
            for number, (lo, hi, order) in enumerate(self.parts):
                copies[number, stage].wait_recv()
                free = [axis for axis in self.axes if axis not in order[: stage + 1]]
                add_all(
                    lo,
                    hi,
                    free,
                    lambda bits, free=free: tuple(bits[axis] for axis in free),
                    slots[number * stages + stage],
                    stage == stages - 1,
                )
                if stage + 1 < stages:
                    start(number, stage + 1)
            yield
        store = pltpu.make_async_copy(total, results[0], local.at[2 * len(self.parts)])
        store.start()
        store.wait()
        for copy in copies.values():
            copy.wait_send()


class Later:
    def __init__(self, flow):
        self.flow, self.flips = flow, flow.flips
        self.operands, self.results, self.scratch = flow.operands, flow.results, flow.scratch

    def run(self, *parts):
        yield
        yield from self.flow.run(*parts)


class Fed(Later):
    def __init__(self, flow, source):
        super().__init__(flow)
        self.source, self.operands = source, []

    def run(self, operands, results, scratch):
        yield
        yield from self.flow.run([self.source()], results, scratch)


class PairSum:
    def __init__(self, axis, task, groups, rows):
        self.axis, self.task, self.groups, self.rows = axis, task, groups, rows
        shape = (groups, rows, task.width)
        self.operands, self.flips = [], [(axis,)]
        self.results = [jax.ShapeDtypeStruct(shape, low)]
        self.scratch = [pltpu.VMEM(shape, low), pltpu.VMEM(shape, low)]
        self.scratch += [sems(groups), sems(groups), sems(groups + 1)]

    def run(self, operands, results, scratch):
        held, added, send, recv, local = scratch
        source, place = self.task.refs[1][0], lax.axis_index(self.axis)
        yield

        def part(group, whose):
            at = pl.multiple_of((group * 2 + whose) * self.rows, self.rows)
            return source.at[pl.ds(at, self.rows)]

        copies = []
        for group in range(self.groups):
            copy = remote(
                part(group, 1 - place), added.at[group], send.at[group], recv.at[group], (self.axis,)
            )
            load = pltpu.make_async_copy(part(group, place), held.at[group], local.at[group])
            copy.start()
            load.start()
            copies += [copy, load]
        yield
        for copy in copies:
            copy.wait()
        for group in range(self.groups):

            def add(step, carry, group=group):
                at = pl.ds(pl.multiple_of(step * ROW_TILE, ROW_TILE), ROW_TILE)
                value = held[group, at].astype(wide) + added[group, at].astype(wide)
                held[group, at] = value.astype(low)
                return carry

            lax.fori_loop(0, self.rows // ROW_TILE, add, 0)
        store = pltpu.make_async_copy(held, results[0], local.at[self.groups])
        store.start()
        store.wait()


class Task:
    flips = ()


def bit_spots(blocks):
    return list(itertools.product((0, 1), repeat=blocks.bit_length() - 1))


def bits_of(step, blocks):
    amount = blocks.bit_length() - 1
    return tuple(step // (blocks >> (bit + 1)) % 2 for bit in range(amount))


class Branch(Task):
    def __init__(self, source, w_mix, seqs, blocks, count):
        self.source, self.seqs, self.blocks, self.count = source, seqs, blocks, count
        self.columns, self.model_width = w_mix.shape
        self.operands = [w_mix]
        shape = (seqs, blocks // seqs * count, self.columns)
        self.results = [jax.ShapeDtypeStruct(shape, low)]
        self.scratch = [pltpu.VMEM(w_mix.shape, low), sems(1)]

    def run(self, operands, results, scratch):
        w_ref, done = scratch
        copy = pltpu.make_async_copy(operands[0], w_ref, done.at[0])
        copy.start()
        copy.wait()
        each = self.blocks // self.seqs

        def body(rows_ref, out_ref):
            out_ref[...] = dot_nt(rows_ref[...], w_ref[...]).astype(low)

        free = (None,) * (self.blocks.bit_length() - 1)
        pltpu.emit_pipeline(
            body,
            grid=(self.blocks,),
            in_specs=[
                pl.BlockSpec(
                    free + (self.count, self.model_width),
                    lambda step: bits_of(step, self.blocks) + (0, 0),
                )
            ],
            out_specs=[
                pl.BlockSpec(
                    (None, self.count, self.columns), lambda step: (step // each, step % each, 0)
                )
            ],
        )(self.source(), results[0])


class HeadsBehind(Task):
    def __init__(self, source, marks, arrays, scale, tile=256):
        self.source, self.scale, self.tile, self.calls = source, scale, tile, 0
        place, segment = marks
        query, keyed = arrays[:2]
        self.seqs, self.length, columns = query.shape
        self.width = keyed.shape[2]
        self.heads = columns // self.width
        self.operands = [place[:, :, None], segment[:, :, None], place[:, None], segment[:, None]]
        self.operands += list(arrays)
        self.results = [
            jax.ShapeDtypeStruct(query.shape, low),
            jax.ShapeDtypeStruct(keyed.shape, wide),
            jax.ShapeDtypeStruct(keyed.shape, wide),
        ]
        total = pltpu.VMEM((self.length, self.width), wide)
        self.scratch = [pltpu.VMEM((self.length, tile), wide), total, total]

    def run(self, operands, results, scratch):
        bias, d_k_total, d_v_total = scratch
        seq = self.calls
        self.calls = (self.calls + 1) % self.seqs
        tiles = self.length // self.tile
        d_k_total[...] = jnp.zeros_like(d_k_total)
        d_v_total[...] = jnp.zeros_like(d_v_total)

        def body(
            k_place,
            k_segment,
            q_place,
            q_segment,
            q_ref,
            k_ref,
            v_ref,
            kt_ref,
            total_ref,
            d_mixed_ref,
            d_q_ref,
            d_k_ref,
            d_v_ref,
        ):
            at, head = pl.program_id(0), pl.program_id(1)

            @pl.when(head == 0)
            def _():
                allowed = (k_segment[...] == q_segment[...]) & (k_place[...] <= q_place[...])
                bias[...] = jnp.where(allowed, 0.0, -1e30)

            query, d_mixed = q_ref[...], d_mixed_ref[...]
            probs = jnp.exp(dot_nt(k_ref[...], query) * self.scale + bias[...] - total_ref[...])
            d_probs = dot_nt(v_ref[...], d_mixed)
            row_dot = jnp.sum(probs * d_probs, axis=0, keepdims=True)
            d_scores = (probs * (d_probs - row_dot)).astype(low)
            d_v_total[...] += dot(probs.astype(low), d_mixed)
            d_k_total[...] += dot(d_scores, query)
            d_q_ref[...] = (dot(kt_ref[...], d_scores) * self.scale).T.astype(low)

            @pl.when((at == tiles - 1) & (head == self.heads - 1))
            def _():
                d_k_ref[...] = d_k_total[...]
                d_v_ref[...] = d_v_total[...]

        column = pl.BlockSpec((None, self.length, 1), lambda i, h: (seq, 0, 0))
        row = pl.BlockSpec((None, 1, self.tile), lambda i, h: (seq, 0, i))
        query = pl.BlockSpec((None, self.tile, self.width), lambda i, h: (seq, i, h))
        keys = pl.BlockSpec((None, self.length, self.width), lambda i, h: (seq, 0, 0))
        flat = pl.BlockSpec((None, self.width, self.length), lambda i, h: (seq, 0, 0))
        total = pl.BlockSpec((None, None, 1, self.tile), lambda i, h: (seq, h, 0, i))
        pltpu.emit_pipeline(
            body,
            grid=(tiles, self.heads),
            in_specs=[column, column, row, row, query, keys, keys, flat, total, query],
            out_specs=[query, keys, keys],
        )(*operands, self.source(), *results)


class WeightGrad(Task):
    def __init__(self, lefts, rights, turns=1, pieces=1, source=None, out=None, room=None):
        self.amount, self.turns, self.pieces, self.calls = len(lefts), turns, pieces, 0
        self.source, self.room = source, room
        self.operands = list(lefts) + (list(rights) if source is None else [])
        self.blocks, self.rows, self.columns = lefts[0].shape
        self.width = rights[0].shape[-1]
        self.out = out or ((self.columns, self.width), (TILE, self.width), self.place)
        self.results = [jax.ShapeDtypeStruct(self.out[0], low)]
        shape = (self.amount, self.blocks, self.rows, self.width)
        self.scratch = [sems(max(self.amount, self.blocks))] + ([] if room else [pltpu.VMEM(shape, low)])

    def run(self, operands, results, scratch):
        done = scratch[0]
        held = self.room.refs[2][1] if self.room else scratch[1]
        span = slice(0, self.width)
        if self.calls == 0:
            rights = operands[self.amount :] if self.source is None else [self.source()]
            copies = [
                pltpu.make_async_copy(
                    right, held.at[number, :, :, pl.ds(0, self.width)], done.at[number]
                )
                for number, right in enumerate(rights)
                if len(right.shape) == 3
            ]
            if not copies:
                copies = [
                    pltpu.make_async_copy(rights[0].at[bits], held.at[0, number], done.at[number])
                    for number, bits in enumerate(bit_spots(self.blocks))
                ]
            for copy in copies:
                copy.start()
            for copy in copies:
                copy.wait()
        share = self.columns // TILE // self.pieces
        first = self.calls * share
        self.calls = (self.calls + 1) % self.pieces

        def body(*refs):
            total = 0.0
            for number, left_ref in enumerate(refs[:-1]):
                right = held[number, :, :, span].reshape(-1, self.width)
                total = total + dot_tn(left_ref[...].reshape(-1, TILE), right)
            refs[-1][...] = total.astype(low).reshape(refs[-1].shape)

        block = pl.BlockSpec((self.blocks, self.rows, TILE), lambda step: (0, 0, step + first))
        pltpu.emit_pipeline(
            body,
            grid=(share,),
            in_specs=[block] * self.amount,
            out_specs=[pl.BlockSpec(self.out[1], lambda step: self.out[2](step + first))],
        )(*operands[: self.amount], results[0])

    def place(self, step):
        steps = self.columns // TILE
        return (step % self.turns * (steps // self.turns) + step // self.turns, 0)


class HeadsBack(Task):
    def __init__(self, heads, scale, tiled, w_qkv, gains, ffn_lines, axes):
        self.heads, self.scale, self.axes = heads, scale, axes
        self.operands = list(tiled) + [w_qkv, ffn_lines] + list(gains)
        self.tiled = len(tiled)
        self.rows, self.width = tiled[1].shape
        self.model_width, self.columns = w_qkv.shape
        self.blocks = 1 << len(axes)
        self.tile = self.rows // self.blocks
        self.results = [
            jax.ShapeDtypeStruct((self.blocks, self.tile, self.columns), low),
            jax.ShapeDtypeStruct((2,) * len(axes) + (self.tile, self.model_width), low),
        ]
        own, ffn = self.model_width // self.width, ffn_lines.shape[0]
        self.lines = -(-(own + ffn + 2) // 8) * 8
        row = pltpu.VMEM((1, self.width), wide)
        long_row = pltpu.VMEM((1, self.model_width), wide)
        self.scratch = [pltpu.VMEM((self.lines, self.width), wide), pltpu.VMEM(w_qkv.shape, low)]
        self.scratch += [row, row, long_row, row, row, long_row, sems(5)]

    def run(self, operands, results, scratch):
        lines, w_ref, gain_q, gain_k, gain, d_gain_q, d_gain_k, d_gain, done = scratch
        w_hbm, ffn, *gains = operands[self.tiled :]
        own, count = self.model_width // self.width, ffn.shape[0]
        lines[...] = jnp.zeros_like(lines)
        targets = [w_ref, lines.at[pl.ds(own, count)], gain_q, gain_k, gain]
        copies = [
            pltpu.make_async_copy(source, target, done.at[number])
            for number, (source, target) in enumerate(zip([w_hbm, ffn] + gains, targets))
        ]
        for copy in copies:
            copy.start()
        for copy in copies:
            copy.wait()
        for total in (d_gain_q, d_gain_k, d_gain):
            total[...] = jnp.zeros_like(total)

        def body(
            d_query_ref,
            d_keyed_ref,
            d_value_ref,
            lin_ref,
            cosine_ref,
            sine_ref,
            rows_ref,
            d_lin_ref,
            d_one_ref,
        ):
            cosine, sine = cosine_ref[...], sine_ref[...]
            for head in range(self.heads + 1):
                span = slice(head * self.width, (head + 1) * self.width)
                values = lin_ref[:, span]
                if head < self.heads:
                    grads, own_gain, d_head = d_query_ref[:, span].astype(wide), gain_q, d_gain_q
                else:
                    grads, own_gain, d_head = d_keyed_ref[...] * self.scale, gain_k, d_gain_k
                grads = turned_back(grads, cosine, sine)
                factor = head_scale(values)
                plain = values * factor
                d_head[...] += jnp.sum(grads * plain, axis=0, keepdims=True)
                grads = grads * own_gain[...]
                mean = jnp.mean(grads * plain, axis=1, keepdims=True)
                d_lin_ref[:, span] = (factor * (grads - plain * mean)).astype(low)
            d_lin_ref[:, (self.heads + 1) * self.width :] = d_value_ref[...].astype(low)
            d_one = dot_nt(d_lin_ref[...], w_ref[...])
            d_one_ref[...] = d_one.astype(low)
            share = jnp.sum(d_one * rows_ref[...].astype(wide), axis=0, keepdims=True)
            d_gain[...] += share / gain[...]

        def by_bits(step):
            bits = [step // (self.blocks >> (bit + 1)) % 2 for bit in range(len(self.axes))]
            return tuple(bits) + (0, 0)

        pltpu.emit_pipeline(
            body,
            grid=(self.blocks,),
            in_specs=[
                pl.BlockSpec((self.tile, array.shape[1]), lambda step: (step, 0))
                for array in operands[: self.tiled]
            ],
            out_specs=[
                pl.BlockSpec((None, self.tile, self.columns), lambda step: (step, 0, 0)),
                pl.BlockSpec((None,) * len(self.axes) + (self.tile, self.model_width), by_bits),
            ],
        )(*operands[: self.tiled], *results)
        for line in range(own):
            lines[line : line + 1] = d_gain[:, line * self.width : (line + 1) * self.width]
        lines[own + count : own + count + 1] = d_gain_q[...]
        lines[own + count + 1 : own + count + 2] = d_gain_k[...]


def flow_kernel(flows, plan, *refs):
    refs = list(refs)

    def cut(amount):
        part = refs[:amount]
        del refs[:amount]
        return part

    operands = [cut(len(flow.operands)) for flow in flows]
    results = [cut(len(flow.results)) for flow in flows]
    scratch = [cut(len(flow.scratch)) for flow in flows]
    partners = []
    for flow in flows:
        partners += [flips for flips in flow.flips if flips not in partners]
    barrier = pltpu.get_barrier_semaphore()
    for flips in partners:
        pl.semaphore_signal(
            barrier, inc=1, device_id=toward(flips), device_id_type=pl.DeviceIdType.MESH
        )
    pl.semaphore_wait(barrier, len(partners))
    for flow, *parts in zip(flows, operands, results, scratch):
        flow.refs = parts
    tasks = [part for part in zip(flows, operands, results, scratch) if isinstance(part[0], Task)]
    runs = [
        flow.run(*parts)
        for flow, *parts in zip(flows, operands, results, scratch)
        if not isinstance(flow, Task)
    ]
    for run in runs:
        next(run)
    for number in plan:
        if number < 0:
            flow, *parts = tasks[-1 - number]
            flow.run(*parts)
        elif number < len(runs):
            next(runs[number], None)
    while runs:
        runs = [run for run in runs if next(run, run) is not run]


def transfer(number, flows, plan=()):
    arrays = [array for flow in flows for array in flow.operands]
    shapes = [shape for flow in flows for shape in flow.results]
    anywhere = pl.BlockSpec(memory_space=pl.ANY)
    return pl.pallas_call(
        functools.partial(flow_kernel, flows, plan),
        out_shape=shapes,
        in_specs=[anywhere] * len(arrays),
        out_specs=[anywhere] * len(shapes),
        scratch_shapes=[one for flow in flows for one in flow.scratch],
        compiler_params=pltpu.CompilerParams(
            collective_id=number, has_side_effects=True, vmem_limit_bytes=60 * MIB
        ),
        cost_estimate=BRIEF,
    )(*arrays)


def tile_of(rows, most):
    steps = -(-rows // most)
    while rows % steps or (rows // steps) % ROW_TILE:
        steps += 1
    return rows // steps


def whole_block(shape):
    return pl.BlockSpec(shape, lambda *ids: (0,) * len(shape), pipeline_mode=pl.Buffered(1))


def expert_kernel(
    near,
    ids_ref,
    rows_ref,
    grad_ref,
    gate_ref,
    pieces_gate,
    pieces_up,
    pieces_down,
    hidden_ref,
    d_in_ref,
    d_gate_ref,
    made_ref,
    back_ref,
    in_ref,
    down_ref,
    done,
):
    @pl.when(pl.program_id(0) == 0)
    def _():
        copies = []
        half = pieces_gate.shape[3]
        for pieces, held, lo in (
            (pieces_gate, in_ref, 0),
            (pieces_up, in_ref, half),
            (pieces_down, down_ref, 0),
        ):
            amount, parts, rows, columns = pieces.shape
            for spot in range(amount):
                for part in range(parts):
                    block = (part // near * amount + spot) * near + part % near
                    copy = pltpu.make_async_copy(
                        pieces.at[spot, part],
                        held.at[pl.ds(block * rows, rows), pl.ds(lo, columns)],
                        done.at[len(copies)],
                    )
                    copy.start()
                    copies.append(copy)
        for copy in copies:
            copy.wait()

    hidden_width = down_ref.shape[0]
    gate = gate_ref[...]
    acts = dot(rows_ref[...], in_ref[...])
    d_plain = dot_nt(grad_ref[...], down_ref[...])
    act_gate, act_up = acts[:, :hidden_width], acts[:, hidden_width:]
    sigmoid = 1.0 / (1.0 + jnp.exp(-act_gate))
    silu_gate = act_gate * sigmoid
    hidden = silu_gate * act_up
    d_gate_ref[...] = jnp.sum(hidden * d_plain, axis=1, keepdims=True)
    d_hidden = d_plain * gate
    hidden_low = (hidden * gate).astype(low)
    d_act_gate = d_hidden * act_up * (sigmoid * (1.0 + act_gate * (1.0 - sigmoid)))
    d_in = jnp.concatenate([d_act_gate.astype(low), (d_hidden * silu_gate).astype(low)], axis=1)
    hidden_ref[...] = hidden_low
    d_in_ref[...] = d_in
    back_ref[...] = dot_nt(d_in, in_ref[...]).astype(low)
    made_ref[...] = dot(hidden_low, down_ref[...]).astype(low)


def expert_rows(rows, grad_rows, gate, pieces, near, ids):
    blocks, tile, model_width = rows.shape
    amount = blocks * tile
    hidden_width = pieces[0].shape[3]

    block = pl.BlockSpec((None, tile, model_width), lambda step, ids: (ids[step], 0, 0))

    def by_place(columns):
        return pl.BlockSpec((tile, columns), lambda step, ids: (ids[step], 0))

    def by_distance(columns):
        return pl.BlockSpec((tile, columns), lambda step, ids: (step, 0))

    outs = [
        (by_place, hidden_width, low),
        (by_place, 2 * hidden_width, low),
        (by_distance, 1, wide),
        (by_distance, model_width, low),
        (by_distance, model_width, low),
    ]
    anywhere = pl.BlockSpec(memory_space=pl.ANY)
    return pl.pallas_call(
        functools.partial(expert_kernel, near),
        grid_spec=pltpu.PrefetchScalarGridSpec(
            num_scalar_prefetch=1,
            grid=(blocks,),
            in_specs=[block, block, by_place(1)]
            + [anywhere] * len(pieces),
            out_specs=[spec(columns) for spec, columns, _ in outs],
            scratch_shapes=[
                pltpu.VMEM((model_width, 2 * hidden_width), low),
                pltpu.VMEM((hidden_width, model_width), low),
                sems(sum(piece.shape[0] * piece.shape[1] for piece in pieces)),
            ],
        ),
        out_shape=[jax.ShapeDtypeStruct((amount, columns), kind) for _, columns, kind in outs],
        compiler_params=pltpu.CompilerParams(vmem_limit_bytes=52 * MIB),
        cost_estimate=pl.CostEstimate(
            flops=LONG * 18 * amount * model_width * hidden_width,
            bytes_accessed=14 * amount * model_width,
            transcendentals=0,
        ),
    )(ids, rows, grad_rows, gate, *pieces)


def weight_kernel(amount, *refs):
    total = 0.0
    for left, right in zip(refs[:amount], refs[amount:-1]):
        total = total + dot_tn(left[...], right[...])
    refs[-1][...] = total.astype(low).reshape(refs[-1].shape)


def weight_grad(lefts, rights, groups=1, parts=1, tile=256):
    amount = len(lefts)
    columns, out_columns = lefts[0].shape[1], rights[0].shape[1]
    piece = columns // (groups * parts)
    tile = min(tile, piece * parts)
    if tile < piece:
        groups, parts, piece = columns // tile, 1, tile
    runs = piece * parts // tile
    return pl.pallas_call(
        functools.partial(weight_kernel, amount),
        grid=(columns // tile,),
        in_specs=[pl.BlockSpec((left.shape[0], tile), lambda step: (0, step)) for left in lefts]
        + [whole_block(right.shape) for right in rights],
        out_specs=pl.BlockSpec(
            (tile // piece, 1, piece, out_columns), lambda step: (step % runs, step // runs, 0, 0)
        ),
        out_shape=jax.ShapeDtypeStruct((parts, groups, piece, out_columns), low),
        compiler_params=pltpu.CompilerParams(vmem_limit_bytes=52 * MIB),
        cost_estimate=BRIEF,
    )(*lefts, *rights)


def widen_kernel(pieces_ref, *out_refs):
    columns = out_refs[0].shape[2]
    for number, out_ref in enumerate(out_refs):
        span = slice(number * columns, (number + 1) * columns)
        out_ref[...] = pieces_ref[:, :, span].astype(wide)


def widen_heads_kernel(parts, piece_ref, query_ref, key_ref, value_ref):
    groups, width = piece_ref.shape[0], key_ref.shape[1]
    columns = piece_ref.shape[2] - 2 * width
    piece = columns // parts
    for part in range(parts):
        for group in range(groups):
            at = (part * groups + group) * piece
            span = slice(part * piece, (part + 1) * piece)
            query_ref[:, at : at + piece] = piece_ref[group, :, span].astype(wide)
    for number, out_ref in enumerate((key_ref, value_ref)):
        span = slice(columns + number * width, columns + (number + 1) * width)
        total = piece_ref[0, :, span].astype(wide)
        for group in range(1, groups):
            total = total + piece_ref[group, :, span].astype(wide)
        out_ref[...] = total


def by_head(pieces, parts, width):
    owners, groups, rows, columns = pieces.shape
    spans = [groups * (columns - 2 * width), width, width]
    return pl.pallas_call(
        functools.partial(widen_heads_kernel, parts),
        grid=(owners,),
        in_specs=[pl.BlockSpec((None, groups, rows, columns), lambda step: (step, 0, 0, 0))],
        out_specs=[pl.BlockSpec((rows, span), lambda step: (0, step)) for span in spans],
        out_shape=[jax.ShapeDtypeStruct((rows, owners * span), wide) for span in spans],
        cost_estimate=BRIEF,
    )(pieces)


def by_expert(pieces, amount):
    team, rows, columns = pieces.shape[0], pieces.shape[-2], pieces.shape[-1]
    pieces = pieces.reshape(team, -1, rows, columns)
    groups = pieces.shape[1]
    out = (groups * team, rows, columns // amount)
    return pl.pallas_call(
        widen_kernel,
        grid=(groups, team // 4),
        in_specs=[pl.BlockSpec((4, None, rows, columns), lambda group, place: (place, group, 0, 0))],
        out_specs=[
            pl.BlockSpec((4,) + out[1:], lambda group, place: (group * (team // 4) + place, 0, 0))
        ]
        * amount,
        out_shape=[jax.ShapeDtypeStruct(out, wide)] * amount,
        cost_estimate=BRIEF,
    )(pieces)


def turned(values, cosine, sine):
    return values * cosine + pltpu.roll(values, values.shape[1] // 2, 1) * sine


def turned_back(grads, cosine, sine):
    return grads * cosine + pltpu.roll(grads * sine, grads.shape[1] // 2, 1)


def head_scale(values):
    return lax.rsqrt(jnp.mean(values * values, axis=1, keepdims=True) + epsilon)


def prep_kernel(
    heads,
    rows_ref,
    w_ref,
    place_ref,
    inverse_ref,
    sign_ref,
    gain_q,
    gain_k,
    lin_ref,
    query_ref,
    keyed_ref,
    value_ref,
    cosine_ref,
    sine_ref,
):
    width = gain_q.shape[1]
    angle = place_ref[...].astype(wide) * inverse_ref[...]
    cosine, sine = jnp.cos(angle), jnp.sin(angle) * sign_ref[...]
    cosine_ref[...] = cosine
    sine_ref[...] = sine
    lin = dot(rows_ref[...], w_ref[...])
    lin_ref[...] = lin[:, : (heads + 1) * width]
    for head in range(heads + 1):
        span = slice(head * width, (head + 1) * width)
        values = lin[:, span]
        gain = gain_q[...] if head < heads else gain_k[...]
        made = turned(values * head_scale(values) * gain, cosine, sine).astype(low)
        if head < heads:
            query_ref[:, span] = made
        else:
            keyed_ref[...] = made
    value_ref[...] = lin[:, (heads + 1) * width :].astype(low)


def row_call(kernel, rows, tiled, fixed, outs, sums):
    tile = tile_of(rows, 256)

    def by_rows(columns):
        return pl.BlockSpec((tile, columns), lambda step: (step, 0))

    return pl.pallas_call(
        kernel,
        grid=(rows // tile,),
        in_specs=[
            whole_block(array.shape) if number in fixed else by_rows(array.shape[1])
            for number, array in enumerate(tiled)
        ],
        out_specs=[by_rows(columns) for columns, _ in outs]
        + [pl.BlockSpec((1, columns), lambda step: (0, 0)) for columns in sums],
        out_shape=[jax.ShapeDtypeStruct((rows, columns), kind) for columns, kind in outs]
        + [jax.ShapeDtypeStruct((1, columns), wide) for columns in sums],
        compiler_params=pltpu.CompilerParams(vmem_limit_bytes=48 * MIB),
        cost_estimate=BRIEF,
    )(*tiled)


def mask_tile(bias, k_place, k_segment, q_place, q_segment):
    allowed = (k_segment[...] == q_segment[0]) & (k_place[...] <= q_place[0])
    bias[...] = jnp.where(allowed, 0.0, -1e30)


def ahead_kernel(
    scale, k_place, k_segment, q_place, q_segment, q_ref, k_ref, vt_ref, mixed_ref, total_ref, bias
):
    @pl.when(pl.program_id(2) == 0)
    def _():
        mask_tile(bias, k_place.at[0], k_segment.at[0], q_place, q_segment)

    scores = dot_nt(k_ref[0], q_ref[0]) * scale + bias[...]
    row_max = jnp.max(scores, axis=0, keepdims=True)
    expd = jnp.exp(scores - row_max)
    row_total = jnp.sum(expd, axis=0, keepdims=True)
    mixed = dot(vt_ref[0], expd.astype(low)) / row_total
    mixed_ref[0] = mixed.T.astype(low)
    total_ref[0, 0] = row_max + jnp.log(row_total)


def behind_kernel(
    scale,
    k_place,
    k_segment,
    q_place,
    q_segment,
    q_ref,
    d_mixed_ref,
    k_ref,
    v_ref,
    kt_ref,
    total_ref,
    d_q_ref,
    d_k_ref,
    d_v_ref,
    bias,
):
    @pl.when(pl.program_id(2) == 0)
    def _():
        mask_tile(bias, k_place.at[0], k_segment.at[0], q_place, q_segment)

    @pl.when((pl.program_id(1) == 0) & (pl.program_id(2) == 0))
    def _():
        d_k_ref[...] = jnp.zeros_like(d_k_ref)
        d_v_ref[...] = jnp.zeros_like(d_v_ref)

    query, d_mixed = q_ref[0], d_mixed_ref[0]
    probs = jnp.exp(dot_nt(k_ref[0], query) * scale + bias[...] - total_ref[0, 0])
    d_probs = dot_nt(v_ref[0], d_mixed)
    row_dot = jnp.sum(probs * d_probs, axis=0, keepdims=True)
    d_scores = (probs * (d_probs - row_dot)).astype(low)
    d_v_ref[0] += dot(probs.astype(low), d_mixed)
    d_k_ref[0] += dot(d_scores, query)
    d_q_ref[0] = (dot(kt_ref[0], d_scores) * scale).T.astype(low)


def attention_call(kernel, marks, arrays, kinds, outs, width, scale, work):
    place, segment = marks
    seqs, length = place.shape
    tile = min(256, length)
    heads = arrays[0].shape[2] // width
    specs = {
        "query": pl.BlockSpec((1, tile, width), lambda s, i, h: (s, i, h)),
        "keys": pl.BlockSpec((1, length, width), lambda s, i, h: (s, 0, 0)),
        "flat": pl.BlockSpec((1, width, length), lambda s, i, h: (s, 0, 0)),
        "total": pl.BlockSpec((1, 1, 1, tile), lambda s, i, h: (s, h, 0, i)),
    }
    column = pl.BlockSpec((1, length, 1), lambda s, i, h: (s, 0, 0))
    row = pl.BlockSpec((1, 1, tile), lambda s, i, h: (s, 0, i))
    return pl.pallas_call(
        functools.partial(kernel, scale),
        grid=(seqs, length // tile, heads),
        in_specs=[column, column, row, row] + [specs[kind] for kind in kinds],
        out_specs=[specs[kind] for kind, _ in outs],
        out_shape=[shape for _, shape in outs],
        scratch_shapes=[pltpu.VMEM((length, tile), wide)],
        compiler_params=pltpu.CompilerParams(vmem_limit_bytes=48 * MIB),
        cost_estimate=BRIEF,
    )(place[:, :, None], segment[:, :, None], place[:, None, :], segment[:, None, :], *arrays)


def per_device(
    g_axes,
    c_axes,
    f_axes,
    tokens,
    places,
    segments,
    routes,
    w_query,
    w_key,
    w_value,
    w_out,
    w_router,
    w_gate,
    w_up,
    w_down,
    gain_attn,
    gain_ffn,
    gain_query,
    gain_key,
    cotangent,
):
    groups, parts_c, parts_f = 1 << len(g_axes), 1 << len(c_axes), 1 << len(f_axes)
    count = tokens.shape[1]
    width = gain_query.shape[0]
    model_width = tokens.shape[2]
    kv_heads = w_key.shape[1] // width // parts_c
    assert kv_heads == 1
    heads = w_query.shape[1] // width // parts_c // groups
    experts = w_gate.shape[0]
    hidden_width = w_gate.shape[2]
    scale = 1.0 / math.sqrt(width)
    rows_d = w_query.shape[0]
    rows_o = w_out.shape[0]
    rows_f = w_down.shape[1]
    pair_count = experts.bit_length() - 1 - len(g_axes) - len(c_axes)
    assert 0 <= pair_count <= len(f_axes)
    far_axes = f_axes[: len(f_axes) - pair_count]
    near_axes = f_axes[len(f_axes) - pair_count :]
    parts_near = 1 << len(near_axes)
    team_axes = c_axes + near_axes
    team = parts_c * parts_near
    own_axes = c_axes + f_axes
    plane_axes = g_axes + c_axes
    cluster_axes = g_axes + team_axes
    all_axes = g_axes + c_axes + f_axes
    all_axes_but_core = c_axes[:-1] + f_axes[::-1] + g_axes
    g_here = flat_index(g_axes)
    core = c_axes[-1:]
    plane_shape = (2,) * len(plane_axes) + (count, model_width)
    cluster_shape = (2,) * len(cluster_axes) + (count, model_width)
    turn = g_axes + c_axes[:-1]
    half = count // 2
    plane_parts = [(0, half, turn), (half, count, turn[1:] + turn[:1])]
    turn = turn + near_axes
    third = (count // 3) // ROW_TILE * ROW_TILE
    cuts = [0, count - 2 * third, count - third, count]
    cluster_parts = [
        (cuts[step], cuts[step + 1], turn[step:] + turn[:step]) for step in range(len(cuts) - 1)
    ]
    def core_last(parts):
        return [(lo, hi, order + core) for lo, hi, order in parts]

    def core_first(parts):
        return [(lo, hi, core + order) for lo, hi, order in parts]

    q_cols = heads * width
    qkv_cols = q_cols + 2 * width
    even = rows_o % (groups * width) == 0
    if even:
        own_query = w_query.reshape(rows_d, parts_c, parts_f, groups, q_cols // parts_f)
        own_query = own_query.transpose(3, 1, 0, 2, 4)
    else:
        own_query = w_query.reshape(rows_d, parts_c, groups, q_cols).transpose(2, 1, 0, 3)
    own_query = take(own_query.reshape(groups, parts_c, rows_d, q_cols), g_here)
    mine_qkv = jnp.concatenate(
        [
            own_query,
            w_key.reshape(rows_d, parts_c, width).transpose(1, 0, 2),
            w_value.reshape(rows_d, parts_c, width).transpose(1, 0, 2),
        ],
        axis=2,
    )
    wide_router = jnp.pad(w_router, ((0, 0), (0, width - experts)))
    resid = tokens[0].astype(jnp.float32)
    norm_one, back_one = jax.vjp(normed, resid, gain_attn)

    def own_expert(place):
        return flat_index(g_axes) * team + place

    mine_out = take(w_out.reshape(groups, -1, model_width), g_here) if even else w_out
    grad_parts = [(lo, hi, near_axes + order) for lo, hi, order in plane_parts]
    all_one, w_qkv, own_grads, pieces_down, w_mix, got_gate, got_up, full_router, marks = transfer(
        1,
        [
            Gather(plane_axes, norm_one.astype(low), core_last(plane_parts)),
            Spread(c_axes, f_axes, mine_qkv, (rows_d, qkv_cols)),
            Gather(turn, cotangent[0], grad_parts),
            Spread(team_axes, far_axes, w_down, w_down.shape[1:], own_expert),
            Gather(f_axes, mine_out, [(0, mine_out.shape[0], f_axes)]),
            Direct(team_axes, w_gate, w_gate.shape[1:], own_expert),
            Direct(team_axes, w_up, w_up.shape[1:], own_expert),
            Direct(own_axes, wide_router[None], wide_router.shape, lambda place: 0),
            Direct(
                g_axes,
                jnp.stack([places[0], segments[0]])[None],
                (2,) + places.shape[1:],
                lambda place: 0,
            ),
        ],
        (1, 0, 2, 3, 0, 2, 4, 1, 0),
    )
    blocks = 1 << len(turn)
    own_grads = own_grads.reshape(blocks, count, model_width)
    far_grads = lax.ppermute(own_grads, core[0], SWAP)
    w_qkv = w_qkv.reshape(model_width, qkv_cols)
    all_one = all_one.reshape(-1, model_width)
    full_router = full_router.reshape(model_width, width)[:, :experts]

    w_mix = w_mix.reshape(-1, model_width)
    if not even:
        w_mix = take(w_mix.reshape(groups, q_cols, model_width), g_here)

    def from_far(got):
        return lax.all_gather(got, far_axes, axis=0, tiled=False) if far_axes else got[None]

    pieces_gate, pieces_up = from_far(got_gate), from_far(got_up)
    pieces_down = pieces_down.reshape((team, -1) + w_down.shape[1:]).transpose(1, 0, 2, 3)
    if rows_f % ROW_TILE:
        pieces_down = pieces_down.reshape((-1, parts_c, parts_near) + w_down.shape[1:])
        pieces_down = pieces_down.transpose(1, 0, 2, 3, 4).reshape(1, 1, hidden_width, model_width)

    place, segment = marks[:, 0], marks[:, 1]
    length = place.shape[1]
    rows = groups * length
    steps = jnp.arange(width // 2).astype(wide)
    inverse = jnp.exp(steps * (-2.0 * math.log(1000000.0) / width))
    inverse = jnp.concatenate([inverse, inverse])[None]
    sign = jnp.where(jnp.arange(width) < width // 2, -1.0, 1.0)[None]
    head_gains = (gain_query[None], gain_key[None])
    lin, query_low, keyed_low, value_low, cosine, sine = row_call(
        functools.partial(prep_kernel, heads),
        rows,
        (all_one, w_qkv, place.reshape(rows, 1), inverse, sign) + head_gains,
        (1, 3, 4, 5, 6),
        [(q_cols + width, wide), (q_cols, low), (width, low), (width, low), (width, wide), (width, wide)],
        [],
    )
    query_low = query_low.reshape(groups, length, q_cols)
    keyed_low = keyed_low.reshape(groups, length, width)
    value_low = value_low.reshape(groups, length, width)
    total_shape = jax.ShapeDtypeStruct((groups, heads, 1, length), wide)
    mixed_low, log_total = attention_call(
        ahead_kernel,
        (place, segment),
        (query_low, keyed_low, value_low.transpose(0, 2, 1)),
        ("query", "keys", "flat"),
        [("query", jax.ShapeDtypeStruct(query_low.shape, low)), ("total", total_shape)],
        width,
        scale,
        4,
    )
    mixed_rows = mixed_low.reshape(groups * length, q_cols)
    branch = dot(mixed_rows, w_mix).astype(low).reshape(plane_shape)
    (branch,) = transfer(2, [Reduce(plane_axes, branch, core_first(plane_parts))])
    resid_one = resid + branch

    norm_two, back_two = jax.vjp(normed, resid_one, gain_ffn)
    normed_two = norm_two.astype(low)
    logits = dot(normed_two, full_router)
    labels = jnp.arange(experts, dtype=jnp.int32)
    chosen = jnp.any(routes[0][:, :, None] == labels[None, None, :], axis=1)
    logits = jnp.where(chosen, logits, -1e30)
    powers = jnp.where(chosen, jnp.exp(logits - jnp.max(logits, axis=-1, keepdims=True)), 0.0)
    gates = powers / jnp.sum(powers, axis=-1, keepdims=True)

    own_two, all_gates = transfer(
        3,
        [
            Gather(turn, normed_two, cluster_parts),
            Gather(cluster_axes, gates.T, [(0, experts, turn + core)]),
        ],
    )
    own_two = own_two.reshape(blocks, count, model_width)
    far_two = lax.ppermute(own_two, core[0], SWAP)
    gate_stack = take_at(all_gates, flat_index(cluster_axes), len(cluster_axes))
    core_here, core_spot = lax.axis_index(core[0]), cluster_axes.index(core[0])
    ids = jnp.bitwise_xor(jnp.arange(blocks), flat_index(turn)).astype(jnp.int32)
    sides = []
    pieces = (pieces_gate, pieces_up, pieces_down)
    for side, side_rows, side_grads in (
        (core_here, own_two, own_grads),
        (1 - core_here, far_two, far_grads),
    ):
        gate = take_at(gate_stack, side, core_spot).reshape(-1, 1)
        sides.append(expert_rows(side_rows, side_grads, gate, pieces, parts_near, ids))
        ids = ids + zero_of(sides[0][2]).astype(jnp.int32)
    hiddens, d_ins, d_gate_parts, made_parts, back_parts = zip(*sides)
    half_shape = (2,) * len(turn) + (count, model_width)
    far_parts = 1 << len(far_axes)
    straight = parts_near * rows_d == TILE
    d_gates = jnp.stack(d_gate_parts).reshape(experts, 1, count)
    hiddens = [part.reshape(blocks, count, hidden_width) for part in hiddens]
    d_ins = [part.reshape(blocks, count, 2 * hidden_width) for part in d_ins]
    back = [part.reshape(half_shape) for part in back_parts]
    down_task = WeightGrad(hiddens, [own_grads, far_grads])
    in_task = WeightGrad(
        [own_two, far_two], d_ins, far_parts if straight else 1, 2, room=down_task
    )
    flows = [
        ReduceBoth(turn, *back, cluster_parts, core),
        Direct(core + turn, d_gates, (1, count)),
        down_task,
        in_task,
    ]
    in_pair = len(far_axes) == 1 and parts_near * rows_f % ROW_TILE == 0
    if in_pair:
        flows.append(PairSum(far_axes[0], down_task, parts_c, parts_near * rows_f))
    d_rows_two, d_gates, part_down, part_in, *sums = transfer(4, flows, (-1, 2, 0, -2, 0, -2, 0))
    d_gates = d_gates.reshape((2,) * len(cluster_axes) + (count,))
    spots = [(core + turn).index(axis) for axis in cluster_axes]
    d_gates = d_gates.transpose(spots + [len(spots)]).reshape(experts, count).T

    reduced = zero_of(d_rows_two).astype(low)

    def to_far(part, rows, done=False):
        stack = part
        if not done:
            stack = part.reshape(parts_c, -1, parts_near, rows, part.shape[1]) + reduced
            stack = stack.transpose(1, 0, 2, 3, 4)
        stack = stack.reshape(-1, team, rows, part.shape[1])
        if not far_axes:
            return stack[0]
        return lax.psum_scatter(stack, far_axes, scatter_dimension=0, tiled=False)

    share_in = to_far(part_in, rows_d, straight)
    if in_pair:
        share_down = sums[0].reshape(team, rows_f, model_width)
    else:
        share_down = to_far(part_down, rows_f)

    d_logits = (gates * (d_gates - jnp.sum(gates * d_gates, axis=-1, keepdims=True))).astype(low)
    part_router = dot_tn(normed_two, d_logits)
    d_normed_two = d_rows_two + dot_nt(d_logits, full_router)
    d_resid_one, d_gain_ffn = back_two(d_normed_two)
    d_resid_one = d_resid_one + cotangent[0].astype(jnp.float32)
    wide_part = jnp.pad(part_router.astype(low), ((0, 0), (0, width - experts)))

    made_axes = turn[: len(turn) - len(near_axes)]
    made_shape = (2,) * len(made_axes) + (parts_near * count, model_width)
    made = [part.reshape(made_shape) for part in made_parts]
    made_spans = [(lo * parts_near, hi * parts_near, order) for lo, hi, order in plane_parts]
    branch_flow = Gather(plane_axes, d_resid_one.astype(low), core_last(plane_parts))
    planes = 1 << len(plane_axes)
    branch_task = Branch(lambda: branch_flow.refs[1][0], w_mix, groups, planes, count)
    behind_task = HeadsBehind(
        lambda: branch_task.refs[1][0],
        (place, segment),
        (query_low, keyed_low, value_low, keyed_low.transpose(0, 2, 1), log_total),
        scale,
    )
    out_task = WeightGrad(
        [mixed_rows.reshape(planes, count, q_cols)],
        [jax.ShapeDtypeStruct((planes, count, model_width), low)],
        source=lambda: branch_flow.refs[1][0],
    )
    _, made, _, d_query, d_keyed, d_value, part_out = transfer(
        5,
        [
            branch_flow,
            ReduceBoth(made_axes, *made, made_spans, core, True),
            branch_task,
            behind_task,
            out_task,
        ],
        (0, 1) + (0,) * (len(plane_axes) - 2) + (1, 0, -1) + (-2,) * groups + (1, -3, 1),
    )
    heads_back = HeadsBack(
        heads,
        scale,
        (
            d_query.reshape(rows, q_cols),
            d_keyed.reshape(rows, width),
            d_value.reshape(rows, width),
            lin,
            cosine,
            sine,
            all_one,
        ),
        w_qkv,
        head_gains + (gain_attn[None],),
        d_gain_ffn.reshape(-1, width),
        plane_axes,
    )
    pieces_tile = TILE // rows_d
    runs = parts_f // pieces_tile
    spare = len(f_axes) - (pieces_tile.bit_length() - 1)
    qkv_shape = (2,) * len(f_axes) + (parts_c * rows_d, qkv_cols)

    def qkv_place(step):
        bits = [step % runs // (runs >> (bit + 1)) % 2 for bit in range(spare)]
        return tuple(bits) + (0,) * (len(f_axes) - spare) + (step // runs, 0)

    qkv_block = (None,) * spare + (2,) * (len(f_axes) - spare) + (rows_d, qkv_cols)
    stack = (1 << len(plane_axes), count)
    qkv_task = WeightGrad(
        [all_one.reshape(stack + (model_width,))],
        [jax.ShapeDtypeStruct(stack + (qkv_cols,), low)],
        source=lambda: heads_back.refs[1][0],
        out=(qkv_shape, qkv_block, qkv_place),
    )

    turn_back = plane_axes[len(g_axes) : -1] + g_axes
    def over_groups(shape):
        return Gather(g_axes, shape, [(0, shape.shape[0], g_axes)])

    def to_column_owners(shape):
        return Spread(c_axes, g_axes, shape, shape.shape[1:])

    flows = [
        Spread(team_axes, g_axes, share_down, share_down.shape[1:]),
        Spread(team_axes, g_axes, share_in, share_in.shape[1:]),
        Fed(
            Reduce(
                plane_axes,
                heads_back.results[1],
                core_first([(lo, hi, turn_back) for lo, hi, _ in plane_parts]),
            ),
            lambda: heads_back.refs[1][1],
        ),
        Fed(
            Reduce(
                f_axes,
                qkv_task.results[0],
                [(0, parts_c * rows_d, f_axes[::-1])],
                jax.ShapeDtypeStruct((parts_c, rows_d, qkv_cols), low),
                to_column_owners,
            ),
            lambda: qkv_task.refs[1][0],
        ),
        Reduce(
            own_axes,
            wide_part.reshape((2,) * len(own_axes) + (rows_d, width)),
            [(0, rows_d, own_axes)],
            jax.ShapeDtypeStruct((rows_d, width), low),
            over_groups,
        ),
    ]
    if even:
        rows = q_cols // parts_f
        stack = part_out.reshape((2,) * len(f_axes) + (rows, model_width))
        shape = jax.ShapeDtypeStruct((rows, model_width), low)
        flows.append(Later(Reduce(f_axes, stack, [(0, rows, f_axes[::-1])], shape, over_groups)))
    if near_axes:
        near_shape = (2,) * len(near_axes) + (count, model_width)
        near_flow = Reduce(
            near_axes, made.astype(low).reshape(near_shape), [(0, count, near_axes)], by_distance=True
        )
        flows.append(Later(near_flow))
    lines = jax.ShapeDtypeStruct((heads_back.lines, width), wide)
    gains_flow = Gather(all_axes, lines, [(0, heads_back.lines, core + all_axes_but_core)])
    flows.insert(5, Fed(gains_flow, lambda: heads_back.refs[2][0]))
    flows += [heads_back, qkv_task]
    all_down, all_in, d_one, all_qkv, share_router, gains, *rest = transfer(
        7,
        flows,
        (-1, 0, 2, -2, 2, 3, 1, 6, 5, 3, 2, 6, 7, 3, 3, 6, 6, 3, 4, 5, 4, 5, 4, 5, 4, 5),
    )
    rest = rest[:-3]
    gains = jnp.sum(gains.reshape(-1, heads_back.lines * width), axis=0)
    share_router = share_router.reshape(groups, rows_d, width)[:, :, :experts]
    grad_router = jnp.sum(share_router.astype(wide), axis=0)
    if near_axes:
        made = rest.pop()
    output = (resid_one + made).astype(low)[None]
    d_resid = back_one(d_one)[0]
    grad_tokens = (d_resid + d_resid_one)[None]
    grad_down, = by_expert(all_down, 1)
    grad_gate, grad_up = by_expert(all_in, 2)
    if even:
        grad_out = rest[0].astype(wide).reshape(rows_o, model_width)
    else:
        stack = jnp.where(jnp.arange(groups)[:, None, None] == g_here, part_out[None], 0)
        share_out = lax.psum_scatter(
            stack.reshape(groups * q_cols, model_width), f_axes, scatter_dimension=0, tiled=True
        )
        grad_out = lax.psum(share_out.astype(wide), g_axes)
    grad_query, grad_key, grad_value = by_head(
        all_qkv.reshape(parts_c, groups, rows_d, qkv_cols), parts_f if even else 1, width
    )
    return (
        output,
        grad_tokens,
        grad_query,
        grad_key,
        grad_value,
        grad_out,
        grad_router,
        grad_gate,
        grad_up,
        grad_down,
        gains[:model_width],
        gains[model_width : 2 * model_width],
        gains[2 * model_width : 2 * model_width + width],
        gains[2 * model_width + width : 2 * model_width + 2 * width],
    )


def solution(mesh):
    def binary(letter, size):
        return tuple(letter + str(step) for step in range(size.bit_length() - 1))

    g_axes = binary("g", mesh.shape["grp"])
    c_axes = binary("c", mesh.shape["ctx"])
    f_axes = binary("f", mesh.shape["fsdp"])
    names = g_axes + c_axes + f_axes
    fine = Mesh(mesh.devices.reshape((2,) * len(names)), names)
    rows = P(g_axes + f_axes, c_axes, None)
    line = P(g_axes + f_axes, None)
    split = P(c_axes + f_axes, None)
    expert = P(None, c_axes + f_axes, None)
    whole = P()
    in_specs = (
        (rows, line, line, rows)
        + (split,) * 5
        + (expert,) * 3
        + (whole,) * 4
        + (rows,)
    )
    out_specs = (rows, rows) + (split,) * 5 + (expert,) * 3 + (whole,) * 4

    def device_part(*arrays):
        return per_device(g_axes, c_axes, f_axes, *arrays)

    return jax.shard_map(
        device_part, mesh=fine, in_specs=in_specs, out_specs=out_specs, check_vma=False
    )
```
